128 devices in a mesh: req: 32 (over y, z, core), grp: 4 (over x).
Axes of the slice: x: 4, y: 4, z: 4, core: 2. Of those that a mesh axis runs over, the one named last changes fastest.
Arguments:
- residual_in: bfloat16 [2048, 2048], P('grp'), may hold values from -6 to 6
- mixer_in: bfloat16 [2048, 3, 2048], P('grp', None, 'req'), may hold values from -6 to 6
- forget_floor: float32 [2048], replicated, may hold values from 0.3 to 0.97
- conv_weight: float32 [4, 2048], P(None, 'req'), may hold values from -3 to 3
- conv_edges: bfloat16 [128, 3, 2048], P('grp', None, 'req'), may hold values from -6 to 6
- state_in: float32 [128, 2048, 128], P('grp', 'req'), may hold values from -6 to 6
- accepted: int32 [128], P('grp'), may hold values from 0 to 16
- home_slot: int32 [128], replicated, may hold values from 0 to 127, each once
- gain_mixer: float32 [2048], P('req'), may hold values from 0.1 to 1.9
- w_out: bfloat16 [2048, 2048], P('req'), may hold values from -0.25 to 0.25
- gain_mlp: float32 [2048], replicated, may hold values from 0.1 to 1.9
- w_gate: bfloat16 [2048, 5632], P(None, 'req'), may hold values from -0.125 to 0.125
- w_up: bfloat16 [2048, 5632], P(None, 'req'), may hold values from -0.125 to 0.125
- w_down: bfloat16 [5632, 2048], P('req'), may hold values from -0.15625 to 0.15625
- gain_next: float32 [2048], replicated, may hold values from 0.1 to 1.9
- w_next: bfloat16 [2048, 3, 2048], P(None, None, 'req'), may hold values from -0.125 to 0.125
Outputs:
- next_mixer: bfloat16 [2048, 3, 2048], P('grp', None, 'req')
- kept_state: float32 [128, 2048, 128], P('grp', 'req')
- kept_edges: bfloat16 [128, 3, 2048], P('grp', None, 'req')
The draws below stay inside these ranges and needn't reach their ends.
Inputs may be any that keep to these rules, and one draw needn't show every extreme that they name: `home_slot`: every row of the kept outputs is the home of exactly one request.
All inputs are finite; a program needn't handle non-finite values.
Results may differ from the reference program's by a relative error of at most 0.029.
Values may be sent and summed in bfloat16 or wider, within the bound.
A program may use at most 64 MiB of HBM per device.

```python
import jax
import jax.numpy as jnp
from jax import lax

D = 2048
K = 128
FF = 5632
STEPS = 16
TAPS = 4
H = 16
EDGE = 3
REQS = 128
TOKENS = 2048
N_REQ = 32


def plant(result, rng, low, high):
    index_at = [jax.random.randint(jax.random.fold_in(rng, axis), (), 0, length) for axis, length in enumerate(result.shape)]
    longest = result.shape.index(max(result.shape))
    beside = index_at[:longest] + [(index_at[longest] + 1) % result.shape[longest]] + index_at[longest + 1:]
    return result.at[tuple(index_at)].set(low).at[tuple(beside)].set(high)


def spiked(drawn, stream_key, source, target, parts, factor):
    owner, partner = [(jnp.arange(drawn.shape[dim]) // (drawn.shape[dim] // parts)).reshape([-1 if axis == dim else 1 for axis in range(drawn.ndim)]) for dim in (source, target)]
    chosen = jax.random.permutation(stream_key, parts)[partner]
    strong = (owner == chosen) | (owner == (partner + parts // 2) % parts)
    return jnp.where(strong, factor * drawn, drawn)


def block_levels(key, shape, split, low, high):
    level, own = 1.0, jax.random.fold_in(key, 6)
    for position, blocks in split:
        draws = jnp.exp(jax.random.uniform(jax.random.fold_in(own, position), (blocks,), jnp.float32, low / len(split), high / len(split)))
        level = level * jnp.repeat(draws, shape[position] // blocks).reshape([-1 if axis == position else 1 for axis in range(len(shape))])
    return level


def centred(rng, dims, width, bound, pieces=(), kind=jnp.bfloat16):
    result = width * jax.random.normal(rng, dims, jnp.float32)
    if pieces:
        result = result * block_levels(rng, dims, pieces, -0.22, 0.18)
    return jnp.clip(result, -bound, bound).astype(kind)


def bell_draw_with(rng, extent, deviation, bound, split, heavy, kind=jnp.bfloat16):
    entries = deviation * jax.random.normal(rng, extent, jnp.float32)
    if split:
        entries = entries * block_levels(rng, extent, split, -0.22, 0.18)
    return jnp.clip(spiked(entries, jax.random.fold_in(rng, 3), *heavy), -bound, bound).astype(kind)


def setup_inputs(seed: int = 0) -> dict:
    seeds = jax.random.split(jax.random.key(seed), 17)
    return {
        "residual_in": centred(seeds[0], (TOKENS, D), 1.0, 6.0, ((0, 4),)),
        "mixer_in": centred(seeds[1], (TOKENS, 3, D), 1.0, 6.0, ((0, 4), (2, 32))),
        "forget_floor": jnp.clip(jax.random.uniform(seeds[2], (D,), jnp.float32, 0.3, 0.97), 0.3, 0.97),
        "conv_weight": centred(seeds[3], (TAPS, D), 0.5, 3.0, ((1, 32),), jnp.float32),
        "conv_edges": centred(seeds[4], (REQS, EDGE, D), 1.0, 6.0, ((0, 4), (2, 32))),
        "state_in": centred(seeds[5], (REQS, D, K), 1.0, 6.0, ((0, 4), (1, 32)), jnp.float32),
        "accepted": plant(jax.random.randint(seeds[6], (REQS,), 0, STEPS + 1), jax.random.fold_in(seeds[6], 1), 0, STEPS).astype(jnp.int32),
        "home_slot": jax.random.permutation(seeds[7], REQS).astype(jnp.int32),
        "gain_mixer": jnp.clip(1.0 + 0.18 * jax.random.normal(seeds[8], (D,), jnp.float32), 0.1, 1.9),
        "w_out": bell_draw_with(seeds[9], (D, D), D ** -0.5, 0.25, ((0, 32),), (0, 1, 32, 2.75)),
        "gain_mlp": jnp.clip(1.0 + 0.18 * jax.random.normal(seeds[10], (D,), jnp.float32), 0.1, 1.9),
        "w_gate": centred(seeds[11], (D, FF), D ** -0.5, 0.125, ((1, 32),)),
        "w_up": centred(seeds[12], (D, FF), D ** -0.5, 0.125, ((1, 32),)),
        "w_down": bell_draw_with(seeds[13], (FF, D), FF ** -0.5, 0.15625, ((0, 32),), (0, 1, 32, 2.75)),
        "gain_next": jnp.clip(1.0 + 0.18 * jax.random.normal(seeds[14], (D,), jnp.float32), 0.1, 1.9),
        "w_next": centred(seeds[15], (D, 3, D), D ** -0.5, 0.125, ((2, 32),)),
    }


EPSILON = 1e-06

def scaled_norm(values_in, gain_row):
    widened = values_in.astype(jnp.float32)
    factor = lax.rsqrt(lax.optimization_barrier(jnp.mean(widened * widened, axis=1, keepdims=True)) + EPSILON)
    return (widened * factor * gain_row).astype(jnp.bfloat16)

def block_sum(left_side, right_side, blocks):
    token_rows = left_side.shape[0]
    block_width = left_side.shape[1] // blocks

    def add_block(total, block_index):
        left_piece = lax.dynamic_slice_in_dim(left_side, block_index * block_width, block_width, 1)
        right_piece = lax.dynamic_slice_in_dim(right_side, block_index * block_width, block_width, 0)
        partial_sum = jnp.dot(left_piece, right_piece, preferred_element_type=jnp.float32)
        rounded = lax.optimization_barrier(partial_sum.astype(jnp.bfloat16))
        return (total + rounded.astype(jnp.float32), None)
    start_total = jnp.zeros((token_rows, right_side.shape[1]), jnp.float32)
    total, _ = lax.scan(add_block, start_total, jnp.arange(blocks, dtype=jnp.int32))
    return total

def mixer_request(inputs, forget_floor, conv_weight):
    mixer_rows, edge_rows, state_rows, count_value = inputs
    query = jax.nn.silu(mixer_rows[:, 0].astype(jnp.float32)).reshape(STEPS, H, K)
    forget = forget_floor + (1.0 - forget_floor) * jax.nn.sigmoid(mixer_rows[:, 1].astype(jnp.float32))
    keyed = (1.0 - forget).reshape(STEPS, H, K)
    forget = forget.reshape(STEPS, H, K)
    sequence = jnp.concatenate([edge_rows, mixer_rows[:, 2]], axis=0)
    seq_float = sequence.astype(jnp.float32)
    conv_input = sum((conv_weight[offset] * seq_float[offset:offset + STEPS] for offset in range(TAPS)))
    conv_input = conv_input.reshape(STEPS, H, K)

    def advance(carry, step_inputs):
        current, kept, counter = carry
        q_step, f_step, k_step, v_step = step_inputs
        current = f_step[:, None, :] * current + v_step[:, :, None] * k_step[:, None, :]
        output = lax.optimization_barrier(jnp.sum(current * q_step[:, None, :], axis=2)) * K ** (-0.5)
        kept = jnp.where(counter + 1 == count_value, current, kept)
        return ((current, kept, counter + 1), output.reshape(D))
    begin_state = state_rows.reshape(H, K, K)
    carry_out, outputs = lax.scan(advance, (begin_state, begin_state, jnp.int32(0)), (query, forget, keyed, conv_input))
    kept_edge = lax.dynamic_slice_in_dim(sequence, count_value.astype(jnp.int32), EDGE, 0)
    return (outputs, carry_out[1].reshape(D, K), kept_edge)

def reference(residual_in, mixer_in, forget_floor, conv_weight, conv_edges, state_in, accepted, home_slot, gain_mixer, w_out, gain_mlp, w_gate, w_up, w_down, gain_next, w_next):
    per_request = mixer_in.reshape(REQS, STEPS, 3, D)
    outputs, kept, kept_edge = lax.map(lambda items: mixer_request(items, forget_floor, conv_weight), (per_request, conv_edges, state_in, accepted))
    mixed = outputs.reshape(TOKENS, D)
    gained = (mixed * gain_mixer).astype(jnp.bfloat16)
    block_squares = lax.optimization_barrier(jnp.sum((mixed * mixed).reshape(TOKENS, N_REQ, D // N_REQ), axis=2))
    block_squares = lax.optimization_barrier(block_squares.astype(jnp.bfloat16))
    squares = lax.optimization_barrier(jnp.sum(block_squares.astype(jnp.float32), axis=1))
    mixer_sum = block_sum(gained, w_out, N_REQ)
    attn = mixer_sum * lax.rsqrt(squares[:, None] / D + EPSILON)
    first = (residual_in.astype(jnp.float32) + attn).astype(jnp.bfloat16)
    normed = scaled_norm(first, gain_mlp)
    gate = jnp.dot(normed, w_gate, preferred_element_type=jnp.float32)
    up_part = jnp.dot(normed, w_up, preferred_element_type=jnp.float32)
    hidden = (jax.nn.silu(gate) * up_part).astype(jnp.bfloat16)
    down = block_sum(hidden, w_down, N_REQ)
    second = (first.astype(jnp.float32) + down).astype(jnp.bfloat16)
    final_norm = scaled_norm(second, gain_next)
    next_flat = jnp.dot(final_norm, w_next.reshape(D, 3 * D), preferred_element_type=jnp.float32)
    next_mixer = next_flat.astype(jnp.bfloat16).reshape(TOKENS, 3, D)
    kept_state = jnp.zeros_like(state_in).at[home_slot].set(kept)
    kept_edges = jnp.zeros_like(conv_edges).at[home_slot].set(kept_edge)
    return (next_mixer, kept_state, kept_edges)
```

```python
import jax
import jax.numpy as jnp
from jax import lax
from jax.experimental import pallas as pl
from jax.experimental.pallas import tpu as pltpu
from jax.sharding import PartitionSpec as P

EPSILON = 1e-06
MESH = pl.DeviceIdType.MESH
F32 = jnp.float32
BF16 = jnp.bfloat16

SIDE = 4
CHIPS = SIDE * SIDE
GROUPS = 4
STEPS = 16
TAPS = 4
EDGES = 3
WIDTH = 2048
HALF = 64
KEYS = 128
EXTRA = 128
REQUESTS = 32
TOKENS = REQUESTS * STEPS
MINE = TOKENS // 2
TILE = 128
TILE_REQ = TILE // STEPS

NT = (((1,), (1,)), ((), ()))
TN = (((0,), (0,)), ((), ()))


def dot(left, right, dims=(((1,), (0,)), ((), ()))):
    return lax.dot_general(left, right, dims, preferred_element_type=F32)


def iota(shape, dim):
    return lax.broadcasted_iota(jnp.int32, shape, dim)


def to_column(row):
    size = row.shape[1]
    square = jnp.broadcast_to(row, (size, size))
    diagonal = iota((size, size), 0) == iota((size, size), 1)
    return jnp.sum(jnp.where(diagonal, square, jnp.zeros_like(square)), axis=1, keepdims=True)


def kernel(
    residual, mixer, floor, taps, edges, state, accepted, home, gain_mixer,
    w_out, gain_mlp, w_gate, w_up, w_down, gain_next, w_next,
    next_out, kept_out, edge_out,
    mix_v, pair, state_v, res_v, wo, wg, wu, wd, wn,
    query_b, key_b, decay, values, picked, gained_own, gained_send, gained_recv,
    send1, recv1, gather1, first_v, hidden, send2, recv2, gather2,
    next_send, next_recv, kept_v, edge_v, kept_all, edge_all,
    load_sem, pair_ss, pair_rs, ss1, rs1, ss2, rs2, ss3, rs3, ss4, rs4, ss_x, rs_x,
):
    member = lax.axis_index("req")
    group = lax.axis_index("grp")
    core = member % 2
    chip = member // 2
    at_y = chip // SIDE
    at_z = chip % SIDE
    sibling = {"req": chip * 2 + (1 - core), "grp": group}

    def peer_chip(k):
        return ((at_y + k // SIDE) % SIDE) * SIDE + (at_z + k % SIDE) % SIDE

    def peer(k):
        return {"req": peer_chip(k) * 2 + core, "grp": group}

    def across(k):
        return {"req": member, "grp": (group + k) % GROUPS}

    barrier = pltpu.get_barrier_semaphore()

    def greet(k, carry):
        pl.semaphore_signal(barrier, inc=1, device_id=peer(k), device_id_type=MESH)
        return carry

    pl.semaphore_signal(barrier, inc=1, device_id=sibling, device_id_type=MESH)
    lax.fori_loop(1, CHIPS, greet, 0)
    for k in range(1, GROUPS):
        pl.semaphore_signal(barrier, inc=1, device_id=across(k), device_id_type=MESH)

    loads = [
        pltpu.make_async_copy(mixer, mix_v, load_sem.at[0]),
        pltpu.make_async_copy(state, state_v, load_sem.at[1]),
        pltpu.make_async_copy(w_out, wo.at[core], load_sem.at[2]),
        pltpu.make_async_copy(
            residual.at[pl.ds(pl.multiple_of(core * MINE + chip * STEPS, STEPS), STEPS)],
            res_v, load_sem.at[3]),
        pltpu.make_async_copy(w_gate, wg.at[core], load_sem.at[4]),
        pltpu.make_async_copy(w_up, wu.at[core], load_sem.at[5]),
        pltpu.make_async_copy(w_down, wd.at[core], load_sem.at[6]),
        pltpu.make_async_copy(w_next, wn.at[core], load_sem.at[7]),
    ]
    for load in loads:
        load.start()

    def to_sibling(source, target, slot):
        return pltpu.make_async_remote_copy(
            src_ref=source, dst_ref=target, send_sem=pair_ss.at[slot], recv_sem=pair_rs.at[slot],
            device_id=sibling, device_id_type=MESH)

    pl.semaphore_wait(barrier, CHIPS + GROUPS - 1)
    halves = to_sibling(mixer.at[0:2], pair.at[:, core], 0)
    halves.start()
    shared = [
        to_sibling(w_out, wo.at[core], 1),
        to_sibling(w_gate, wg.at[core], 2),
        to_sibling(w_up, wu.at[core], 3),
        to_sibling(w_down, wd.at[core], 4),
        to_sibling(w_next, wn.at[core], 5),
    ]
    for copy in shared:
        copy.start()

    loads[0].wait()
    lane = iota((1, TOKENS), 1)
    step_of = lane % STEPS
    inputs_raw = mix_v[2]
    inputs_f = inputs_raw.astype(F32)
    stacked = jnp.concatenate([edges[i] for i in range(EDGES)], axis=0)
    row96 = iota((EDGES * REQUESTS, TOKENS), 0)
    lane96 = iota((EDGES * REQUESTS, TOKENS), 1)
    conv = to_column(taps[TAPS - 1:TAPS, :]) * inputs_f
    for j in range(TAPS - 1):
        shift = TAPS - 1 - j
        early = row96 // REQUESTS - j
        place = (early >= 0) & (lane96 == (row96 % REQUESTS) * STEPS + early)
        from_edges = dot(stacked, jnp.where(place, 1.0, 0.0).astype(BF16), TN)
        moved = jnp.where(step_of >= shift, pltpu.roll(inputs_f, shift, axis=1), 0.0)
        conv = conv + to_column(taps[j:j + 1, :]) * (moved + from_edges)
    values[...] = conv.astype(BF16)

    pair[:, core] = mix_v[0:2]
    floor_row = floor[pl.ds(chip, 1), :]
    low = to_column(floor_row)
    halves.wait()
    for tile in range(TOKENS // TILE):
        at = slice(tile * TILE, (tile + 1) * TILE)
        step_t = iota((KEYS, TILE), 1) % STEPS
        q_pre = pair[0, :, :, at].reshape(KEYS, TILE).astype(F32)
        f_pre = pair[1, :, :, at].reshape(KEYS, TILE).astype(F32)
        query = q_pre * jax.nn.sigmoid(q_pre)
        forget = low + (1.0 - low) * jax.nn.sigmoid(f_pre)
        keyed = 1.0 - forget
        run = forget
        for shift in (1, 2, 4, 8):
            run = jnp.where(step_t >= shift, run * pltpu.roll(run, shift, axis=1), run)
        decay[:, at] = run
        query_b[:, at] = (query * run).astype(BF16)
        key_b[:, at] = (keyed / run).astype(BF16)

    loads[1].wait()
    gain_column = to_column(gain_mixer[...])
    squares = []
    for tile in range(TOKENS // TILE):
        at = slice(tile * TILE, (tile + 1) * TILE)
        q_t = query_b[:, at]
        begin = state_v[tile * TILE_REQ:(tile + 1) * TILE_REQ].astype(BF16).reshape(TILE_REQ * HALF, KEYS)
        through = dot(begin, q_t).reshape(TILE_REQ, HALF, TILE)
        ours = iota((TILE_REQ, HALF, TILE), 0) == iota((TILE_REQ, HALF, TILE), 2) // STEPS
        total = jnp.sum(jnp.where(ours, through, 0.0), axis=0)
        scores = dot(key_b[:, at], q_t, TN)
        source = iota((TILE, TILE), 0)
        sink = iota((TILE, TILE), 1)
        causal = (source // STEPS == sink // STEPS) & (source <= sink)
        scores = jnp.where(causal, scores, 0.0).astype(BF16)
        total = (total + dot(values[:, at], scores)) * KEYS ** (-0.5)
        gained_own[0:HALF, at] = (total * gain_column).astype(BF16)
        square = jnp.sum(total * total, axis=0, keepdims=True)
        gained_own[HALF:HALF + STEPS, at] = jnp.broadcast_to(square, (STEPS, TILE)).astype(BF16)

    own_lanes = pl.ds(pl.multiple_of(core * MINE, MINE), MINE)
    other_lanes = pl.ds(pl.multiple_of((1 - core) * MINE, MINE), MINE)
    gained_send[...] = gained_own[:, other_lanes]
    swap = to_sibling(gained_send, gained_recv, 6)
    swap.start()
    mine = gained_own[:, own_lanes]
    swap.wait()
    theirs = gained_recv[...]
    lower = jnp.where(core == 0, mine[0:HALF], theirs[0:HALF])
    upper = jnp.where(core == 0, theirs[0:HALF], mine[0:HALF])
    both = jnp.concatenate([lower, upper], axis=0)
    loads[2].wait()
    shared[0].wait()
    squares2 = jnp.concatenate([mine[HALF:], theirs[HALF:]], axis=0)
    pick_one = jnp.where(iota((2 * STEPS, EXTRA), 0) % STEPS == 0, 1.0, 0.0).astype(BF16)
    send1[:, :, WIDTH:] = dot(squares2, pick_one, TN).astype(BF16).reshape(CHIPS, STEPS, EXTRA)
    cut = 512

    def project(n, carry):
        at = pl.ds(pl.multiple_of(n * cut, cut), cut)
        block = wo[:, :, at].reshape(2 * HALF, cut)
        send1[:, :, at] = dot(both, block, TN).astype(BF16).reshape(CHIPS, STEPS, cut)
        return carry

    lax.fori_loop(0, WIDTH // cut, project, 0)

    def scatter(source, target, ssem, rsem):
        def copy(k):
            return pltpu.make_async_remote_copy(
                src_ref=source.at[peer_chip(k)], dst_ref=target.at[k], send_sem=ssem.at[k],
                recv_sem=rsem.at[k], device_id=peer(k), device_id_type=MESH)
        return copy

    def gather(source, target, ssem, rsem):
        def copy(k):
            return pltpu.make_async_remote_copy(
                src_ref=source.at[chip], dst_ref=target.at[chip], send_sem=ssem.at[k],
                recv_sem=rsem.at[k], device_id=peer(k), device_id_type=MESH)
        return copy

    def start_all(copy):
        def body(k, carry):
            copy(k).start()
            return carry
        lax.fori_loop(1, CHIPS, body, 0)

    def wait_all(copy):
        def body(k, carry):
            copy(k).wait_recv()
            return carry
        lax.fori_loop(1, CHIPS, body, 0)

    def drain(copy):
        def body(k, carry):
            copy(k).wait_send()
            return carry
        lax.fori_loop(1, CHIPS, body, 0)

    copy1 = scatter(send1, recv1, ss1, rs1)
    start_all(copy1)
    recv1[0] = send1[chip]

    acc_column = to_column(accepted[...])
    row32 = iota((REQUESTS, TOKENS), 0)
    lane32 = iota((REQUESTS, TOKENS), 1)
    acc_lanes = jnp.sum(jnp.where(lane32 // STEPS == row32, acc_column, 0), axis=0, keepdims=True)
    last = jnp.where(lane32 == row32 * STEPS + acc_column - 1, 1.0, 0.0)
    last = jnp.where(acc_column > 0, last, 0.0).astype(BF16)
    run_all = decay[...]
    run_high = run_all.astype(BF16)
    run_low = (run_all - run_high.astype(F32)).astype(BF16)
    run_picked = dot(last, run_high, NT) + dot(last, run_low, NT)
    picked[...] = jnp.where(acc_column == 0, 1.0, run_picked)
    live = step_of < acc_lanes
    for tile in range(TOKENS // TILE):
        at = slice(tile * TILE, (tile + 1) * TILE)
        taken = jnp.where(live[:, at], values[:, at].astype(F32), 0.0)
        spread = jnp.broadcast_to(taken[None], (TILE_REQ, HALF, TILE))
        ours = iota((TILE_REQ, HALF, TILE), 0) == iota((TILE_REQ, HALF, TILE), 2) // STEPS
        spread = jnp.where(ours, spread, 0.0).astype(BF16).reshape(TILE_REQ * HALF, TILE)
        added = dot(spread, key_b[:, at], NT)
        for i in range(TILE_REQ):
            r = tile * TILE_REQ + i
            kept_v[r] = (picked[r:r + 1, :] * (state_v[r] + added[i * HALF:(i + 1) * HALF])).astype(BF16)
    for e in range(EDGES):
        place = jnp.where(lane32 == row32 * STEPS + acc_column + (e - EDGES), 1.0, 0.0)
        place = jnp.where(acc_column + e >= EDGES, place, 0.0).astype(BF16)
        kept_edge = dot(place, inputs_raw, NT)
        for i in range(EDGES):
            kept_edge = kept_edge + jnp.where(acc_column + e == i, edges[i].astype(F32), 0.0)
        edge_v[e] = kept_edge.astype(BF16)

    def cross(k):
        return [
            pltpu.make_async_remote_copy(
                src_ref=source, dst_ref=target.at[group], send_sem=ss_x.at[slot, k],
                recv_sem=rs_x.at[slot, k], device_id=across(k), device_id_type=MESH)
            for slot, (source, target) in enumerate(((kept_v, kept_all), (edge_v, edge_all)))
        ]

    crossing = [copy for k in range(1, GROUPS) for copy in cross(k)]
    for copy in crossing:
        copy.start()
    kept_all[group] = kept_v[...]
    edge_all[group] = edge_v[...]

    for load in loads[3:]:
        load.wait()
    wait_all(copy1)

    def total_of(ref, width):
        def add(k, sums):
            return sums + ref[k, :, 0:width].astype(F32)
        return lax.fori_loop(1, CHIPS, add, ref[0, :, 0:width].astype(F32))

    sums = total_of(recv1, WIDTH + EXTRA)
    attn = sums[:, 0:WIDTH] * lax.rsqrt(sums[:, WIDTH:WIDTH + 1] / WIDTH + EPSILON)
    first = (res_v[...].astype(F32) + attn).astype(BF16)
    first_v[...] = first

    def scaled_norm(rows, gain):
        wide = rows.astype(F32)
        factor = lax.rsqrt(jnp.mean(wide * wide, axis=1, keepdims=True) + EPSILON)
        return (wide * factor * gain).astype(BF16)

    gather1[chip] = scaled_norm(first, gain_mlp[...])
    copy2 = gather(gather1, gather1, ss2, rs2)
    start_all(copy2)
    drain(copy1)
    for copy in shared[1:]:
        copy.wait()
    wait_all(copy2)

    rows = gather1[...].reshape(MINE, WIDTH)
    for side in range(2):
        gate = dot(rows, wg[side], NT)
        up = dot(rows, wu[side], NT)
        hidden[side] = (gate * jax.nn.sigmoid(gate) * up).astype(BF16)

    def lower_part(n, carry):
        at = pl.ds(pl.multiple_of(n * cut, cut), cut)
        terms = dot(hidden[0], wd[0, :, at]) + dot(hidden[1], wd[1, :, at])
        send2[:, :, at] = terms.astype(BF16).reshape(CHIPS, STEPS, cut)
        return carry

    lax.fori_loop(0, WIDTH // cut, lower_part, 0)
    copy3 = scatter(send2, recv2, ss3, rs3)
    start_all(copy3)
    recv2[0] = send2[chip]
    drain(copy2)

    for copy in crossing:
        copy.wait()
    home_row = home[...]
    source_lane = iota((1, GROUPS * REQUESTS), 1)
    for i in range(REQUESTS):
        found = jnp.max(jnp.where(home_row == group * REQUESTS + i, source_lane, 0))
        kept_out[i] = kept_all[found // REQUESTS, found % REQUESTS]
    target_row = iota((REQUESTS, GROUPS * REQUESTS), 0) + group * REQUESTS
    chosen = jnp.where(home_row == target_row, 1.0, 0.0).astype(BF16)
    for e in range(EDGES):
        pool = edge_all[:, e].reshape(GROUPS * REQUESTS, HALF)
        edge_out[e] = dot(chosen, pool).astype(BF16)

    wait_all(copy3)
    second = (first_v[...].astype(F32) + total_of(recv2, WIDTH)).astype(BF16)
    gather2[chip] = scaled_norm(second, gain_next[...])
    copy4 = gather(gather2, gather2, ss4, rs4)
    start_all(copy4)
    drain(copy3)
    wait_all(copy4)

    normed = gather2[...].reshape(MINE, WIDTH)
    theirs_next = dot(wn[1 - core].reshape(3 * HALF, WIDTH), normed, NT)
    next_send[...] = theirs_next.astype(BF16).reshape(3, HALF, MINE)
    last_swap = to_sibling(next_send, next_recv, 7)
    last_swap.start()
    own_next = dot(wn[core].reshape(3 * HALF, WIDTH), normed, NT)
    next_out[:, :, own_lanes] = own_next.astype(BF16).reshape(3, HALF, MINE)
    drain(copy4)
    last_swap.wait()
    next_out[:, :, other_lanes] = next_recv[...]


def per_device(
    residual_in, mixer_in, forget_floor, conv_weight, conv_edges, state_in, accepted, home_slot,
    gain_mixer, w_out, gain_mlp, w_gate, w_up, w_down, gain_next, w_next,
):
    hidden_width = w_gate.shape[1]
    anywhere = pl.BlockSpec(memory_space=pl.ANY)
    vmem = pl.BlockSpec(memory_space=pltpu.VMEM)
    dma = pltpu.SemaphoreType.DMA
    next_flat, kept, kept_edges = pl.pallas_call(
        kernel,
        name="draft_check",
        out_shape=(
            jax.ShapeDtypeStruct((3, HALF, TOKENS), BF16),
            jax.ShapeDtypeStruct((REQUESTS, HALF, KEYS), BF16),
            jax.ShapeDtypeStruct((EDGES, REQUESTS, HALF), BF16),
        ),
        in_specs=[
            anywhere, anywhere, vmem, vmem, vmem, anywhere, vmem, vmem, vmem,
            anywhere, vmem, anywhere, anywhere, anywhere, vmem, anywhere,
        ],
        out_specs=(vmem, vmem, vmem),
        scratch_shapes=[
            pltpu.VMEM((3, HALF, TOKENS), BF16),
            pltpu.VMEM((2, 2, HALF, TOKENS), BF16),
            pltpu.VMEM((REQUESTS, HALF, KEYS), F32),
            pltpu.VMEM((STEPS, WIDTH), BF16),
            pltpu.VMEM((2, HALF, WIDTH), BF16),
            pltpu.VMEM((2, hidden_width, WIDTH), BF16),
            pltpu.VMEM((2, hidden_width, WIDTH), BF16),
            pltpu.VMEM((2, hidden_width, WIDTH), BF16),
            pltpu.VMEM((2, 3, HALF, WIDTH), BF16),
            pltpu.VMEM((KEYS, TOKENS), BF16),
            pltpu.VMEM((KEYS, TOKENS), BF16),
            pltpu.VMEM((KEYS, TOKENS), F32),
            pltpu.VMEM((HALF, TOKENS), BF16),
            pltpu.VMEM((REQUESTS, KEYS), F32),
            pltpu.VMEM((HALF + STEPS, TOKENS), BF16),
            pltpu.VMEM((HALF + STEPS, MINE), BF16),
            pltpu.VMEM((HALF + STEPS, MINE), BF16),
            pltpu.VMEM((CHIPS, STEPS, WIDTH + EXTRA), BF16),
            pltpu.VMEM((CHIPS, STEPS, WIDTH + EXTRA), BF16),
            pltpu.VMEM((CHIPS, STEPS, WIDTH), BF16),
            pltpu.VMEM((STEPS, WIDTH), BF16),
            pltpu.VMEM((2, MINE, hidden_width), BF16),
            pltpu.VMEM((CHIPS, STEPS, WIDTH), BF16),
            pltpu.VMEM((CHIPS, STEPS, WIDTH), BF16),
            pltpu.VMEM((CHIPS, STEPS, WIDTH), BF16),
            pltpu.VMEM((3, HALF, MINE), BF16),
            pltpu.VMEM((3, HALF, MINE), BF16),
            pltpu.VMEM((REQUESTS, HALF, KEYS), BF16),
            pltpu.VMEM((EDGES, REQUESTS, HALF), BF16),
            pltpu.VMEM((GROUPS, REQUESTS, HALF, KEYS), BF16),
            pltpu.VMEM((GROUPS, EDGES, REQUESTS, HALF), BF16),
            dma((8,)), dma((8,)), dma((8,)),
            dma((CHIPS,)), dma((CHIPS,)), dma((CHIPS,)), dma((CHIPS,)),
            dma((CHIPS,)), dma((CHIPS,)), dma((CHIPS,)), dma((CHIPS,)),
            dma((2, GROUPS)), dma((2, GROUPS)),
        ],
        compiler_params=pltpu.CompilerParams(
            collective_id=0, has_side_effects=True, vmem_limit_bytes=56 * 2**20),
    )(
        residual_in,
        mixer_in.transpose(1, 2, 0),
        forget_floor.reshape(-1, KEYS),
        conv_weight,
        conv_edges.transpose(1, 0, 2),
        state_in,
        accepted.reshape(1, -1),
        home_slot.reshape(1, -1),
        gain_mixer.reshape(1, -1),
        w_out,
        gain_mlp.reshape(1, -1),
        w_gate.T,
        w_up.T,
        w_down,
        gain_next.reshape(1, -1),
        w_next.transpose(1, 2, 0),
    )
    return (
        next_flat.transpose(2, 0, 1),
        kept.astype(F32),
        kept_edges.transpose(1, 0, 2),
    )


def solution(mesh):
    in_specs = (
        P("grp", None),
        P("grp", None, "req"),
        P(),
        P(None, "req"),
        P("grp", None, "req"),
        P("grp", "req", None),
        P("grp"),
        P(),
        P("req"),
        P("req", None),
        P(),
        P(None, "req"),
        P(None, "req"),
        P("req", None),
        P(),
        P(None, None, "req"),
    )
    out_specs = (P("grp", None, "req"), P("grp", "req", None), P("grp", None, "req"))
    return jax.shard_map(
        per_device, mesh=mesh, in_specs=in_specs, out_specs=out_specs, check_vma=False
    )
```

```python
import jax
import jax.numpy as jnp
from jax import lax
from jax.experimental import pallas as pl
from jax.experimental.pallas import tpu as pltpu
from jax.sharding import PartitionSpec as P

EPSILON = 1e-06
MESH = pl.DeviceIdType.MESH
F32 = jnp.float32
BF16 = jnp.bfloat16

SIDE = 4
CHIPS = SIDE * SIDE
GROUPS = 4
STEPS = 16
TAPS = 4
EDGES = 3
WIDTH = 2048
HALF = 64
KEYS = 128
EXTRA = 128
REQUESTS = 32
TOKENS = REQUESTS * STEPS
MINE = TOKENS // 2
TILE = 128
TILE_REQ = TILE // STEPS
CHUNKS = 2
PART = MINE // CHUNKS
ROWS = PART // CHIPS
FOLD = WIDTH // 2

NT = (((1,), (1,)), ((), ()))
TN = (((0,), (0,)), ((), ()))


def dot(left, right, dims=(((1,), (0,)), ((), ()))):
    return lax.dot_general(left, right, dims, preferred_element_type=F32)


def iota(shape, dim):
    return lax.broadcasted_iota(jnp.int32, shape, dim)


def to_column(row):
    size = row.shape[1]
    square = jnp.broadcast_to(row, (size, size))
    diagonal = iota((size, size), 0) == iota((size, size), 1)
    return jnp.sum(jnp.where(diagonal, square, jnp.zeros_like(square)), axis=1, keepdims=True)


def kernel(
    residual, mixer, floor, taps, edges, state, accepted, home, gain_mixer,
    w_out, gain_mlp, w_gate, w_up, w_down, gain_next, w_next,
    next_out, kept_out, edge_out,
    mix_v, pair, state_v, res_v, wo, wgu, wd, wn,
    query_b, key_b, decay, values, picked, gained_own, gained_send, gained_recv,
    send1, recv1, gather1, first_v, send2, recv2, gather2,
    next_send, next_recv, kept_v, edge_v, kept_all, edge_all,
    load_sem, pair_ss, pair_rs, ss1, rs1, ss2, rs2, ss3, rs3, ss4, rs4, ss_x, rs_x,
):
    member = lax.axis_index("req")
    group = lax.axis_index("grp")
    core = member % 2
    chip = member // 2
    at_y = chip // SIDE
    at_z = chip % SIDE
    sibling = {"req": chip * 2 + (1 - core), "grp": group}

    def peer_chip(k):
        return ((at_y + k // SIDE) % SIDE) * SIDE + (at_z + k % SIDE) % SIDE

    def peer(k):
        return {"req": peer_chip(k) * 2 + core, "grp": group}

    def across(k):
        return {"req": member, "grp": (group + k) % GROUPS}

    barrier = pltpu.get_barrier_semaphore()

    def greet(k, carry):
        pl.semaphore_signal(barrier, inc=1, device_id=peer(k), device_id_type=MESH)
        return carry

    pl.semaphore_signal(barrier, inc=1, device_id=sibling, device_id_type=MESH)
    lax.fori_loop(1, CHIPS, greet, 0)
    for k in range(1, GROUPS):
        pl.semaphore_signal(barrier, inc=1, device_id=across(k), device_id_type=MESH)

    loads = [
        pltpu.make_async_copy(mixer, mix_v, load_sem.at[0]),
        pltpu.make_async_copy(state, state_v, load_sem.at[1]),
        pltpu.make_async_copy(w_out, wo.at[core], load_sem.at[2]),
        pltpu.make_async_copy(w_gate, wgu.at[0, core], load_sem.at[4]),
        pltpu.make_async_copy(w_up, wgu.at[1, core], load_sem.at[5]),
        pltpu.make_async_copy(w_down, wd.at[core], load_sem.at[6]),
        pltpu.make_async_copy(w_next, wn.at[core], load_sem.at[7]),
    ]
    for c in range(CHUNKS):
        near = core * MINE + c * PART + chip // 2 * (2 * ROWS)
        loads.append(pltpu.make_async_copy(
            residual.at[pl.ds(pl.multiple_of(near, 2 * ROWS), 2 * ROWS)], res_v.at[c], load_sem.at[8 + c]))
    for load in loads:
        load.start()

    def to_sibling(source, target, slot):
        return pltpu.make_async_remote_copy(
            src_ref=source, dst_ref=target, send_sem=pair_ss.at[slot], recv_sem=pair_rs.at[slot],
            device_id=sibling, device_id_type=MESH)

    pl.semaphore_wait(barrier, CHIPS + GROUPS - 1)
    halves = to_sibling(mixer.at[0:2], pair.at[:, core], 0)
    halves.start()
    shared = [
        to_sibling(w_out, wo.at[core], 1),
        to_sibling(w_gate, wgu.at[0, core], 2),
        to_sibling(w_up, wgu.at[1, core], 3),
        to_sibling(w_down, wd.at[core], 4),
        to_sibling(w_next, wn.at[core], 5),
    ]
    for copy in shared:
        copy.start()

    loads[0].wait()
    lane = iota((1, TOKENS), 1)
    step_of = lane % STEPS
    inputs_raw = mix_v[2]
    inputs_f = inputs_raw.astype(F32)
    stacked = jnp.concatenate([edges[i] for i in range(EDGES)], axis=0)
    row96 = iota((EDGES * REQUESTS, TOKENS), 0)
    lane96 = iota((EDGES * REQUESTS, TOKENS), 1)
    conv = to_column(taps[TAPS - 1:TAPS, :]) * inputs_f
    for j in range(TAPS - 1):
        shift = TAPS - 1 - j
        early = row96 // REQUESTS - j
        place = (early >= 0) & (lane96 == (row96 % REQUESTS) * STEPS + early)
        from_edges = dot(stacked, jnp.where(place, 1.0, 0.0).astype(BF16), TN)
        moved = jnp.where(step_of >= shift, pltpu.roll(inputs_f, shift, axis=1), 0.0)
        conv = conv + to_column(taps[j:j + 1, :]) * (moved + from_edges)
    values[...] = conv.astype(BF16)

    pair[:, core] = mix_v[0:2]
    floor_row = floor[pl.ds(chip, 1), :]
    low = to_column(floor_row)
    halves.wait()
    for tile in range(TOKENS // TILE):
        at = slice(tile * TILE, (tile + 1) * TILE)
        step_t = iota((KEYS, TILE), 1) % STEPS
        q_pre = pair[0, :, :, at].reshape(KEYS, TILE).astype(F32)
        f_pre = pair[1, :, :, at].reshape(KEYS, TILE).astype(F32)
        query = q_pre * jax.nn.sigmoid(q_pre)
        forget = low + (1.0 - low) * jax.nn.sigmoid(f_pre)
        keyed = 1.0 - forget
        run = forget
        for shift in (1, 2, 4, 8):
            run = jnp.where(step_t >= shift, run * pltpu.roll(run, shift, axis=1), run)
        decay[:, at] = run
        query_b[:, at] = (query * run).astype(BF16)
        key_b[:, at] = (keyed / run).astype(BF16)

    loads[1].wait()
    gain_column = to_column(gain_mixer[...])
    squares = []
    for tile in range(TOKENS // TILE):
        at = slice(tile * TILE, (tile + 1) * TILE)
        q_t = query_b[:, at]
        begin = state_v[tile * TILE_REQ:(tile + 1) * TILE_REQ].astype(BF16).reshape(TILE_REQ * HALF, KEYS)
        through = dot(begin, q_t).reshape(TILE_REQ, HALF, TILE)
        ours = iota((TILE_REQ, HALF, TILE), 0) == iota((TILE_REQ, HALF, TILE), 2) // STEPS
        total = jnp.sum(jnp.where(ours, through, 0.0), axis=0)
        scores = dot(key_b[:, at], q_t, TN)
        source = iota((TILE, TILE), 0)
        sink = iota((TILE, TILE), 1)
        causal = (source // STEPS == sink // STEPS) & (source <= sink)
        scores = jnp.where(causal, scores, 0.0).astype(BF16)
        total = (total + dot(values[:, at], scores)) * KEYS ** (-0.5)
        gained_own[0:HALF, at] = (total * gain_column).astype(BF16)
        square = jnp.sum(total * total, axis=0, keepdims=True)
        gained_own[HALF:HALF + STEPS, at] = jnp.broadcast_to(square, (STEPS, TILE)).astype(BF16)

    own_lanes = pl.ds(pl.multiple_of(core * MINE, MINE), MINE)
    other_lanes = pl.ds(pl.multiple_of((1 - core) * MINE, MINE), MINE)
    gained_send[...] = gained_own[:, other_lanes]
    swap = to_sibling(gained_send, gained_recv, 6)
    swap.start()
    mine = gained_own[:, own_lanes]
    swap.wait()
    theirs = gained_recv[...]
    lower = jnp.where(core == 0, mine[0:HALF], theirs[0:HALF])
    upper = jnp.where(core == 0, theirs[0:HALF], mine[0:HALF])
    both = jnp.concatenate([lower, upper], axis=0)
    loads[2].wait()
    shared[0].wait()
    squares2 = jnp.concatenate([mine[HALF:], theirs[HALF:]], axis=0)
    pick_one = jnp.where(iota((2 * STEPS, EXTRA), 0) % STEPS == 0, 1.0, 0.0).astype(BF16)
    cut = 512

    def folded(low_part, high_part):
        width = low_part.shape[1]
        return jnp.concatenate(
            [low_part.reshape(CHIPS, ROWS, width), high_part.reshape(CHIPS, ROWS, width)], axis=1
        ).astype(BF16)

    def scatter(source, target, ssem, rsem, c):
        def copy(k):
            return pltpu.make_async_remote_copy(
                src_ref=source.at[c, peer_chip(k)], dst_ref=target.at[c, k], send_sem=ssem.at[c, k],
                recv_sem=rsem.at[c, k], device_id=peer(k), device_id_type=MESH)
        return copy

    def gather(target, ssem, rsem, c):
        def copy(k):
            return pltpu.make_async_remote_copy(
                src_ref=target.at[c, chip], dst_ref=target.at[c, chip], send_sem=ssem.at[c, k],
                recv_sem=rsem.at[c, k], device_id=peer(k), device_id_type=MESH)
        return copy

    def start_all(copy):
        def body(k, carry):
            copy(k).start()
            return carry
        lax.fori_loop(1, CHIPS, body, 0)

    def wait_all(copy):
        def body(k, carry):
            copy(k).wait_recv()
            return carry
        lax.fori_loop(1, CHIPS, body, 0)

    def drain(copy):
        def body(k, carry):
            copy(k).wait_send()
            return carry
        lax.fori_loop(1, CHIPS, body, 0)

    copy1 = [scatter(send1, recv1, ss1, rs1, c) for c in range(CHUNKS)]
    copy2 = [gather(gather1, ss2, rs2, c) for c in range(CHUNKS)]
    copy3 = [scatter(send2, recv2, ss3, rs3, c) for c in range(CHUNKS)]
    copy4 = [gather(gather2, ss4, rs4, c) for c in range(CHUNKS)]

    for c in range(CHUNKS):
        part = slice(c * PART, (c + 1) * PART)
        square = dot(squares2[:, part], pick_one, TN)
        send1[c, :, :, FOLD:] = folded(square, square)
        channels = both[:, part]

        def project(n, carry):
            at = pl.ds(pl.multiple_of(n * cut, cut), cut)
            above = pl.ds(pl.multiple_of(FOLD + n * cut, cut), cut)
            send1[c, :, :, at] = folded(
                dot(channels, wo[:, :, at].reshape(2 * HALF, cut), TN),
                dot(channels, wo[:, :, above].reshape(2 * HALF, cut), TN))
            return carry

        lax.fori_loop(0, FOLD // cut, project, 0)
        start_all(copy1[c])
        recv1[c, 0] = send1[c, chip]

    acc_column = to_column(accepted[...])
    row32 = iota((REQUESTS, TOKENS), 0)
    lane32 = iota((REQUESTS, TOKENS), 1)
    acc_lanes = jnp.sum(jnp.where(lane32 // STEPS == row32, acc_column, 0), axis=0, keepdims=True)
    last = jnp.where(lane32 == row32 * STEPS + acc_column - 1, 1.0, 0.0)
    last = jnp.where(acc_column > 0, last, 0.0).astype(BF16)
    run_all = decay[...]
    run_high = run_all.astype(BF16)
    run_low = (run_all - run_high.astype(F32)).astype(BF16)
    run_picked = dot(last, run_high, NT) + dot(last, run_low, NT)
    picked[...] = jnp.where(acc_column == 0, 1.0, run_picked)
    live = step_of < acc_lanes
    for tile in range(TOKENS // TILE):
        at = slice(tile * TILE, (tile + 1) * TILE)
        taken = jnp.where(live[:, at], values[:, at].astype(F32), 0.0)
        spread = jnp.broadcast_to(taken[None], (TILE_REQ, HALF, TILE))
        ours = iota((TILE_REQ, HALF, TILE), 0) == iota((TILE_REQ, HALF, TILE), 2) // STEPS
        spread = jnp.where(ours, spread, 0.0).astype(BF16).reshape(TILE_REQ * HALF, TILE)
        added = dot(spread, key_b[:, at], NT)
        for i in range(TILE_REQ):
            r = tile * TILE_REQ + i
            kept_v[r] = (picked[r:r + 1, :] * (state_v[r] + added[i * HALF:(i + 1) * HALF])).astype(BF16)
    for e in range(EDGES):
        place = jnp.where(lane32 == row32 * STEPS + acc_column + (e - EDGES), 1.0, 0.0)
        place = jnp.where(acc_column + e >= EDGES, place, 0.0).astype(BF16)
        kept_edge = dot(place, inputs_raw, NT)
        for i in range(EDGES):
            kept_edge = kept_edge + jnp.where(acc_column + e == i, edges[i].astype(F32), 0.0)
        edge_v[e] = kept_edge.astype(BF16)

    def cross(k):
        return [
            pltpu.make_async_remote_copy(
                src_ref=source, dst_ref=target.at[group], send_sem=ss_x.at[slot, k],
                recv_sem=rs_x.at[slot, k], device_id=across(k), device_id_type=MESH)
            for slot, (source, target) in enumerate(((kept_v, kept_all), (edge_v, edge_all)))
        ]

    crossing = [copy for k in range(1, GROUPS) for copy in cross(k)]
    for copy in crossing:
        copy.start()
    kept_all[group] = kept_v[...]
    edge_all[group] = edge_v[...]

    def total_of(ref, c):
        def add(k, sums):
            return sums + ref[c, k].astype(F32)
        return lax.fori_loop(1, CHIPS, add, ref[c, 0].astype(F32))

    def unfold(block):
        return jnp.concatenate([block[0:ROWS], block[ROWS:]], axis=1)

    def fold(rows):
        return jnp.concatenate([rows[:, 0:FOLD], rows[:, FOLD:]], axis=0)

    def scaled_norm(rows, gain):
        factor = lax.rsqrt(jnp.mean(rows * rows, axis=1, keepdims=True) + EPSILON)
        return rows * factor * gain

    def all_rows(ref, c):
        blocks = ref[c].astype(F32)
        low_part = blocks[:, 0:ROWS].reshape(PART, FOLD)
        high_part = blocks[:, ROWS:].reshape(PART, FOLD)
        return jnp.concatenate([low_part, high_part], axis=1).astype(BF16)

    for load in loads[3:]:
        load.wait()
    for c in range(CHUNKS):
        wait_all(copy1[c])
        sums = total_of(recv1, c)
        near = res_v[c].astype(F32)
        before = jnp.where(chip % 2 == 0, near[0:ROWS], near[ROWS:])
        square = sums[0:ROWS, FOLD:FOLD + 1]
        attn = unfold(sums[:, 0:FOLD]) * lax.rsqrt(square / WIDTH + EPSILON)
        first = (before + attn).astype(BF16).astype(F32)
        first_v[c] = first
        gather1[c, chip] = fold(scaled_norm(first, gain_mlp[...])).astype(BF16)
        start_all(copy2[c])
    for c in range(CHUNKS):
        drain(copy1[c])
    for copy in shared[1:]:
        copy.wait()

    hidden_width = wd.shape[0] * wd.shape[1]
    for c in range(CHUNKS):
        wait_all(copy2[c])
        both_parts = dot(wgu[...].reshape(2 * hidden_width, WIDTH), all_rows(gather1, c), NT)
        gate = both_parts[0:hidden_width]
        hidden = (gate * jax.nn.sigmoid(gate) * both_parts[hidden_width:]).astype(BF16)

        def lower_part(n, carry):
            at = pl.ds(pl.multiple_of(n * cut, cut), cut)
            above = pl.ds(pl.multiple_of(FOLD + n * cut, cut), cut)
            send2[c, :, :, at] = folded(
                dot(hidden, wd[:, :, at].reshape(hidden_width, cut), TN),
                dot(hidden, wd[:, :, above].reshape(hidden_width, cut), TN))
            return carry

        lax.fori_loop(0, FOLD // cut, lower_part, 0)
        start_all(copy3[c])
        recv2[c, 0] = send2[c, chip]
    for c in range(CHUNKS):
        drain(copy2[c])

    for copy in crossing:
        copy.wait()
    home_row = home[...]
    source_lane = iota((1, GROUPS * REQUESTS), 1)
    for i in range(REQUESTS):
        found = jnp.max(jnp.where(home_row == group * REQUESTS + i, source_lane, 0))
        kept_out[i] = kept_all[found // REQUESTS, found % REQUESTS]
    target_row = iota((REQUESTS, GROUPS * REQUESTS), 0) + group * REQUESTS
    chosen = jnp.where(home_row == target_row, 1.0, 0.0).astype(BF16)
    for e in range(EDGES):
        pool = edge_all[:, e].reshape(GROUPS * REQUESTS, HALF)
        edge_out[e] = dot(chosen, pool).astype(BF16)

    for c in range(CHUNKS):
        wait_all(copy3[c])
        second = (first_v[c] + unfold(total_of(recv2, c))).astype(BF16).astype(F32)
        gather2[c, chip] = fold(scaled_norm(second, gain_next[...])).astype(BF16)
        start_all(copy4[c])
    for c in range(CHUNKS):
        drain(copy3[c])

    swaps = []
    for c in range(CHUNKS):
        wait_all(copy4[c])
        normed = all_rows(gather2, c)
        theirs_next = dot(wn[1 - core].reshape(3 * HALF, WIDTH), normed, NT)
        next_send[c] = theirs_next.astype(BF16).reshape(3, HALF, PART)
        swaps.append(to_sibling(next_send.at[c], next_recv.at[c], 7 + c))
        swaps[c].start()
        own_next = dot(wn[core].reshape(3 * HALF, WIDTH), normed, NT)
        here = pl.ds(pl.multiple_of(core * MINE + c * PART, PART), PART)
        next_out[:, :, here] = own_next.astype(BF16).reshape(3, HALF, PART)
    for c in range(CHUNKS):
        drain(copy4[c])
        swaps[c].wait()
        there = pl.ds(pl.multiple_of((1 - core) * MINE + c * PART, PART), PART)
        next_out[:, :, there] = next_recv[c]


def per_device(
    residual_in, mixer_in, forget_floor, conv_weight, conv_edges, state_in, accepted, home_slot,
    gain_mixer, w_out, gain_mlp, w_gate, w_up, w_down, gain_next, w_next,
):
    hidden_width = w_gate.shape[1]
    anywhere = pl.BlockSpec(memory_space=pl.ANY)
    vmem = pl.BlockSpec(memory_space=pltpu.VMEM)
    dma = pltpu.SemaphoreType.DMA
    next_flat, kept, kept_edges = pl.pallas_call(
        kernel,
        name="draft_check",
        out_shape=(
            jax.ShapeDtypeStruct((3, HALF, TOKENS), BF16),
            jax.ShapeDtypeStruct((REQUESTS, HALF, KEYS), BF16),
            jax.ShapeDtypeStruct((EDGES, REQUESTS, HALF), BF16),
        ),
        in_specs=[
            anywhere, anywhere, vmem, vmem, vmem, anywhere, vmem, vmem, vmem,
            anywhere, vmem, anywhere, anywhere, anywhere, vmem, anywhere,
        ],
        out_specs=(vmem, vmem, vmem),
        scratch_shapes=[
            pltpu.VMEM((3, HALF, TOKENS), BF16),
            pltpu.VMEM((2, 2, HALF, TOKENS), BF16),
            pltpu.VMEM((REQUESTS, HALF, KEYS), F32),
            pltpu.VMEM((CHUNKS, 2 * ROWS, WIDTH), BF16),
            pltpu.VMEM((2, HALF, WIDTH), BF16),
            pltpu.VMEM((2, 2, hidden_width, WIDTH), BF16),
            pltpu.VMEM((2, hidden_width, WIDTH), BF16),
            pltpu.VMEM((2, 3, HALF, WIDTH), BF16),
            pltpu.VMEM((KEYS, TOKENS), BF16),
            pltpu.VMEM((KEYS, TOKENS), BF16),
            pltpu.VMEM((KEYS, TOKENS), F32),
            pltpu.VMEM((HALF, TOKENS), BF16),
            pltpu.VMEM((REQUESTS, KEYS), F32),
            pltpu.VMEM((HALF + STEPS, TOKENS), BF16),
            pltpu.VMEM((HALF + STEPS, MINE), BF16),
            pltpu.VMEM((HALF + STEPS, MINE), BF16),
            pltpu.VMEM((CHUNKS, CHIPS, 2 * ROWS, FOLD + EXTRA), BF16),
            pltpu.VMEM((CHUNKS, CHIPS, 2 * ROWS, FOLD + EXTRA), BF16),
            pltpu.VMEM((CHUNKS, CHIPS, 2 * ROWS, FOLD), BF16),
            pltpu.VMEM((CHUNKS, ROWS, WIDTH), F32),
            pltpu.VMEM((CHUNKS, CHIPS, 2 * ROWS, FOLD), BF16),
            pltpu.VMEM((CHUNKS, CHIPS, 2 * ROWS, FOLD), BF16),
            pltpu.VMEM((CHUNKS, CHIPS, 2 * ROWS, FOLD), BF16),
            pltpu.VMEM((CHUNKS, 3, HALF, PART), BF16),
            pltpu.VMEM((CHUNKS, 3, HALF, PART), BF16),
            pltpu.VMEM((REQUESTS, HALF, KEYS), BF16),
            pltpu.VMEM((EDGES, REQUESTS, HALF), BF16),
            pltpu.VMEM((GROUPS, REQUESTS, HALF, KEYS), BF16),
            pltpu.VMEM((GROUPS, EDGES, REQUESTS, HALF), BF16),
            dma((8 + CHUNKS,)), dma((7 + CHUNKS,)), dma((7 + CHUNKS,)),
            *[dma((CHUNKS, CHIPS))] * 8,
            dma((2, GROUPS)), dma((2, GROUPS)),
        ],
        compiler_params=pltpu.CompilerParams(
            collective_id=0, has_side_effects=True, vmem_limit_bytes=56 * 2**20),
    )(
        residual_in,
        mixer_in.transpose(1, 2, 0),
        forget_floor.reshape(-1, KEYS),
        conv_weight,
        conv_edges.transpose(1, 0, 2),
        state_in,
        accepted.reshape(1, -1),
        home_slot.reshape(1, -1),
        gain_mixer.reshape(1, -1),
        w_out,
        gain_mlp.reshape(1, -1),
        w_gate.T,
        w_up.T,
        w_down,
        gain_next.reshape(1, -1),
        w_next.transpose(1, 2, 0),
    )
    return (
        next_flat.transpose(2, 0, 1),
        kept.astype(F32),
        kept_edges.transpose(1, 0, 2),
    )


def solution(mesh):
    in_specs = (
        P("grp", None),
        P("grp", None, "req"),
        P(),
        P(None, "req"),
        P("grp", None, "req"),
        P("grp", "req", None),
        P("grp"),
        P(),
        P("req"),
        P("req", None),
        P(),
        P(None, "req"),
        P(None, "req"),
        P("req", None),
        P(),
        P(None, None, "req"),
    )
    out_specs = (P("grp", None, "req"), P("grp", "req", None), P("grp", None, "req"))
    return jax.shard_map(
        per_device, mesh=mesh, in_specs=in_specs, out_specs=out_specs, check_vma=False
    )
```

```python
import jax
import jax.numpy as jnp
from jax import lax
from jax.experimental import pallas as pl
from jax.experimental.pallas import tpu as pltpu
from jax.sharding import PartitionSpec as P

EPSILON = 1e-06
MESH = pl.DeviceIdType.MESH
F32 = jnp.float32
BF16 = jnp.bfloat16

SIDE = 4
CHIPS = SIDE * SIDE
GROUPS = 4
STEPS = 16
TAPS = 4
EDGES = 3
WIDTH = 2048
HALF = 64
KEYS = 128
EXTRA = 128
REQUESTS = 32
TOKENS = REQUESTS * STEPS
MINE = TOKENS // 2
TILE = 128
TILE_REQ = TILE // STEPS
CHUNKS = 2
PART = MINE // CHUNKS
ROWS = PART // CHIPS
FOLD = WIDTH // 2
LANES = FOLD // 2

NT = (((1,), (1,)), ((), ()))
TN = (((0,), (0,)), ((), ()))


def dot(left, right, dims=(((1,), (0,)), ((), ()))):
    return lax.dot_general(left, right, dims, preferred_element_type=F32)


def iota(shape, dim):
    return lax.broadcasted_iota(jnp.int32, shape, dim)


def to_column(row):
    size = row.shape[1]
    square = jnp.broadcast_to(row, (size, size))
    diagonal = iota((size, size), 0) == iota((size, size), 1)
    return jnp.sum(jnp.where(diagonal, square, jnp.zeros_like(square)), axis=1, keepdims=True)


def kernel(
    residual, mixer, floor, taps, edges, state, accepted, home, gain_mixer,
    w_out, gain_mlp, w_gate, w_up, w_down, gain_next, w_next,
    next_out, kept_out, edge_out,
    mix_v, pair, state_v, res_v, wo, wgu, wd, wn,
    query_b, key_b, decay, values, picked, gained_own, gained_send, gained_recv,
    send1a, send1b, early1a, early1b, middle1a, middle1b, late1a, late1b, gather1a, gather1b, first_v,
    send2a, send2b, early2a, early2b, middle2a, middle2b, late2a, late2b, gather2a, gather2b,
    next_send, next_recv, kept_v, edge_v, kept_all, edge_all,
    load_sem, pair_ss, pair_rs, ss1, rs1, ss2, rs2, ss3, rs3, ss4, rs4, ss_x, rs_x,
):
    member = lax.axis_index("req")
    group = lax.axis_index("grp")
    core = member % 2
    chip = member // 2
    at_y = chip // SIDE
    at_z = chip % SIDE
    sibling = {"req": chip * 2 + (1 - core), "grp": group}

    def along(axis, k):
        if axis == 0:
            chip_at = (at_y + k) % SIDE * SIDE + at_z
        else:
            chip_at = at_y * SIDE + (at_z + k) % SIDE
        return {"req": chip_at * 2 + core, "grp": group}

    places = (at_y, at_z)

    def across(k):
        return {"req": member, "grp": (group + k) % GROUPS}

    barrier = pltpu.get_barrier_semaphore()

    pl.semaphore_signal(barrier, inc=1, device_id=sibling, device_id_type=MESH)
    for axis in range(2):
        for k in range(1, SIDE):
            pl.semaphore_signal(barrier, inc=1, device_id=along(axis, k), device_id_type=MESH)
    for k in range(1, GROUPS):
        pl.semaphore_signal(barrier, inc=1, device_id=across(k), device_id_type=MESH)

    loads = [
        pltpu.make_async_copy(mixer, mix_v, load_sem.at[0]),
        pltpu.make_async_copy(state, state_v, load_sem.at[1]),
        pltpu.make_async_copy(w_out, wo.at[core], load_sem.at[2]),
        pltpu.make_async_copy(w_gate, wgu.at[0, core], load_sem.at[4]),
        pltpu.make_async_copy(w_up, wgu.at[1, core], load_sem.at[5]),
        pltpu.make_async_copy(w_down, wd.at[core], load_sem.at[6]),
        pltpu.make_async_copy(w_next, wn.at[core], load_sem.at[7]),
    ]
    for c in range(CHUNKS):
        near = core * MINE + c * PART + chip // 2 * (2 * ROWS)
        loads.append(pltpu.make_async_copy(
            residual.at[pl.ds(pl.multiple_of(near, 2 * ROWS), 2 * ROWS)], res_v.at[c], load_sem.at[8 + c]))
    for load in loads:
        load.start()

    def to_sibling(source, target, slot):
        return pltpu.make_async_remote_copy(
            src_ref=source, dst_ref=target, send_sem=pair_ss.at[slot], recv_sem=pair_rs.at[slot],
            device_id=sibling, device_id_type=MESH)

    pl.semaphore_wait(barrier, 1 + 2 * (SIDE - 1) + GROUPS - 1)
    halves = to_sibling(mixer.at[0:2], pair.at[:, core], 0)
    halves.start()
    shared = [
        to_sibling(w_out, wo.at[core], 1),
        to_sibling(w_gate, wgu.at[0, core], 2),
        to_sibling(w_up, wgu.at[1, core], 3),
        to_sibling(w_down, wd.at[core], 4),
        to_sibling(w_next, wn.at[core], 5),
    ]
    for copy in shared:
        copy.start()

    loads[0].wait()
    lane = iota((1, TOKENS), 1)
    step_of = lane % STEPS
    inputs_raw = mix_v[2]
    inputs_f = inputs_raw.astype(F32)
    stacked = jnp.concatenate([edges[i] for i in range(EDGES)], axis=0)
    row96 = iota((EDGES * REQUESTS, TOKENS), 0)
    lane96 = iota((EDGES * REQUESTS, TOKENS), 1)
    conv = to_column(taps[TAPS - 1:TAPS, :]) * inputs_f
    for j in range(TAPS - 1):
        shift = TAPS - 1 - j
        early = row96 // REQUESTS - j
        place = (early >= 0) & (lane96 == (row96 % REQUESTS) * STEPS + early)
        from_edges = dot(stacked, jnp.where(place, 1.0, 0.0).astype(BF16), TN)
        moved = jnp.where(step_of >= shift, pltpu.roll(inputs_f, shift, axis=1), 0.0)
        conv = conv + to_column(taps[j:j + 1, :]) * (moved + from_edges)
    values[...] = conv.astype(BF16)

    pair[:, core] = mix_v[0:2]
    floor_row = floor[pl.ds(chip, 1), :]
    low = to_column(floor_row)
    halves.wait()
    for tile in range(TOKENS // TILE):
        at = slice(tile * TILE, (tile + 1) * TILE)
        step_t = iota((KEYS, TILE), 1) % STEPS
        q_pre = pair[0, :, :, at].reshape(KEYS, TILE).astype(F32)
        f_pre = pair[1, :, :, at].reshape(KEYS, TILE).astype(F32)
        query = q_pre * jax.nn.sigmoid(q_pre)
        forget = low + (1.0 - low) * jax.nn.sigmoid(f_pre)
        keyed = 1.0 - forget
        run = forget
        for shift in (1, 2, 4, 8):
            run = jnp.where(step_t >= shift, run * pltpu.roll(run, shift, axis=1), run)
        decay[:, at] = run
        query_b[:, at] = (query * run).astype(BF16)
        key_b[:, at] = (keyed / run).astype(BF16)

    loads[1].wait()
    gain_column = to_column(gain_mixer[...])
    squares = []
    for tile in range(TOKENS // TILE):
        at = slice(tile * TILE, (tile + 1) * TILE)
        q_t = query_b[:, at]
        begin = state_v[tile * TILE_REQ:(tile + 1) * TILE_REQ].astype(BF16).reshape(TILE_REQ * HALF, KEYS)
        through = dot(begin, q_t).reshape(TILE_REQ, HALF, TILE)
        ours = iota((TILE_REQ, HALF, TILE), 0) == iota((TILE_REQ, HALF, TILE), 2) // STEPS
        total = jnp.sum(jnp.where(ours, through, 0.0), axis=0)
        scores = dot(key_b[:, at], q_t, TN)
        source = iota((TILE, TILE), 0)
        sink = iota((TILE, TILE), 1)
        causal = (source // STEPS == sink // STEPS) & (source <= sink)
        scores = jnp.where(causal, scores, 0.0).astype(BF16)
        total = (total + dot(values[:, at], scores)) * KEYS ** (-0.5)
        gained_own[0:HALF, at] = (total * gain_column).astype(BF16)
        square = jnp.sum(total * total, axis=0, keepdims=True)
        gained_own[HALF:HALF + STEPS, at] = jnp.broadcast_to(square, (STEPS, TILE)).astype(BF16)

    own_lanes = pl.ds(pl.multiple_of(core * MINE, MINE), MINE)
    other_lanes = pl.ds(pl.multiple_of((1 - core) * MINE, MINE), MINE)
    gained_send[...] = gained_own[:, other_lanes]
    swap = to_sibling(gained_send, gained_recv, 6)
    swap.start()
    mine = gained_own[:, own_lanes]
    swap.wait()
    theirs = gained_recv[...]
    lower = jnp.where(core == 0, mine[0:HALF], theirs[0:HALF])
    upper = jnp.where(core == 0, theirs[0:HALF], mine[0:HALF])
    both = jnp.concatenate([lower, upper], axis=0)
    loads[2].wait()
    shared[0].wait()
    squares2 = jnp.concatenate([mine[HALF:], theirs[HALF:]], axis=0)
    pick_one = jnp.where(iota((2 * STEPS, EXTRA), 0) % STEPS == 0, 1.0, 0.0).astype(BF16)

    def folded(low_part, high_part):
        width = low_part.shape[1]
        return jnp.concatenate(
            [low_part.reshape(CHIPS, ROWS, width), high_part.reshape(CHIPS, ROWS, width)], axis=1
        ).astype(BF16)

    def put(blocks, ref, c, axis):
        width = blocks.shape[2]
        blocks = blocks.reshape(SIDE, SIDE, 2 * ROWS, width)
        if axis == 0:
            ref[c, :, :, :, 0:width] = blocks
        else:
            for y in range(SIDE):
                ref[c, :, y, :, 0:width] = blocks[y]

    def link(source, target, ssem, rsem, c, axis, stage, k, towards):
        return pltpu.make_async_remote_copy(
            src_ref=source, dst_ref=target, send_sem=ssem.at[c, axis, stage, k],
            recv_sem=rsem.at[c, axis, stage, k], device_id=along(towards, k), device_id_type=MESH)

    class Sum:
        def __init__(self, sends, early, middle, late, sems):
            self.sends, self.early, self.middle, self.late, self.sems = sends, early, middle, late, sems

        def first(self, c, axis):
            return [
                link(self.sends[axis].at[c, (places[axis] + k) % SIDE], self.early[axis].at[c, k],
                     *self.sems, c, axis, 0, k, axis)
                for k in range(1, SIDE)
            ]

        def second(self, c, axis):
            other = 1 - axis
            return [
                link(self.middle[axis].at[c, (places[other] + k) % SIDE], self.late[axis].at[c, k],
                     *self.sems, c, axis, 1, k, other)
                for k in range(1, SIDE)
            ]

        def begin(self, c, axis):
            for copy in self.first(c, axis):
                copy.start()

        def turn(self, c, axis):
            for copy in self.first(c, axis):
                copy.wait_recv()
            sums = self.sends[axis][c, places[axis]].astype(F32)
            for k in range(1, SIDE):
                sums = sums + self.early[axis][c, k].astype(F32)
            self.middle[axis][c] = sums.astype(BF16)
            for copy in self.second(c, axis):
                copy.start()

        def end(self, c, axis):
            for copy in self.second(c, axis):
                copy.wait_recv()
            sums = self.middle[axis][c, places[1 - axis]].astype(F32)
            for k in range(1, SIDE):
                sums = sums + self.late[axis][c, k].astype(F32)
            return sums

        def drain(self, c, axis):
            for copy in self.first(c, axis) + self.second(c, axis):
                copy.wait_send()

    class Gather:
        def __init__(self, refs, sems):
            self.refs, self.sems = refs, sems

        def first(self, c, axis):
            other = 1 - axis
            mine_at = self.refs[axis].at[c, places[axis], places[other]]
            return [link(mine_at, mine_at, *self.sems, c, axis, 0, k, other) for k in range(1, SIDE)]

        def second(self, c, axis):
            mine_at = self.refs[axis].at[c, places[axis]]
            return [link(mine_at, mine_at, *self.sems, c, axis, 1, k, axis) for k in range(1, SIDE)]

        def begin(self, c, rows):
            block = jnp.concatenate([rows[:, 0:FOLD], rows[:, FOLD:]], axis=0).astype(BF16)
            for axis in range(2):
                self.refs[axis][c, places[axis], places[1 - axis]] = block[:, axis * LANES:(axis + 1) * LANES]
                for copy in self.first(c, axis):
                    copy.start()

        def turn(self, c):
            for axis in range(2):
                for copy in self.first(c, axis):
                    copy.wait_recv()
                for copy in self.second(c, axis):
                    copy.start()

        def end(self, c):
            for axis in range(2):
                for copy in self.second(c, axis):
                    copy.wait_recv()
            pieces = [[], []]
            for axis in range(2):
                if axis == 0:
                    blocks = self.refs[axis][c].astype(F32)
                else:
                    blocks = jnp.stack([self.refs[axis][c, :, y] for y in range(SIDE)], axis=0).astype(F32)
                blocks = blocks.reshape(CHIPS, 2 * ROWS, LANES)
                pieces[0].append(blocks[:, 0:ROWS].reshape(PART, LANES))
                pieces[1].append(blocks[:, ROWS:].reshape(PART, LANES))
            return jnp.concatenate(pieces[0] + pieces[1], axis=1).astype(BF16)

        def drain(self, c):
            for axis in range(2):
                for copy in self.first(c, axis) + self.second(c, axis):
                    copy.wait_send()

    def unfold(left, right):
        return jnp.concatenate([left[0:ROWS], right[0:ROWS], left[ROWS:], right[ROWS:]], axis=1)

    sum1 = Sum((send1a, send1b), (early1a, early1b), (middle1a, middle1b), (late1a, late1b), (ss1, rs1))
    spread1 = Gather((gather1a, gather1b), (ss2, rs2))
    sum2 = Sum((send2a, send2b), (early2a, early2b), (middle2a, middle2b), (late2a, late2b), (ss3, rs3))
    spread2 = Gather((gather2a, gather2b), (ss4, rs4))

    for c in range(CHUNKS):
        part = slice(c * PART, (c + 1) * PART)
        square = dot(squares2[:, part], pick_one, TN)
        square = folded(square, square).reshape(SIDE, SIDE, 2 * ROWS, EXTRA)
        send1a[c, :, :, :, LANES:] = square
        channels = both[:, part]
        for axis in range(2):
            low_at = slice(axis * LANES, (axis + 1) * LANES)
            high_at = slice(FOLD + axis * LANES, FOLD + (axis + 1) * LANES)
            put(folded(
                dot(channels, wo[:, :, low_at].reshape(2 * HALF, LANES), TN),
                dot(channels, wo[:, :, high_at].reshape(2 * HALF, LANES), TN),
            ), sum1.sends[axis], c, axis)
            sum1.begin(c, axis)

    acc_column = to_column(accepted[...])
    row32 = iota((REQUESTS, TOKENS), 0)
    lane32 = iota((REQUESTS, TOKENS), 1)
    acc_lanes = jnp.sum(jnp.where(lane32 // STEPS == row32, acc_column, 0), axis=0, keepdims=True)
    last = jnp.where(lane32 == row32 * STEPS + acc_column - 1, 1.0, 0.0)
    last = jnp.where(acc_column > 0, last, 0.0).astype(BF16)
    run_all = decay[...]
    run_high = run_all.astype(BF16)
    run_low = (run_all - run_high.astype(F32)).astype(BF16)
    run_picked = dot(last, run_high, NT) + dot(last, run_low, NT)
    picked[...] = jnp.where(acc_column == 0, 1.0, run_picked)
    live = step_of < acc_lanes
    for tile in range(TOKENS // TILE):
        at = slice(tile * TILE, (tile + 1) * TILE)
        taken = jnp.where(live[:, at], values[:, at].astype(F32), 0.0)
        spread = jnp.broadcast_to(taken[None], (TILE_REQ, HALF, TILE))
        ours = iota((TILE_REQ, HALF, TILE), 0) == iota((TILE_REQ, HALF, TILE), 2) // STEPS
        spread = jnp.where(ours, spread, 0.0).astype(BF16).reshape(TILE_REQ * HALF, TILE)
        added = dot(spread, key_b[:, at], NT)
        for i in range(TILE_REQ):
            r = tile * TILE_REQ + i
            kept_v[r] = (picked[r:r + 1, :] * (state_v[r] + added[i * HALF:(i + 1) * HALF])).astype(BF16)
    for e in range(EDGES):
        place = jnp.where(lane32 == row32 * STEPS + acc_column + (e - EDGES), 1.0, 0.0)
        place = jnp.where(acc_column + e >= EDGES, place, 0.0).astype(BF16)
        kept_edge = dot(place, inputs_raw, NT)
        for i in range(EDGES):
            kept_edge = kept_edge + jnp.where(acc_column + e == i, edges[i].astype(F32), 0.0)
        edge_v[e] = kept_edge.astype(BF16)

    def cross(k):
        return [
            pltpu.make_async_remote_copy(
                src_ref=source, dst_ref=target.at[group], send_sem=ss_x.at[slot, k],
                recv_sem=rs_x.at[slot, k], device_id=across(k), device_id_type=MESH)
            for slot, (source, target) in enumerate(((kept_v, kept_all), (edge_v, edge_all)))
        ]

    crossing = [copy for k in range(1, GROUPS) for copy in cross(k)]
    for copy in crossing:
        copy.start()
    kept_all[group] = kept_v[...]
    edge_all[group] = edge_v[...]

    def scaled_norm(rows, gain):
        factor = lax.rsqrt(jnp.mean(rows * rows, axis=1, keepdims=True) + EPSILON)
        return rows * factor * gain

    for c in range(CHUNKS):
        for axis in range(2):
            sum1.turn(c, axis)
    for load in loads[3:]:
        load.wait()
    for c in range(CHUNKS):
        left = sum1.end(c, 0)
        right = sum1.end(c, 1)
        near = res_v[c].astype(F32)
        before = jnp.where(chip % 2 == 0, near[0:ROWS], near[ROWS:])
        square = left[0:ROWS, LANES:LANES + 1]
        attn = unfold(left[:, 0:LANES], right) * lax.rsqrt(square / WIDTH + EPSILON)
        first = (before + attn).astype(BF16).astype(F32)
        first_v[c] = first
        spread1.begin(c, scaled_norm(first, gain_mlp[...]))
    for c in range(CHUNKS):
        spread1.turn(c)
    for c in range(CHUNKS):
        for axis in range(2):
            sum1.drain(c, axis)
    for copy in shared[1:]:
        copy.wait()

    hidden_width = wd.shape[0] * wd.shape[1]
    for c in range(CHUNKS):
        both_parts = dot(wgu[...].reshape(2 * hidden_width, WIDTH), spread1.end(c), NT)
        gate = both_parts[0:hidden_width]
        hidden = (gate * jax.nn.sigmoid(gate) * both_parts[hidden_width:]).astype(BF16)
        for axis in range(2):
            low_at = slice(axis * LANES, (axis + 1) * LANES)
            high_at = slice(FOLD + axis * LANES, FOLD + (axis + 1) * LANES)
            put(folded(
                dot(hidden, wd[:, :, low_at].reshape(hidden_width, LANES), TN),
                dot(hidden, wd[:, :, high_at].reshape(hidden_width, LANES), TN),
            ), sum2.sends[axis], c, axis)
            sum2.begin(c, axis)
    for c in range(CHUNKS):
        spread1.drain(c)

    for copy in crossing:
        copy.wait()
    home_row = home[...]
    source_lane = iota((1, GROUPS * REQUESTS), 1)
    for i in range(REQUESTS):
        found = jnp.max(jnp.where(home_row == group * REQUESTS + i, source_lane, 0))
        kept_out[i] = kept_all[found // REQUESTS, found % REQUESTS]
    target_row = iota((REQUESTS, GROUPS * REQUESTS), 0) + group * REQUESTS
    chosen = jnp.where(home_row == target_row, 1.0, 0.0).astype(BF16)
    for e in range(EDGES):
        pool = edge_all[:, e].reshape(GROUPS * REQUESTS, HALF)
        edge_out[e] = dot(chosen, pool).astype(BF16)

    for c in range(CHUNKS):
        for axis in range(2):
            sum2.turn(c, axis)
    for c in range(CHUNKS):
        down = unfold(sum2.end(c, 0), sum2.end(c, 1))
        second = (first_v[c] + down).astype(BF16).astype(F32)
        spread2.begin(c, scaled_norm(second, gain_next[...]))
    for c in range(CHUNKS):
        spread2.turn(c)
    for c in range(CHUNKS):
        for axis in range(2):
            sum2.drain(c, axis)

    swaps = []
    for c in range(CHUNKS):
        normed = spread2.end(c)
        theirs_next = dot(wn[1 - core].reshape(3 * HALF, WIDTH), normed, NT)
        next_send[c] = theirs_next.astype(BF16).reshape(3, HALF, PART)
        swaps.append(to_sibling(next_send.at[c], next_recv.at[c], 7 + c))
        swaps[c].start()
        own_next = dot(wn[core].reshape(3 * HALF, WIDTH), normed, NT)
        here = pl.ds(pl.multiple_of(core * MINE + c * PART, PART), PART)
        next_out[:, :, here] = own_next.astype(BF16).reshape(3, HALF, PART)
    for c in range(CHUNKS):
        spread2.drain(c)
        swaps[c].wait()
        there = pl.ds(pl.multiple_of((1 - core) * MINE + c * PART, PART), PART)
        next_out[:, :, there] = next_recv[c]


def sum_buffers(width_a):
    grids = [(SIDE, SIDE), (SIDE, SIDE), (SIDE,), (SIDE,)]
    return [
        pltpu.VMEM((CHUNKS, *grid, 2 * ROWS, width), BF16) for grid in grids for width in (width_a, LANES)
    ]


def gather_buffers():
    return [pltpu.VMEM((CHUNKS, SIDE, SIDE, 2 * ROWS, LANES), BF16)] * 2


def per_device(
    residual_in, mixer_in, forget_floor, conv_weight, conv_edges, state_in, accepted, home_slot,
    gain_mixer, w_out, gain_mlp, w_gate, w_up, w_down, gain_next, w_next,
):
    hidden_width = w_gate.shape[1]
    anywhere = pl.BlockSpec(memory_space=pl.ANY)
    vmem = pl.BlockSpec(memory_space=pltpu.VMEM)
    dma = pltpu.SemaphoreType.DMA
    next_flat, kept, kept_edges = pl.pallas_call(
        kernel,
        name="draft_check",
        out_shape=(
            jax.ShapeDtypeStruct((3, HALF, TOKENS), BF16),
            jax.ShapeDtypeStruct((REQUESTS, HALF, KEYS), BF16),
            jax.ShapeDtypeStruct((EDGES, REQUESTS, HALF), BF16),
        ),
        in_specs=[
            anywhere, anywhere, vmem, vmem, vmem, anywhere, vmem, vmem, vmem,
            anywhere, vmem, anywhere, anywhere, anywhere, vmem, anywhere,
        ],
        out_specs=(vmem, vmem, vmem),
        scratch_shapes=[
            pltpu.VMEM((3, HALF, TOKENS), BF16),
            pltpu.VMEM((2, 2, HALF, TOKENS), BF16),
            pltpu.VMEM((REQUESTS, HALF, KEYS), F32),
            pltpu.VMEM((CHUNKS, 2 * ROWS, WIDTH), BF16),
            pltpu.VMEM((2, HALF, WIDTH), BF16),
            pltpu.VMEM((2, 2, hidden_width, WIDTH), BF16),
            pltpu.VMEM((2, hidden_width, WIDTH), BF16),
            pltpu.VMEM((2, 3, HALF, WIDTH), BF16),
            pltpu.VMEM((KEYS, TOKENS), BF16),
            pltpu.VMEM((KEYS, TOKENS), BF16),
            pltpu.VMEM((KEYS, TOKENS), F32),
            pltpu.VMEM((HALF, TOKENS), BF16),
            pltpu.VMEM((REQUESTS, KEYS), F32),
            pltpu.VMEM((HALF + STEPS, TOKENS), BF16),
            pltpu.VMEM((HALF + STEPS, MINE), BF16),
            pltpu.VMEM((HALF + STEPS, MINE), BF16),
            *sum_buffers(LANES + EXTRA), *gather_buffers(),
            pltpu.VMEM((CHUNKS, ROWS, WIDTH), F32),
            *sum_buffers(LANES), *gather_buffers(),
            pltpu.VMEM((CHUNKS, 3, HALF, PART), BF16),
            pltpu.VMEM((CHUNKS, 3, HALF, PART), BF16),
            pltpu.VMEM((REQUESTS, HALF, KEYS), BF16),
            pltpu.VMEM((EDGES, REQUESTS, HALF), BF16),
            pltpu.VMEM((GROUPS, REQUESTS, HALF, KEYS), BF16),
            pltpu.VMEM((GROUPS, EDGES, REQUESTS, HALF), BF16),
            dma((8 + CHUNKS,)), dma((7 + CHUNKS,)), dma((7 + CHUNKS,)),
            *[dma((CHUNKS, 2, 2, SIDE))] * 8,
            dma((2, GROUPS)), dma((2, GROUPS)),
        ],
        compiler_params=pltpu.CompilerParams(
            collective_id=0, has_side_effects=True, vmem_limit_bytes=56 * 2**20),
    )(
        residual_in,
        mixer_in.transpose(1, 2, 0),
        forget_floor.reshape(-1, KEYS),
        conv_weight,
        conv_edges.transpose(1, 0, 2),
        state_in,
        accepted.reshape(1, -1),
        home_slot.reshape(1, -1),
        gain_mixer.reshape(1, -1),
        w_out,
        gain_mlp.reshape(1, -1),
        w_gate.T,
        w_up.T,
        w_down,
        gain_next.reshape(1, -1),
        w_next.transpose(1, 2, 0),
    )
    return (
        next_flat.transpose(2, 0, 1),
        kept.astype(F32),
        kept_edges.transpose(1, 0, 2),
    )


def solution(mesh):
    in_specs = (
        P("grp", None),
        P("grp", None, "req"),
        P(),
        P(None, "req"),
        P("grp", None, "req"),
        P("grp", "req", None),
        P("grp"),
        P(),
        P("req"),
        P("req", None),
        P(),
        P(None, "req"),
        P(None, "req"),
        P("req", None),
        P(),
        P(None, None, "req"),
    )
    out_specs = (P("grp", None, "req"), P("grp", "req", None), P("grp", None, "req"))
    return jax.shard_map(
        per_device, mesh=mesh, in_specs=in_specs, out_specs=out_specs, check_vma=False
    )
```

```python
import jax
import jax.numpy as jnp
from jax import lax
from jax.experimental import pallas as pl
from jax.experimental.pallas import tpu as pltpu
from jax.sharding import PartitionSpec as P

EPSILON = 1e-06
MESH = pl.DeviceIdType.MESH
F32 = jnp.float32
BF16 = jnp.bfloat16

SIDE = 4
CHIPS = SIDE * SIDE
GROUPS = 4
STEPS = 16
TAPS = 4
EDGES = 3
WIDTH = 2048
HALF = 64
KEYS = 128
EXTRA = 128
REQUESTS = 32
TOKENS = REQUESTS * STEPS
MINE = TOKENS // 2
TILE = 128
TILE_REQ = TILE // STEPS
CHUNKS = 2
PART = MINE // CHUNKS
ROWS = PART // CHIPS
FOLD = WIDTH // 2
LANES = FOLD // 2

NT = (((1,), (1,)), ((), ()))
TN = (((0,), (0,)), ((), ()))


def dot(left, right, dims=(((1,), (0,)), ((), ()))):
    return lax.dot_general(left, right, dims, preferred_element_type=F32)


def iota(shape, dim):
    return lax.broadcasted_iota(jnp.int32, shape, dim)


def to_column(row):
    size = row.shape[1]
    square = jnp.broadcast_to(row, (size, size))
    diagonal = iota((size, size), 0) == iota((size, size), 1)
    return jnp.sum(jnp.where(diagonal, square, jnp.zeros_like(square)), axis=1, keepdims=True)


def kernel(
    residual, mixer, floor_in, taps_in, edges_in, state, accepted_in, home_in, gain_mixer_in,
    w_out, gain_mlp_in, w_gate, w_up, w_down, gain_next_in, w_next,
    next_out, kept_home, edge_out,
    floor, taps, edges, accepted, home, gain_mixer, gain_mlp, gain_next, kept_out, mix_v, pair, state_v, res_v, wo, wgu, wd, wn,
    query_b, key_b, decay, values, picked, gained_own, gained_send, gained_recv,
    send1a, send1b, early1a, early1b, middle1a, middle1b, late1a, late1b, gather1a, gather1b, first_v,
    send2a, send2b, early2a, early2b, middle2a, middle2b, late2a, late2b, gather2a, gather2b,
    next_send, next_recv, kept_v, edge_v, kept_all, edge_all,
    load_sem, small_sem, pair_ss, pair_rs, ss1, rs1, ss2, rs2, ss_x, rs_x,
):
    member = lax.axis_index("req")
    group = lax.axis_index("grp")
    core = member % 2
    chip = member // 2
    at_y = chip // SIDE
    at_z = chip % SIDE
    sibling = {"req": chip * 2 + (1 - core), "grp": group}

    def along(axis, k):
        if axis == 0:
            chip_at = (at_y + k) % SIDE * SIDE + at_z
        else:
            chip_at = at_y * SIDE + (at_z + k) % SIDE
        return {"req": chip_at * 2 + core, "grp": group}

    places = (at_y, at_z)

    def across(k):
        return {"req": member, "grp": (group + k) % GROUPS}

    barrier = pltpu.get_barrier_semaphore()

    pl.semaphore_signal(barrier, inc=1, device_id=sibling, device_id_type=MESH)
    for axis in range(2):
        for k in range(1, SIDE):
            pl.semaphore_signal(barrier, inc=1, device_id=along(axis, k), device_id_type=MESH)
    for k in range(1, GROUPS):
        pl.semaphore_signal(barrier, inc=1, device_id=across(k), device_id_type=MESH)

    loads = [
        pltpu.make_async_copy(mixer, mix_v, load_sem.at[0]),
        pltpu.make_async_copy(state, state_v, load_sem.at[1]),
        pltpu.make_async_copy(w_out, wo.at[core], load_sem.at[2]),
        pltpu.make_async_copy(w_gate, wgu.at[0, core], load_sem.at[4]),
        pltpu.make_async_copy(w_up, wgu.at[1, core], load_sem.at[5]),
        pltpu.make_async_copy(w_down, wd.at[core], load_sem.at[6]),
        pltpu.make_async_copy(w_next, wn.at[core], load_sem.at[7]),
    ]
    for c in range(CHUNKS):
        near = core * MINE + c * PART + chip // 2 * (2 * ROWS)
        loads.append(pltpu.make_async_copy(
            residual.at[pl.ds(pl.multiple_of(near, 2 * ROWS), 2 * ROWS)], res_v.at[c], load_sem.at[8 + c]))
    smalls = [
        pltpu.make_async_copy(source, target, small_sem.at[i])
        for i, (source, target) in enumerate((
            (taps_in, taps), (edges_in, edges), (floor_in, floor), (gain_mixer_in, gain_mixer),
            (accepted_in, accepted), (home_in, home), (gain_mlp_in, gain_mlp), (gain_next_in, gain_next)))
    ]
    for load in loads[:1] + smalls + loads[1:]:
        load.start()

    def to_sibling(source, target, slot):
        return pltpu.make_async_remote_copy(
            src_ref=source, dst_ref=target, send_sem=pair_ss.at[slot], recv_sem=pair_rs.at[slot],
            device_id=sibling, device_id_type=MESH)

    pl.semaphore_wait(barrier, 1 + 2 * (SIDE - 1) + GROUPS - 1)
    halves = to_sibling(mixer.at[0:2], pair.at[:, core], 0)
    halves.start()
    shared = [
        to_sibling(w_out, wo.at[core], 1),
        to_sibling(w_gate, wgu.at[0, core], 2),
        to_sibling(w_up, wgu.at[1, core], 3),
        to_sibling(w_down, wd.at[core], 4),
        to_sibling(w_next, wn.at[core], 5),
    ]
    for copy in shared:
        copy.start()

    for load in smalls + loads[:1]:
        load.wait()
    lane = iota((1, TOKENS), 1)
    step_of = lane % STEPS
    inputs_raw = mix_v[2]
    inputs_f = inputs_raw.astype(F32)
    stacked = jnp.concatenate([edges[i] for i in range(EDGES)], axis=0)
    row96 = iota((EDGES * REQUESTS, TOKENS), 0)
    lane96 = iota((EDGES * REQUESTS, TOKENS), 1)
    conv = to_column(taps[TAPS - 1:TAPS, :]) * inputs_f
    for j in range(TAPS - 1):
        shift = TAPS - 1 - j
        early = row96 // REQUESTS - j
        place = (early >= 0) & (lane96 == (row96 % REQUESTS) * STEPS + early)
        from_edges = dot(stacked, jnp.where(place, 1.0, 0.0).astype(BF16), TN)
        moved = jnp.where(step_of >= shift, pltpu.roll(inputs_f, shift, axis=1), 0.0)
        conv = conv + to_column(taps[j:j + 1, :]) * (moved + from_edges)
    values[...] = conv.astype(BF16)

    pair[:, core] = mix_v[0:2]
    floor_row = floor[pl.ds(chip, 1), :]
    low = to_column(floor_row)
    halves.wait()
    for tile in range(TOKENS // TILE):
        at = slice(tile * TILE, (tile + 1) * TILE)
        step_t = iota((KEYS, TILE), 1) % STEPS
        q_pre = pair[0, :, :, at].reshape(KEYS, TILE).astype(F32)
        f_pre = pair[1, :, :, at].reshape(KEYS, TILE).astype(F32)
        query = q_pre * jax.nn.sigmoid(q_pre)
        forget = low + (1.0 - low) * jax.nn.sigmoid(f_pre)
        keyed = 1.0 - forget
        run = forget
        for shift in (1, 2, 4, 8):
            run = jnp.where(step_t >= shift, run * pltpu.roll(run, shift, axis=1), run)
        decay[:, at] = run
        query_b[:, at] = (query * run).astype(BF16)
        key_b[:, at] = (keyed / run).astype(BF16)

    loads[1].wait()
    gain_column = to_column(gain_mixer[...])
    squares = []
    for tile in range(TOKENS // TILE):
        at = slice(tile * TILE, (tile + 1) * TILE)
        q_t = query_b[:, at]
        begin = state_v[tile * TILE_REQ:(tile + 1) * TILE_REQ].astype(BF16).reshape(TILE_REQ * HALF, KEYS)
        through = dot(begin, q_t).reshape(TILE_REQ, HALF, TILE)
        ours = iota((TILE_REQ, HALF, TILE), 0) == iota((TILE_REQ, HALF, TILE), 2) // STEPS
        total = jnp.sum(jnp.where(ours, through, 0.0), axis=0)
        scores = dot(key_b[:, at], q_t, TN)
        source = iota((TILE, TILE), 0)
        sink = iota((TILE, TILE), 1)
        causal = (source // STEPS == sink // STEPS) & (source <= sink)
        scores = jnp.where(causal, scores, 0.0).astype(BF16)
        total = (total + dot(values[:, at], scores)) * KEYS ** (-0.5)
        gained_own[0:HALF, at] = (total * gain_column).astype(BF16)
        square = jnp.sum(total * total, axis=0, keepdims=True)
        gained_own[HALF:HALF + STEPS, at] = jnp.broadcast_to(square, (STEPS, TILE)).astype(BF16)

    own_lanes = pl.ds(pl.multiple_of(core * MINE, MINE), MINE)
    other_lanes = pl.ds(pl.multiple_of((1 - core) * MINE, MINE), MINE)
    gained_send[...] = gained_own[:, other_lanes]
    swap = to_sibling(gained_send, gained_recv, 6)
    swap.start()
    mine = gained_own[:, own_lanes]
    swap.wait()
    theirs = gained_recv[...]
    lower = jnp.where(core == 0, mine[0:HALF], theirs[0:HALF])
    upper = jnp.where(core == 0, theirs[0:HALF], mine[0:HALF])
    both = jnp.concatenate([lower, upper], axis=0)
    loads[2].wait()
    shared[0].wait()
    squares2 = jnp.concatenate([mine[HALF:], theirs[HALF:]], axis=0)
    pick_one = jnp.where(iota((2 * STEPS, EXTRA), 0) % STEPS == 0, 1.0, 0.0).astype(BF16)

    def folded(low_part, high_part):
        width = low_part.shape[1]
        return jnp.concatenate(
            [low_part.reshape(CHIPS, ROWS, width), high_part.reshape(CHIPS, ROWS, width)], axis=1
        ).astype(BF16)

    def put(blocks, ref, c, axis):
        width = blocks.shape[2]
        blocks = blocks.reshape(SIDE, SIDE, 2 * ROWS, width)
        if axis == 0:
            ref[c, :, :, :, 0:width] = blocks
        else:
            for y in range(SIDE):
                ref[c, :, y, :, 0:width] = blocks[y]

    def link(source, target, ssem, rsem, c, axis, stage, k, towards):
        return pltpu.make_async_remote_copy(
            src_ref=source, dst_ref=target, send_sem=ssem.at[c, axis, stage, k - 1],
            recv_sem=rsem.at[c, axis, stage, k - 1], device_id=along(towards, k), device_id_type=MESH)

    class Sum:
        def __init__(self, sends, early, middle, late, sems):
            self.sends, self.early, self.middle, self.late, self.sems = sends, early, middle, late, sems

        def first(self, c, axis):
            return [
                link(self.sends[axis].at[c, (places[axis] + k) % SIDE], self.early[axis].at[c, k],
                     *self.sems, c, axis, 0, k, axis)
                for k in range(1, SIDE)
            ]

        def second(self, c, axis):
            other = 1 - axis
            return [
                link(self.middle[axis].at[c, (places[other] + k) % SIDE], self.late[axis].at[c, k],
                     *self.sems, c, axis, 1, k, other)
                for k in range(1, SIDE)
            ]

        def begin(self, c, axis):
            for copy in self.first(c, axis):
                copy.start()

        def turn(self, c, axis):
            for copy in self.first(c, axis):
                copy.wait_recv()
            sums = self.sends[axis][c, places[axis]].astype(F32)
            for k in range(1, SIDE):
                sums = sums + self.early[axis][c, k].astype(F32)
            self.middle[axis][c] = sums.astype(BF16)
            for copy in self.second(c, axis):
                copy.start()

        def end(self, c, axis):
            for copy in self.second(c, axis):
                copy.wait_recv()
            sums = self.middle[axis][c, places[1 - axis]].astype(F32)
            for k in range(1, SIDE):
                sums = sums + self.late[axis][c, k].astype(F32)
            return sums

        def drain(self, c, axis):
            for copy in self.first(c, axis) + self.second(c, axis):
                copy.wait_send()

    class Gather:
        def __init__(self, refs, sems):
            self.refs, self.sems = refs, sems

        def first(self, c, axis):
            other = 1 - axis
            mine_at = self.refs[axis].at[c, places[axis], places[other]]
            return [link(mine_at, mine_at, *self.sems, c, axis, 0, k, other) for k in range(1, SIDE)]

        def second(self, c, axis):
            mine_at = self.refs[axis].at[c, places[axis]]
            return [link(mine_at, mine_at, *self.sems, c, axis, 1, k, axis) for k in range(1, SIDE)]

        def begin(self, c, rows):
            block = jnp.concatenate([rows[:, 0:FOLD], rows[:, FOLD:]], axis=0).astype(BF16)
            for axis in range(2):
                self.refs[axis][c, places[axis], places[1 - axis]] = block[:, axis * LANES:(axis + 1) * LANES]
                for copy in self.first(c, axis):
                    copy.start()

        def turn(self, c):
            for axis in range(2):
                for copy in self.first(c, axis):
                    copy.wait_recv()
                for copy in self.second(c, axis):
                    copy.start()

        def end(self, c):
            for axis in range(2):
                for copy in self.second(c, axis):
                    copy.wait_recv()
            pieces = [[], []]
            for axis in range(2):
                if axis == 0:
                    blocks = self.refs[axis][c].astype(F32)
                else:
                    blocks = jnp.stack([self.refs[axis][c, :, y] for y in range(SIDE)], axis=0).astype(F32)
                blocks = blocks.reshape(CHIPS, 2 * ROWS, LANES)
                pieces[0].append(blocks[:, 0:ROWS].reshape(PART, LANES))
                pieces[1].append(blocks[:, ROWS:].reshape(PART, LANES))
            return jnp.concatenate(pieces[0] + pieces[1], axis=1).astype(BF16)

        def drain(self, c):
            for axis in range(2):
                for copy in self.first(c, axis) + self.second(c, axis):
                    copy.wait_send()

    def unfold(left, right):
        return jnp.concatenate([left[0:ROWS], right[0:ROWS], left[ROWS:], right[ROWS:]], axis=1)

    sum1 = Sum((send1a, send1b), (early1a, early1b), (middle1a, middle1b), (late1a, late1b), (ss1, rs1))
    spread1 = Gather((gather1a, gather1b), (ss2, rs2))
    sum2 = Sum((send2a, send2b), (early2a, early2b), (middle2a, middle2b), (late2a, late2b), (ss1, rs1))
    spread2 = Gather((gather2a, gather2b), (ss2, rs2))

    for c in range(CHUNKS):
        part = slice(c * PART, (c + 1) * PART)
        square = dot(squares2[:, part], pick_one, TN)
        square = folded(square, square).reshape(SIDE, SIDE, 2 * ROWS, EXTRA)
        send1a[c, :, :, :, LANES:] = square
        channels = both[:, part]
        for axis in range(2):
            low_at = slice(axis * LANES, (axis + 1) * LANES)
            high_at = slice(FOLD + axis * LANES, FOLD + (axis + 1) * LANES)
            put(folded(
                dot(channels, wo[:, :, low_at].reshape(2 * HALF, LANES), TN),
                dot(channels, wo[:, :, high_at].reshape(2 * HALF, LANES), TN),
            ), sum1.sends[axis], c, axis)
            sum1.begin(c, axis)

    acc_column = to_column(accepted[...])
    row32 = iota((REQUESTS, TOKENS), 0)
    lane32 = iota((REQUESTS, TOKENS), 1)
    acc_lanes = jnp.sum(jnp.where(lane32 // STEPS == row32, acc_column, 0), axis=0, keepdims=True)
    last = jnp.where(lane32 == row32 * STEPS + acc_column - 1, 1.0, 0.0)
    last = jnp.where(acc_column > 0, last, 0.0).astype(BF16)
    run_all = decay[...]
    run_high = run_all.astype(BF16)
    run_low = (run_all - run_high.astype(F32)).astype(BF16)
    run_picked = dot(last, run_high, NT) + dot(last, run_low, NT)
    picked[...] = jnp.where(acc_column == 0, 1.0, run_picked)
    live = step_of < acc_lanes
    for tile in range(TOKENS // TILE):
        at = slice(tile * TILE, (tile + 1) * TILE)
        taken = jnp.where(live[:, at], values[:, at].astype(F32), 0.0)
        spread = jnp.broadcast_to(taken[None], (TILE_REQ, HALF, TILE))
        ours = iota((TILE_REQ, HALF, TILE), 0) == iota((TILE_REQ, HALF, TILE), 2) // STEPS
        spread = jnp.where(ours, spread, 0.0).astype(BF16).reshape(TILE_REQ * HALF, TILE)
        added = dot(spread, key_b[:, at], NT)
        for i in range(TILE_REQ):
            r = tile * TILE_REQ + i
            kept_v[r] = (picked[r:r + 1, :] * (state_v[r] + added[i * HALF:(i + 1) * HALF])).astype(BF16)
    for e in range(EDGES):
        place = jnp.where(lane32 == row32 * STEPS + acc_column + (e - EDGES), 1.0, 0.0)
        place = jnp.where(acc_column + e >= EDGES, place, 0.0).astype(BF16)
        kept_edge = dot(place, inputs_raw, NT)
        for i in range(EDGES):
            kept_edge = kept_edge + jnp.where(acc_column + e == i, edges[i].astype(F32), 0.0)
        edge_v[e] = kept_edge.astype(BF16)

    def cross(k):
        return [
            pltpu.make_async_remote_copy(
                src_ref=source, dst_ref=target.at[group], send_sem=ss_x.at[slot, k - 1],
                recv_sem=rs_x.at[slot, k - 1], device_id=across(k), device_id_type=MESH)
            for slot, (source, target) in enumerate(((kept_v, kept_all), (edge_v, edge_all)))
        ]

    crossing = [copy for k in range(1, GROUPS) for copy in cross(k)]
    for copy in crossing:
        copy.start()
    kept_all[group] = kept_v[...]
    edge_all[group] = edge_v[...]

    def scaled_norm(rows, gain):
        factor = lax.rsqrt(jnp.mean(rows * rows, axis=1, keepdims=True) + EPSILON)
        return rows * factor * gain

    for c in range(CHUNKS):
        for axis in range(2):
            sum1.turn(c, axis)
    for load in loads[3:]:
        load.wait()
    for c in range(CHUNKS):
        left = sum1.end(c, 0)
        right = sum1.end(c, 1)
        near = res_v[c].astype(F32)
        before = jnp.where(chip % 2 == 0, near[0:ROWS], near[ROWS:])
        square = left[0:ROWS, LANES:LANES + 1]
        attn = unfold(left[:, 0:LANES], right) * lax.rsqrt(square / WIDTH + EPSILON)
        first = (before + attn).astype(BF16).astype(F32)
        first_v[c] = first
        spread1.begin(c, scaled_norm(first, gain_mlp[...]))
    for c in range(CHUNKS):
        spread1.turn(c)
    for c in range(CHUNKS):
        for axis in range(2):
            sum1.drain(c, axis)
    for copy in shared[1:]:
        copy.wait()

    hidden_width = wd.shape[0] * wd.shape[1]
    for c in range(CHUNKS):
        both_parts = dot(wgu[...].reshape(2 * hidden_width, WIDTH), spread1.end(c), NT)
        gate = both_parts[0:hidden_width]
        hidden = (gate * jax.nn.sigmoid(gate) * both_parts[hidden_width:]).astype(BF16)
        for axis in range(2):
            low_at = slice(axis * LANES, (axis + 1) * LANES)
            high_at = slice(FOLD + axis * LANES, FOLD + (axis + 1) * LANES)
            put(folded(
                dot(hidden, wd[:, :, low_at].reshape(hidden_width, LANES), TN),
                dot(hidden, wd[:, :, high_at].reshape(hidden_width, LANES), TN),
            ), sum2.sends[axis], c, axis)
            sum2.begin(c, axis)
    for c in range(CHUNKS):
        spread1.drain(c)

    for c in range(CHUNKS):
        for axis in range(2):
            sum2.turn(c, axis)
    for c in range(CHUNKS):
        down = unfold(sum2.end(c, 0), sum2.end(c, 1))
        second = (first_v[c] + down).astype(BF16).astype(F32)
        spread2.begin(c, scaled_norm(second, gain_next[...]))
    for c in range(CHUNKS):
        spread2.turn(c)

    for copy in crossing:
        copy.wait()
    home_row = home[...]
    source_lane = iota((1, GROUPS * REQUESTS), 1)
    for i in range(REQUESTS):
        found = jnp.max(jnp.where(home_row == group * REQUESTS + i, source_lane, 0))
        kept_out[i] = kept_all[found // REQUESTS, found % REQUESTS].astype(F32)
    leaving = pltpu.make_async_copy(kept_out, kept_home, load_sem.at[8 + CHUNKS])
    leaving.start()
    target_row = iota((REQUESTS, GROUPS * REQUESTS), 0) + group * REQUESTS
    chosen = jnp.where(home_row == target_row, 1.0, 0.0).astype(BF16)
    for e in range(EDGES):
        pool = edge_all[:, e].reshape(GROUPS * REQUESTS, HALF)
        edge_out[e] = dot(chosen, pool).astype(BF16)

    for c in range(CHUNKS):
        for axis in range(2):
            sum2.drain(c, axis)

    swaps = []
    for c in range(CHUNKS):
        normed = spread2.end(c)
        theirs_next = dot(wn[1 - core].reshape(3 * HALF, WIDTH), normed, NT)
        next_send[c] = theirs_next.astype(BF16).reshape(3, HALF, PART)
        swaps.append(to_sibling(next_send.at[c], next_recv.at[c], 7 + c))
        swaps[c].start()
        own_next = dot(wn[core].reshape(3 * HALF, WIDTH), normed, NT)
        here = pl.ds(pl.multiple_of(core * MINE + c * PART, PART), PART)
        next_out[:, :, here] = own_next.astype(BF16).reshape(3, HALF, PART)
    for c in range(CHUNKS):
        spread2.drain(c)
        swaps[c].wait()
        there = pl.ds(pl.multiple_of((1 - core) * MINE + c * PART, PART), PART)
        next_out[:, :, there] = next_recv[c]
    leaving.wait()


def finish(next_in, kept_in, edge_in, next_out, kept_out, edge_out, sems):
    pairs = ((kept_in, kept_out), (next_in, next_out), (edge_in, edge_out))
    copies = [pltpu.make_async_copy(source, target, sems.at[i]) for i, (source, target) in enumerate(pairs)]
    for copy in copies:
        copy.start()
    for copy in copies:
        copy.wait()


def sum_buffers(width_a):
    grids = [(SIDE, SIDE), (SIDE, SIDE), (SIDE,), (SIDE,)]
    return [
        pltpu.VMEM((CHUNKS, *grid, 2 * ROWS, width), BF16) for grid in grids for width in (width_a, LANES)
    ]


def gather_buffers():
    return [pltpu.VMEM((CHUNKS, SIDE, SIDE, 2 * ROWS, LANES), BF16)] * 2


def per_device(
    residual_in, mixer_in, forget_floor, conv_weight, conv_edges, state_in, accepted, home_slot,
    gain_mixer, w_out, gain_mlp, w_gate, w_up, w_down, gain_next, w_next,
):
    hidden_width = w_gate.shape[1]
    anywhere = pl.BlockSpec(memory_space=pl.ANY)
    vmem = pl.BlockSpec(memory_space=pltpu.VMEM)
    dma = pltpu.SemaphoreType.DMA
    outputs = (
        jax.ShapeDtypeStruct((3, HALF, TOKENS), BF16),
        jax.ShapeDtypeStruct((REQUESTS, HALF, KEYS), F32),
        jax.ShapeDtypeStruct((EDGES, REQUESTS, HALF), BF16),
    )
    results = pl.pallas_call(
        kernel,
        name="draft_check",
        out_shape=outputs,
        in_specs=[anywhere] * 16,
        out_specs=(vmem, anywhere, vmem),
        scratch_shapes=[
            pltpu.VMEM((CHIPS, KEYS), F32),
            pltpu.VMEM((TAPS, HALF), F32),
            pltpu.VMEM((EDGES, REQUESTS, HALF), BF16),
            pltpu.VMEM((1, REQUESTS), jnp.int32),
            pltpu.VMEM((1, GROUPS * REQUESTS), jnp.int32),
            pltpu.VMEM((1, HALF), F32),
            pltpu.VMEM((1, WIDTH), F32),
            pltpu.VMEM((1, WIDTH), F32),
            pltpu.VMEM((REQUESTS, HALF, KEYS), F32),
            pltpu.VMEM((3, HALF, TOKENS), BF16),
            pltpu.VMEM((2, 2, HALF, TOKENS), BF16),
            pltpu.VMEM((REQUESTS, HALF, KEYS), F32),
            pltpu.VMEM((CHUNKS, 2 * ROWS, WIDTH), BF16),
            pltpu.VMEM((2, HALF, WIDTH), BF16),
            pltpu.VMEM((2, 2, hidden_width, WIDTH), BF16),
            pltpu.VMEM((2, hidden_width, WIDTH), BF16),
            pltpu.VMEM((2, 3, HALF, WIDTH), BF16),
            pltpu.VMEM((KEYS, TOKENS), BF16),
            pltpu.VMEM((KEYS, TOKENS), BF16),
            pltpu.VMEM((KEYS, TOKENS), F32),
            pltpu.VMEM((HALF, TOKENS), BF16),
            pltpu.VMEM((REQUESTS, KEYS), F32),
            pltpu.VMEM((HALF + STEPS, TOKENS), BF16),
            pltpu.VMEM((HALF + STEPS, MINE), BF16),
            pltpu.VMEM((HALF + STEPS, MINE), BF16),
            *sum_buffers(LANES + EXTRA), *gather_buffers(),
            pltpu.VMEM((CHUNKS, ROWS, WIDTH), F32),
            *sum_buffers(LANES), *gather_buffers(),
            pltpu.VMEM((CHUNKS, 3, HALF, PART), BF16),
            pltpu.VMEM((CHUNKS, 3, HALF, PART), BF16),
            pltpu.VMEM((REQUESTS, HALF, KEYS), BF16),
            pltpu.VMEM((EDGES, REQUESTS, HALF), BF16),
            pltpu.VMEM((GROUPS, REQUESTS, HALF, KEYS), BF16),
            pltpu.VMEM((GROUPS, EDGES, REQUESTS, HALF), BF16),
            dma((9 + CHUNKS,)), dma((8,)), dma((7 + CHUNKS,)), dma((7 + CHUNKS,)),
            *[dma((CHUNKS, 2, 2, SIDE - 1))] * 4,
            dma((2, GROUPS - 1)), dma((2, GROUPS - 1)),
        ],
        compiler_params=pltpu.CompilerParams(
            collective_id=0, has_side_effects=True, vmem_limit_bytes=56 * 2**20),
    )(
        residual_in,
        mixer_in.transpose(1, 2, 0),
        forget_floor.reshape(-1, KEYS),
        conv_weight,
        conv_edges.transpose(1, 0, 2),
        state_in,
        accepted.reshape(1, -1),
        home_slot.reshape(1, -1),
        gain_mixer.reshape(1, -1),
        w_out,
        gain_mlp.reshape(1, -1),
        w_gate.T,
        w_up.T,
        w_down,
        gain_next.reshape(1, -1),
        w_next.transpose(1, 2, 0),
    )
    next_flat, kept, kept_edges = pl.pallas_call(
        finish,
        name="finish",
        out_shape=outputs,
        in_specs=[anywhere] * 3,
        out_specs=(anywhere,) * 3,
        scratch_shapes=[dma((3,))],
        compiler_params=pltpu.CompilerParams(vmem_limit_bytes=56 * 2**20),
    )(*results)
    return next_flat.transpose(2, 0, 1), kept, kept_edges.transpose(1, 0, 2)


def solution(mesh):
    in_specs = (
        P("grp", None),
        P("grp", None, "req"),
        P(),
        P(None, "req"),
        P("grp", None, "req"),
        P("grp", "req", None),
        P("grp"),
        P(),
        P("req"),
        P("req", None),
        P(),
        P(None, "req"),
        P(None, "req"),
        P("req", None),
        P(),
        P(None, None, "req"),
    )
    out_specs = (P("grp", None, "req"), P("grp", "req", None), P("grp", None, "req"))
    return jax.shard_map(
        per_device, mesh=mesh, in_specs=in_specs, out_specs=out_specs, check_vma=False
    )
```

```python
import jax
import jax.numpy as jnp
from jax import lax
from jax.experimental import pallas as pl
from jax.experimental.pallas import tpu as pltpu
from jax.sharding import PartitionSpec as P

EPSILON = 1e-06
MESH = pl.DeviceIdType.MESH
F32 = jnp.float32
BF16 = jnp.bfloat16

SIDE = 4
CHIPS = SIDE * SIDE
GROUPS = 4
STEPS = 16
TAPS = 4
EDGES = 3
WIDTH = 2048
HALF = 64
KEYS = 128
EXTRA = 128
REQUESTS = 32
TOKENS = REQUESTS * STEPS
MINE = TOKENS // 2
TILE = 128
TILE_REQ = TILE // STEPS
CHUNKS = 2
PART = MINE // CHUNKS
ROWS = PART // CHIPS
FOLD = WIDTH // 2
LANES = FOLD // 2

NT = (((1,), (1,)), ((), ()))
TN = (((0,), (0,)), ((), ()))


def dot(left, right, dims=(((1,), (0,)), ((), ()))):
    return lax.dot_general(left, right, dims, preferred_element_type=F32)


def iota(shape, dim):
    return lax.broadcasted_iota(jnp.int32, shape, dim)


def to_column(row):
    size = row.shape[1]
    square = jnp.broadcast_to(row, (size, size))
    diagonal = iota((size, size), 0) == iota((size, size), 1)
    return jnp.sum(jnp.where(diagonal, square, jnp.zeros_like(square)), axis=1, keepdims=True)


def kernel(
    residual, mixer, floor_in, taps_in, edges_in, state, accepted_in, home_in, gain_mixer_in,
    w_out, gain_mlp_in, w_gate, w_up, w_down, gain_next_in, w_next,
    next_out, kept_home, edge_out,
    floor, taps, edges, accepted, home, gain_mixer, gain_mlp, gain_next, kept_out, mix_v, pair, state_v, res_v, wo, wgu, wd, wn,
    query_b, key_b, decay, values, picked, gained_own, gained_send, gained_recv,
    send1a, send1b, early1a, early1b, middle1a, middle1b, late1a, late1b, gather1a, gather1b, first_v,
    send2a, send2b, early2a, early2b, middle2a, middle2b, late2a, late2b, gather2a, gather2b,
    next_send, next_recv, kept_v, edge_v, kept_all, edge_all,
    load_sem, small_sem, pair_ss, pair_rs, ss1, rs1, ss2, rs2, ss_x, rs_x,
):
    member = lax.axis_index("req")
    group = lax.axis_index("grp")
    core = member % 2
    chip = member // 2
    at_y = chip // SIDE
    at_z = chip % SIDE
    sibling = {"req": chip * 2 + (1 - core), "grp": group}

    def along(axis, k):
        if axis == 0:
            chip_at = (at_y + k) % SIDE * SIDE + at_z
        else:
            chip_at = at_y * SIDE + (at_z + k) % SIDE
        return {"req": chip_at * 2 + core, "grp": group}

    places = (at_y, at_z)

    def across(k):
        return {"req": member, "grp": (group + k) % GROUPS}

    barrier = pltpu.get_barrier_semaphore()

    pl.semaphore_signal(barrier, inc=1, device_id=sibling, device_id_type=MESH)
    for axis in range(2):
        for k in range(1, SIDE):
            pl.semaphore_signal(barrier, inc=1, device_id=along(axis, k), device_id_type=MESH)
    for k in range(1, GROUPS):
        pl.semaphore_signal(barrier, inc=1, device_id=across(k), device_id_type=MESH)

    loads = [
        pltpu.make_async_copy(mixer, mix_v, load_sem.at[0]),
        pltpu.make_async_copy(state, state_v, load_sem.at[1]),
        pltpu.make_async_copy(w_out, wo.at[core], load_sem.at[2]),
        pltpu.make_async_copy(w_gate, wgu.at[0, core], load_sem.at[4]),
        pltpu.make_async_copy(w_up, wgu.at[1, core], load_sem.at[5]),
        pltpu.make_async_copy(w_down, wd.at[core], load_sem.at[6]),
        pltpu.make_async_copy(w_next, wn.at[core], load_sem.at[7]),
    ]
    for c in range(CHUNKS):
        near = core * MINE + c * PART + chip // 2 * (2 * ROWS)
        loads.append(pltpu.make_async_copy(
            residual.at[pl.ds(pl.multiple_of(near, 2 * ROWS), 2 * ROWS)], res_v.at[c], load_sem.at[8 + c]))
    smalls = [
        pltpu.make_async_copy(source, target, small_sem.at[i])
        for i, (source, target) in enumerate((
            (taps_in, taps), (edges_in, edges), (floor_in, floor), (gain_mixer_in, gain_mixer),
            (accepted_in, accepted), (home_in, home), (gain_mlp_in, gain_mlp), (gain_next_in, gain_next)))
    ]
    for load in loads[:1] + smalls + loads[1:]:
        load.start()

    def to_sibling(source, target, slot):
        return pltpu.make_async_remote_copy(
            src_ref=source, dst_ref=target, send_sem=pair_ss.at[slot], recv_sem=pair_rs.at[slot],
            device_id=sibling, device_id_type=MESH)

    pl.semaphore_wait(barrier, 1 + 2 * (SIDE - 1) + GROUPS - 1)
    halves = to_sibling(mixer.at[0:2], pair.at[:, core], 0)
    halves.start()
    shared = [
        to_sibling(w_out, wo.at[core], 1),
        to_sibling(w_gate, wgu.at[0, core], 2),
        to_sibling(w_up, wgu.at[1, core], 3),
        to_sibling(w_down, wd.at[core], 4),
        to_sibling(w_next, wn.at[core], 5),
    ]
    for copy in shared:
        copy.start()

    for load in smalls + loads[:1]:
        load.wait()
    lane = iota((1, TOKENS), 1)
    step_of = lane % STEPS
    inputs_raw = mix_v[2]
    inputs_f = inputs_raw.astype(F32)
    stacked = jnp.concatenate([edges[i] for i in range(EDGES)], axis=0)
    row96 = iota((EDGES * REQUESTS, TOKENS), 0)
    lane96 = iota((EDGES * REQUESTS, TOKENS), 1)
    conv = to_column(taps[TAPS - 1:TAPS, :]) * inputs_f
    for j in range(TAPS - 1):
        shift = TAPS - 1 - j
        early = row96 // REQUESTS - j
        place = (early >= 0) & (lane96 == (row96 % REQUESTS) * STEPS + early)
        from_edges = dot(stacked, jnp.where(place, 1.0, 0.0).astype(BF16), TN)
        moved = jnp.where(step_of >= shift, pltpu.roll(inputs_f, shift, axis=1), 0.0)
        conv = conv + to_column(taps[j:j + 1, :]) * (moved + from_edges)
    values[...] = conv.astype(BF16)

    pair[:, core] = mix_v[0:2]
    floor_row = floor[pl.ds(chip, 1), :]
    low = to_column(floor_row)
    halves.wait()
    for tile in range(TOKENS // TILE):
        at = slice(tile * TILE, (tile + 1) * TILE)
        step_t = iota((KEYS, TILE), 1) % STEPS
        q_pre = pair[0, :, :, at].reshape(KEYS, TILE).astype(F32)
        f_pre = pair[1, :, :, at].reshape(KEYS, TILE).astype(F32)
        query = q_pre * jax.nn.sigmoid(q_pre)
        forget = low + (1.0 - low) * jax.nn.sigmoid(f_pre)
        keyed = 1.0 - forget
        run = forget
        for shift in (1, 2, 4, 8):
            run = jnp.where(step_t >= shift, run * pltpu.roll(run, shift, axis=1), run)
        decay[:, at] = run
        query_b[:, at] = (query * run).astype(BF16)
        key_b[:, at] = (keyed / run).astype(BF16)

    loads[1].wait()
    gain_column = to_column(gain_mixer[...])
    squares = []
    for tile in range(TOKENS // TILE):
        at = slice(tile * TILE, (tile + 1) * TILE)
        q_t = query_b[:, at]
        begin = state_v[tile * TILE_REQ:(tile + 1) * TILE_REQ].astype(BF16).reshape(TILE_REQ * HALF, KEYS)
        through = dot(begin, q_t).reshape(TILE_REQ, HALF, TILE)
        ours = iota((TILE_REQ, HALF, TILE), 0) == iota((TILE_REQ, HALF, TILE), 2) // STEPS
        total = jnp.sum(jnp.where(ours, through, 0.0), axis=0)
        scores = dot(key_b[:, at], q_t, TN)
        source = iota((TILE, TILE), 0)
        sink = iota((TILE, TILE), 1)
        causal = (source // STEPS == sink // STEPS) & (source <= sink)
        scores = jnp.where(causal, scores, 0.0).astype(BF16)
        total = (total + dot(values[:, at], scores)) * KEYS ** (-0.5)
        gained_own[0:HALF, at] = (total * gain_column).astype(BF16)
        square = jnp.sum(total * total, axis=0, keepdims=True)
        gained_own[HALF:HALF + STEPS, at] = jnp.broadcast_to(square, (STEPS, TILE)).astype(BF16)

    own_lanes = pl.ds(pl.multiple_of(core * MINE, MINE), MINE)
    other_lanes = pl.ds(pl.multiple_of((1 - core) * MINE, MINE), MINE)
    gained_send[...] = gained_own[:, other_lanes]
    swap = to_sibling(gained_send, gained_recv, 6)
    swap.start()
    mine = gained_own[:, own_lanes]
    swap.wait()
    theirs = gained_recv[...]
    lower = jnp.where(core == 0, mine[0:HALF], theirs[0:HALF])
    upper = jnp.where(core == 0, theirs[0:HALF], mine[0:HALF])
    both = jnp.concatenate([lower, upper], axis=0)
    loads[2].wait()
    shared[0].wait()
    squares2 = jnp.concatenate([mine[HALF:], theirs[HALF:]], axis=0)
    pick_one = jnp.where(iota((2 * STEPS, EXTRA), 0) % STEPS == 0, 1.0, 0.0).astype(BF16)

    def folded(low_part, high_part):
        width = low_part.shape[1]
        return jnp.concatenate(
            [low_part.reshape(CHIPS, ROWS, width), high_part.reshape(CHIPS, ROWS, width)], axis=1
        ).astype(BF16)

    def put(blocks, ref, c, axis):
        width = blocks.shape[2]
        blocks = blocks.reshape(SIDE, SIDE, 2 * ROWS, width)
        if axis == 0:
            ref[c, :, :, :, 0:width] = blocks
        else:
            for y in range(SIDE):
                ref[c, :, y, :, 0:width] = blocks[y]

    def link(source, target, ssem, rsem, c, axis, stage, k, towards):
        return pltpu.make_async_remote_copy(
            src_ref=source, dst_ref=target, send_sem=ssem.at[c, axis, stage, k - 1],
            recv_sem=rsem.at[c, axis, stage, k - 1], device_id=along(towards, k), device_id_type=MESH)

    class Sum:
        def __init__(self, sends, early, middle, late, sems):
            self.sends, self.early, self.middle, self.late, self.sems = sends, early, middle, late, sems

        def first(self, c, axis):
            return [
                link(self.sends[axis].at[c, (places[axis] + k) % SIDE], self.early[axis].at[c, k],
                     *self.sems, c, axis, 0, k, axis)
                for k in range(1, SIDE)
            ]

        def second(self, c, axis):
            other = 1 - axis
            return [
                link(self.middle[axis].at[c, (places[other] + k) % SIDE], self.late[axis].at[c, k],
                     *self.sems, c, axis, 1, k, other)
                for k in range(1, SIDE)
            ]

        def begin(self, c, axis):
            for copy in self.first(c, axis):
                copy.start()

        def turn(self, c, axis):
            for copy in self.first(c, axis):
                copy.wait_recv()
            sums = self.sends[axis][c, places[axis]].astype(F32)
            for k in range(1, SIDE):
                sums = sums + self.early[axis][c, k].astype(F32)
            self.middle[axis][c] = sums.astype(BF16)
            for copy in self.second(c, axis):
                copy.start()

        def end(self, c, axis):
            for copy in self.second(c, axis):
                copy.wait_recv()
            sums = self.middle[axis][c, places[1 - axis]].astype(F32)
            for k in range(1, SIDE):
                sums = sums + self.late[axis][c, k].astype(F32)
            return sums

        def drain(self, c, axis):
            for copy in self.first(c, axis) + self.second(c, axis):
                copy.wait_send()

    class Gather:
        def __init__(self, refs, sems):
            self.refs, self.sems = refs, sems

        def first(self, c, axis):
            other = 1 - axis
            mine_at = self.refs[axis].at[c, places[axis], places[other]]
            return [link(mine_at, mine_at, *self.sems, c, axis, 0, k, other) for k in range(1, SIDE)]

        def second(self, c, axis):
            mine_at = self.refs[axis].at[c, places[axis]]
            return [link(mine_at, mine_at, *self.sems, c, axis, 1, k, axis) for k in range(1, SIDE)]

        def begin(self, c, rows):
            block = jnp.concatenate([rows[:, 0:FOLD], rows[:, FOLD:]], axis=0).astype(BF16)
            for axis in range(2):
                self.refs[axis][c, places[axis], places[1 - axis]] = block[:, axis * LANES:(axis + 1) * LANES]
                for copy in self.first(c, axis):
                    copy.start()

        def turn(self, c):
            for axis in range(2):
                for copy in self.first(c, axis):
                    copy.wait_recv()
                for copy in self.second(c, axis):
                    copy.start()

        def end(self, c):
            for axis in range(2):
                for copy in self.second(c, axis):
                    copy.wait_recv()
            pieces = [[], []]
            for axis in range(2):
                if axis == 0:
                    blocks = self.refs[axis][c].astype(F32)
                else:
                    blocks = jnp.stack([self.refs[axis][c, :, y] for y in range(SIDE)], axis=0).astype(F32)
                blocks = blocks.reshape(CHIPS, 2 * ROWS, LANES)
                pieces[0].append(blocks[:, 0:ROWS].reshape(PART, LANES))
                pieces[1].append(blocks[:, ROWS:].reshape(PART, LANES))
            return jnp.concatenate(pieces[0] + pieces[1], axis=1).astype(BF16)

        def drain(self, c):
            for axis in range(2):
                for copy in self.first(c, axis) + self.second(c, axis):
                    copy.wait_send()

    def unfold(left, right):
        return jnp.concatenate([left[0:ROWS], right[0:ROWS], left[ROWS:], right[ROWS:]], axis=1)

    sum1 = Sum((send1a, send1b), (early1a, early1b), (middle1a, middle1b), (late1a, late1b), (ss1, rs1))
    spread1 = Gather((gather1a, gather1b), (ss2, rs2))
    sum2 = Sum((send2a, send2b), (early2a, early2b), (middle2a, middle2b), (late2a, late2b), (ss1, rs1))
    spread2 = Gather((gather2a, gather2b), (ss2, rs2))

    for c in range(CHUNKS):
        part = slice(c * PART, (c + 1) * PART)
        square = dot(squares2[:, part], pick_one, TN)
        square = folded(square, square).reshape(SIDE, SIDE, 2 * ROWS, EXTRA)
        send1a[c, :, :, :, LANES:] = square
        channels = both[:, part]
        for axis in range(2):
            low_at = slice(axis * LANES, (axis + 1) * LANES)
            high_at = slice(FOLD + axis * LANES, FOLD + (axis + 1) * LANES)
            put(folded(
                dot(channels, wo[:, :, low_at].reshape(2 * HALF, LANES), TN),
                dot(channels, wo[:, :, high_at].reshape(2 * HALF, LANES), TN),
            ), sum1.sends[axis], c, axis)
            sum1.begin(c, axis)

    acc_column = to_column(accepted[...])
    row32 = iota((REQUESTS, TOKENS), 0)
    lane32 = iota((REQUESTS, TOKENS), 1)
    acc_lanes = jnp.sum(jnp.where(lane32 // STEPS == row32, acc_column, 0), axis=0, keepdims=True)
    last = jnp.where(lane32 == row32 * STEPS + acc_column - 1, 1.0, 0.0)
    last = jnp.where(acc_column > 0, last, 0.0).astype(BF16)
    run_all = decay[...]
    run_high = run_all.astype(BF16)
    run_low = (run_all - run_high.astype(F32)).astype(BF16)
    run_picked = dot(last, run_high, NT) + dot(last, run_low, NT)
    picked[...] = jnp.where(acc_column == 0, 1.0, run_picked)
    live = step_of < acc_lanes
    for tile in range(TOKENS // TILE):
        at = slice(tile * TILE, (tile + 1) * TILE)
        taken = jnp.where(live[:, at], values[:, at].astype(F32), 0.0)
        spread = jnp.broadcast_to(taken[None], (TILE_REQ, HALF, TILE))
        ours = iota((TILE_REQ, HALF, TILE), 0) == iota((TILE_REQ, HALF, TILE), 2) // STEPS
        spread = jnp.where(ours, spread, 0.0).astype(BF16).reshape(TILE_REQ * HALF, TILE)
        added = dot(spread, key_b[:, at], NT)
        for i in range(TILE_REQ):
            r = tile * TILE_REQ + i
            kept_v[r] = (picked[r:r + 1, :] * (state_v[r] + added[i * HALF:(i + 1) * HALF])).astype(BF16)
    for e in range(EDGES):
        place = jnp.where(lane32 == row32 * STEPS + acc_column + (e - EDGES), 1.0, 0.0)
        place = jnp.where(acc_column + e >= EDGES, place, 0.0).astype(BF16)
        kept_edge = dot(place, inputs_raw, NT)
        for i in range(EDGES):
            kept_edge = kept_edge + jnp.where(acc_column + e == i, edges[i].astype(F32), 0.0)
        edge_v[e] = kept_edge.astype(BF16)

    def cross(k):
        return [
            pltpu.make_async_remote_copy(
                src_ref=source, dst_ref=target.at[group], send_sem=ss_x.at[slot, k - 1],
                recv_sem=rs_x.at[slot, k - 1], device_id=across(k), device_id_type=MESH)
            for slot, (source, target) in enumerate(((kept_v, kept_all), (edge_v, edge_all)))
        ]

    crossing = [copy for k in range(1, GROUPS) for copy in cross(k)]
    for copy in crossing:
        copy.start()
    kept_all[group] = kept_v[...]
    edge_all[group] = edge_v[...]

    def scaled_norm(rows, gain):
        factor = lax.rsqrt(jnp.mean(rows * rows, axis=1, keepdims=True) + EPSILON)
        return rows * factor * gain

    for c in range(CHUNKS):
        for axis in range(2):
            sum1.turn(c, axis)
    for load in loads[3:]:
        load.wait()
    for c in range(CHUNKS):
        left = sum1.end(c, 0)
        right = sum1.end(c, 1)
        near = res_v[c].astype(F32)
        before = jnp.where(chip % 2 == 0, near[0:ROWS], near[ROWS:])
        square = left[0:ROWS, LANES:LANES + 1]
        attn = unfold(left[:, 0:LANES], right) * lax.rsqrt(square / WIDTH + EPSILON)
        first = (before + attn).astype(BF16).astype(F32)
        first_v[c] = first
        spread1.begin(c, scaled_norm(first, gain_mlp[...]))
    for c in range(CHUNKS):
        spread1.turn(c)
    for c in range(CHUNKS):
        for axis in range(2):
            sum1.drain(c, axis)
    for copy in shared[1:]:
        copy.wait()

    hidden_width = wd.shape[0] * wd.shape[1]
    for c in range(CHUNKS):
        both_parts = dot(wgu[...].reshape(2 * hidden_width, WIDTH), spread1.end(c), NT)
        gate = both_parts[0:hidden_width]
        hidden = (gate * jax.nn.sigmoid(gate) * both_parts[hidden_width:]).astype(BF16)
        for axis in range(2):
            low_at = slice(axis * LANES, (axis + 1) * LANES)
            high_at = slice(FOLD + axis * LANES, FOLD + (axis + 1) * LANES)
            put(folded(
                dot(hidden, wd[:, :, low_at].reshape(hidden_width, LANES), TN),
                dot(hidden, wd[:, :, high_at].reshape(hidden_width, LANES), TN),
            ), sum2.sends[axis], c, axis)
            sum2.begin(c, axis)
    for c in range(CHUNKS):
        spread1.drain(c)

    for c in range(CHUNKS):
        for axis in range(2):
            sum2.turn(c, axis)
    for c in range(CHUNKS):
        down = unfold(sum2.end(c, 0), sum2.end(c, 1))
        second = (first_v[c] + down).astype(BF16).astype(F32)
        spread2.begin(c, scaled_norm(second, gain_next[...]))
    for c in range(CHUNKS):
        spread2.turn(c)

    for copy in crossing:
        copy.wait()
    home_row = home[...]
    source_lane = iota((1, GROUPS * REQUESTS), 1)
    for i in range(REQUESTS):
        found = jnp.max(jnp.where(home_row == group * REQUESTS + i, source_lane, 0))
        kept_out[i] = kept_all[found // REQUESTS, found % REQUESTS].astype(F32)
    leaving = pltpu.make_async_copy(kept_out, kept_home, load_sem.at[8 + CHUNKS])
    leaving.start()
    target_row = iota((REQUESTS, GROUPS * REQUESTS), 0) + group * REQUESTS
    chosen = jnp.where(home_row == target_row, 1.0, 0.0).astype(BF16)
    for e in range(EDGES):
        pool = edge_all[:, e].reshape(GROUPS * REQUESTS, HALF)
        edge_out[e] = dot(chosen, pool).astype(BF16)

    for c in range(CHUNKS):
        for axis in range(2):
            sum2.drain(c, axis)

    swaps = []
    for c in range(CHUNKS):
        normed = spread2.end(c)
        theirs_next = dot(wn[1 - core].reshape(3 * HALF, WIDTH), normed, NT)
        next_send[c] = theirs_next.astype(BF16).reshape(3, HALF, PART)
        swaps.append(to_sibling(next_send.at[c], next_recv.at[c], 7 + c))
        swaps[c].start()
        own_next = dot(wn[core].reshape(3 * HALF, WIDTH), normed, NT)
        here = pl.ds(pl.multiple_of(core * MINE + c * PART, PART), PART)
        next_out[:, :, here] = own_next.astype(BF16).reshape(3, HALF, PART)
    for c in range(CHUNKS):
        spread2.drain(c)
        swaps[c].wait()
        there = pl.ds(pl.multiple_of((1 - core) * MINE + c * PART, PART), PART)
        next_out[:, :, there] = next_recv[c]
    leaving.wait()


PIECES = 4
PIECE = REQUESTS // PIECES


def finish(next_in, kept_in, edge_in, next_out, kept_out, edge_out, next_v, kept_v, edge_v, in_sems, out_sems):
    parts = [slice(i * PIECE, (i + 1) * PIECE) for i in range(PIECES)]
    routes = [(kept_in.at[part], kept_v.at[part], kept_out.at[part]) for part in parts]
    routes += [(next_in, next_v, next_out), (edge_in, edge_v, edge_out)]
    arrive = [pltpu.make_async_copy(a, b, in_sems.at[i]) for i, (a, b, _) in enumerate(routes)]
    leave = [pltpu.make_async_copy(b, c, out_sems.at[i]) for i, (_, b, c) in enumerate(routes)]
    for copy in arrive:
        copy.start()
    for copy, further in zip(arrive, leave):
        copy.wait()
        further.start()
    for copy in leave:
        copy.wait()


def sum_buffers(width_a):
    grids = [(SIDE, SIDE), (SIDE, SIDE), (SIDE,), (SIDE,)]
    return [
        pltpu.VMEM((CHUNKS, *grid, 2 * ROWS, width), BF16) for grid in grids for width in (width_a, LANES)
    ]


def gather_buffers():
    return [pltpu.VMEM((CHUNKS, SIDE, SIDE, 2 * ROWS, LANES), BF16)] * 2


def per_device(
    residual_in, mixer_in, forget_floor, conv_weight, conv_edges, state_in, accepted, home_slot,
    gain_mixer, w_out, gain_mlp, w_gate, w_up, w_down, gain_next, w_next,
):
    hidden_width = w_gate.shape[1]
    anywhere = pl.BlockSpec(memory_space=pl.ANY)
    vmem = pl.BlockSpec(memory_space=pltpu.VMEM)
    dma = pltpu.SemaphoreType.DMA
    outputs = (
        jax.ShapeDtypeStruct((3, HALF, TOKENS), BF16),
        jax.ShapeDtypeStruct((REQUESTS, HALF, KEYS), F32),
        jax.ShapeDtypeStruct((EDGES, REQUESTS, HALF), BF16),
    )
    results = pl.pallas_call(
        kernel,
        name="draft_check",
        out_shape=outputs,
        in_specs=[anywhere] * 16,
        out_specs=(vmem, anywhere, vmem),
        scratch_shapes=[
            pltpu.VMEM((CHIPS, KEYS), F32),
            pltpu.VMEM((TAPS, HALF), F32),
            pltpu.VMEM((EDGES, REQUESTS, HALF), BF16),
            pltpu.VMEM((1, REQUESTS), jnp.int32),
            pltpu.VMEM((1, GROUPS * REQUESTS), jnp.int32),
            pltpu.VMEM((1, HALF), F32),
            pltpu.VMEM((1, WIDTH), F32),
            pltpu.VMEM((1, WIDTH), F32),
            pltpu.VMEM((REQUESTS, HALF, KEYS), F32),
            pltpu.VMEM((3, HALF, TOKENS), BF16),
            pltpu.VMEM((2, 2, HALF, TOKENS), BF16),
            pltpu.VMEM((REQUESTS, HALF, KEYS), F32),
            pltpu.VMEM((CHUNKS, 2 * ROWS, WIDTH), BF16),
            pltpu.VMEM((2, HALF, WIDTH), BF16),
            pltpu.VMEM((2, 2, hidden_width, WIDTH), BF16),
            pltpu.VMEM((2, hidden_width, WIDTH), BF16),
            pltpu.VMEM((2, 3, HALF, WIDTH), BF16),
            pltpu.VMEM((KEYS, TOKENS), BF16),
            pltpu.VMEM((KEYS, TOKENS), BF16),
            pltpu.VMEM((KEYS, TOKENS), F32),
            pltpu.VMEM((HALF, TOKENS), BF16),
            pltpu.VMEM((REQUESTS, KEYS), F32),
            pltpu.VMEM((HALF + STEPS, TOKENS), BF16),
            pltpu.VMEM((HALF + STEPS, MINE), BF16),
            pltpu.VMEM((HALF + STEPS, MINE), BF16),
            *sum_buffers(LANES + EXTRA), *gather_buffers(),
            pltpu.VMEM((CHUNKS, ROWS, WIDTH), F32),
            *sum_buffers(LANES), *gather_buffers(),
            pltpu.VMEM((CHUNKS, 3, HALF, PART), BF16),
            pltpu.VMEM((CHUNKS, 3, HALF, PART), BF16),
            pltpu.VMEM((REQUESTS, HALF, KEYS), BF16),
            pltpu.VMEM((EDGES, REQUESTS, HALF), BF16),
            pltpu.VMEM((GROUPS, REQUESTS, HALF, KEYS), BF16),
            pltpu.VMEM((GROUPS, EDGES, REQUESTS, HALF), BF16),
            dma((9 + CHUNKS,)), dma((8,)), dma((7 + CHUNKS,)), dma((7 + CHUNKS,)),
            *[dma((CHUNKS, 2, 2, SIDE - 1))] * 4,
            dma((2, GROUPS - 1)), dma((2, GROUPS - 1)),
        ],
        compiler_params=pltpu.CompilerParams(
            collective_id=0, has_side_effects=True, vmem_limit_bytes=56 * 2**20),
    )(
        residual_in,
        mixer_in.transpose(1, 2, 0),
        forget_floor.reshape(-1, KEYS),
        conv_weight,
        conv_edges.transpose(1, 0, 2),
        state_in,
        accepted.reshape(1, -1),
        home_slot.reshape(1, -1),
        gain_mixer.reshape(1, -1),
        w_out,
        gain_mlp.reshape(1, -1),
        w_gate.T,
        w_up.T,
        w_down,
        gain_next.reshape(1, -1),
        w_next.transpose(1, 2, 0),
    )
    next_flat, kept, kept_edges = pl.pallas_call(
        finish,
        name="finish",
        out_shape=outputs,
        in_specs=[anywhere] * 3,
        out_specs=(anywhere,) * 3,
        scratch_shapes=[
            *[pltpu.VMEM(output.shape, output.dtype) for output in outputs],
            dma((PIECES + 2,)), dma((PIECES + 2,)),
        ],
        compiler_params=pltpu.CompilerParams(vmem_limit_bytes=56 * 2**20),
    )(*results)
    return next_flat.transpose(2, 0, 1), kept, kept_edges.transpose(1, 0, 2)


def solution(mesh):
    in_specs = (
        P("grp", None),
        P("grp", None, "req"),
        P(),
        P(None, "req"),
        P("grp", None, "req"),
        P("grp", "req", None),
        P("grp"),
        P(),
        P("req"),
        P("req", None),
        P(),
        P(None, "req"),
        P(None, "req"),
        P("req", None),
        P(),
        P(None, None, "req"),
    )
    out_specs = (P("grp", None, "req"), P("grp", "req", None), P("grp", None, "req"))
    return jax.shard_map(
        per_device, mesh=mesh, in_specs=in_specs, out_specs=out_specs, check_vma=False
    )
```

```python
import jax
import jax.numpy as jnp
from jax import lax
from jax.experimental import pallas as pl
from jax.experimental.pallas import tpu as pltpu
from jax.sharding import PartitionSpec as P

EPSILON = 1e-06
MESH = pl.DeviceIdType.MESH
F32 = jnp.float32
BF16 = jnp.bfloat16

SIDE = 4
CHIPS = SIDE * SIDE
GROUPS = 4
STEPS = 16
TAPS = 4
EDGES = 3
WIDTH = 2048
HALF = 64
KEYS = 128
EXTRA = 128
REQUESTS = 32
TOKENS = REQUESTS * STEPS
MINE = TOKENS // 2
TILE = 128
TILE_REQ = TILE // STEPS
CHUNKS = 2
PART = MINE // CHUNKS
ROWS = PART // CHIPS
FOLD = WIDTH // 2
LANES = FOLD // 2

NT = (((1,), (1,)), ((), ()))
TN = (((0,), (0,)), ((), ()))


def dot(left, right, dims=(((1,), (0,)), ((), ()))):
    return lax.dot_general(left, right, dims, preferred_element_type=F32)


def iota(shape, dim):
    return lax.broadcasted_iota(jnp.int32, shape, dim)


def to_column(row):
    size = row.shape[1]
    square = jnp.broadcast_to(row, (size, size))
    diagonal = iota((size, size), 0) == iota((size, size), 1)
    return jnp.sum(jnp.where(diagonal, square, jnp.zeros_like(square)), axis=1, keepdims=True)


def kernel(
    residual, mixer, floor_in, taps_in, edges_in, state, accepted_in, home_in, gain_mixer_in,
    w_out, gain_mlp_in, w_gate, w_up, w_down, gain_next_in, w_next,
    next_out, kept_home, edge_out,
    floor, taps, edges, accepted, home, gain_mixer, gain_mlp, gain_next, kept_out, mix_v, pair, state_v, res_v, wo, wgu, wd, wn,
    query_b, key_b, decay, values, picked, gained_own, gained_send, gained_recv,
    send1a, send1b, early1a, early1b, middle1a, middle1b, late1a, late1b, gather1a, gather1b, first_v,
    send2a, send2b, early2a, early2b, middle2a, middle2b, late2a, late2b, gather2a, gather2b,
    next_send, next_recv, kept_v, edge_v, kept_all, edge_all,
    load_sem, small_sem, pair_ss, pair_rs, ss1, rs1, ss2, rs2, ss_x, rs_x,
):
    member = lax.axis_index("req")
    group = lax.axis_index("grp")
    core = member % 2
    chip = member // 2
    at_y = chip // SIDE
    at_z = chip % SIDE
    sibling = {"req": chip * 2 + (1 - core), "grp": group}

    def along(axis, k):
        if axis == 0:
            chip_at = (at_y + k) % SIDE * SIDE + at_z
        else:
            chip_at = at_y * SIDE + (at_z + k) % SIDE
        return {"req": chip_at * 2 + core, "grp": group}

    def across(k):
        return {"req": member, "grp": (group + k) % GROUPS}

    barrier = pltpu.get_barrier_semaphore()

    pl.semaphore_signal(barrier, inc=1, device_id=sibling, device_id_type=MESH)
    for axis in range(2):
        for k in range(1, SIDE):
            pl.semaphore_signal(barrier, inc=1, device_id=along(axis, k), device_id_type=MESH)
    for k in range(1, GROUPS):
        pl.semaphore_signal(barrier, inc=1, device_id=across(k), device_id_type=MESH)

    loads = [
        pltpu.make_async_copy(mixer, mix_v, load_sem.at[0]),
        pltpu.make_async_copy(state, state_v, load_sem.at[1]),
        pltpu.make_async_copy(w_out, wo.at[core], load_sem.at[2]),
        pltpu.make_async_copy(w_gate, wgu.at[0, core], load_sem.at[4]),
        pltpu.make_async_copy(w_up, wgu.at[1, core], load_sem.at[5]),
        pltpu.make_async_copy(w_down, wd.at[core], load_sem.at[6]),
        pltpu.make_async_copy(w_next, wn.at[core], load_sem.at[7]),
    ]
    for c in range(CHUNKS):
        near = core * MINE + c * PART + chip // 2 * (2 * ROWS)
        loads.append(pltpu.make_async_copy(
            residual.at[pl.ds(pl.multiple_of(near, 2 * ROWS), 2 * ROWS)], res_v.at[c], load_sem.at[8 + c]))
    smalls = [
        pltpu.make_async_copy(source, target, small_sem.at[i])
        for i, (source, target) in enumerate((
            (taps_in, taps), (edges_in, edges), (floor_in, floor), (gain_mixer_in, gain_mixer),
            (accepted_in, accepted), (home_in, home), (gain_mlp_in, gain_mlp), (gain_next_in, gain_next)))
    ]
    for load in loads[:1] + smalls + loads[1:]:
        load.start()

    def to_sibling(source, target, slot):
        return pltpu.make_async_remote_copy(
            src_ref=source, dst_ref=target, send_sem=pair_ss.at[slot], recv_sem=pair_rs.at[slot],
            device_id=sibling, device_id_type=MESH)

    pl.semaphore_wait(barrier, 1 + 2 * (SIDE - 1) + GROUPS - 1)
    halves = to_sibling(mixer.at[0:2], pair.at[:, core], 0)
    halves.start()
    shared = [
        to_sibling(w_out, wo.at[core], 1),
        to_sibling(w_gate, wgu.at[0, core], 2),
        to_sibling(w_up, wgu.at[1, core], 3),
        to_sibling(w_down, wd.at[core], 4),
        to_sibling(w_next, wn.at[core], 5),
    ]
    for copy in shared:
        copy.start()

    for load in smalls + loads[:1]:
        load.wait()
    lane = iota((1, TOKENS), 1)
    step_of = lane % STEPS
    inputs_raw = mix_v[2]
    inputs_f = inputs_raw.astype(F32)
    stacked = jnp.concatenate([edges[i] for i in range(EDGES)], axis=0)
    row96 = iota((EDGES * REQUESTS, TOKENS), 0)
    lane96 = iota((EDGES * REQUESTS, TOKENS), 1)
    conv = to_column(taps[TAPS - 1:TAPS, :]) * inputs_f
    for j in range(TAPS - 1):
        shift = TAPS - 1 - j
        early = row96 // REQUESTS - j
        place = (early >= 0) & (lane96 == (row96 % REQUESTS) * STEPS + early)
        from_edges = dot(stacked, jnp.where(place, 1.0, 0.0).astype(BF16), TN)
        moved = jnp.where(step_of >= shift, pltpu.roll(inputs_f, shift, axis=1), 0.0)
        conv = conv + to_column(taps[j:j + 1, :]) * (moved + from_edges)
    values[...] = conv.astype(BF16)

    pair[:, core] = mix_v[0:2]
    floor_row = floor[pl.ds(chip, 1), :]
    low = to_column(floor_row)
    halves.wait()
    for tile in range(TOKENS // TILE):
        at = slice(tile * TILE, (tile + 1) * TILE)
        step_t = iota((KEYS, TILE), 1) % STEPS
        q_pre = pair[0, :, :, at].reshape(KEYS, TILE).astype(F32)
        f_pre = pair[1, :, :, at].reshape(KEYS, TILE).astype(F32)
        query = q_pre * jax.nn.sigmoid(q_pre)
        forget = low + (1.0 - low) * jax.nn.sigmoid(f_pre)
        keyed = 1.0 - forget
        run = forget
        for shift in (1, 2, 4, 8):
            run = jnp.where(step_t >= shift, run * pltpu.roll(run, shift, axis=1), run)
        decay[:, at] = run
        query_b[:, at] = (query * run).astype(BF16)
        key_b[:, at] = (keyed / run).astype(BF16)

    loads[1].wait()
    gain_column = to_column(gain_mixer[...])
    squares = []
    for tile in range(TOKENS // TILE):
        at = slice(tile * TILE, (tile + 1) * TILE)
        q_t = query_b[:, at]
        begin = state_v[tile * TILE_REQ:(tile + 1) * TILE_REQ].astype(BF16).reshape(TILE_REQ * HALF, KEYS)
        through = dot(begin, q_t).reshape(TILE_REQ, HALF, TILE)
        ours = iota((TILE_REQ, HALF, TILE), 0) == iota((TILE_REQ, HALF, TILE), 2) // STEPS
        total = jnp.sum(jnp.where(ours, through, 0.0), axis=0)
        scores = dot(key_b[:, at], q_t, TN)
        source = iota((TILE, TILE), 0)
        sink = iota((TILE, TILE), 1)
        causal = (source // STEPS == sink // STEPS) & (source <= sink)
        scores = jnp.where(causal, scores, 0.0).astype(BF16)
        total = (total + dot(values[:, at], scores)) * KEYS ** (-0.5)
        gained_own[0:HALF, at] = (total * gain_column).astype(BF16)
        square = jnp.sum(total * total, axis=0, keepdims=True)
        gained_own[HALF:HALF + STEPS, at] = jnp.broadcast_to(square, (STEPS, TILE)).astype(BF16)

    own_lanes = pl.ds(pl.multiple_of(core * MINE, MINE), MINE)
    other_lanes = pl.ds(pl.multiple_of((1 - core) * MINE, MINE), MINE)
    gained_send[...] = gained_own[:, other_lanes]
    swap = to_sibling(gained_send, gained_recv, 6)
    swap.start()
    mine = gained_own[:, own_lanes]
    swap.wait()
    theirs = gained_recv[...]
    lower = jnp.where(core == 0, mine[0:HALF], theirs[0:HALF])
    upper = jnp.where(core == 0, theirs[0:HALF], mine[0:HALF])
    both = jnp.concatenate([lower, upper], axis=0)
    loads[2].wait()
    shared[0].wait()
    squares2 = jnp.concatenate([mine[HALF:], theirs[HALF:]], axis=0)
    pick_one = jnp.where(iota((2 * STEPS, EXTRA), 0) % STEPS == 0, 1.0, 0.0).astype(BF16)

    def folded(low_part, high_part):
        width = low_part.shape[1]
        return jnp.concatenate(
            [low_part.reshape(CHIPS, ROWS, width), high_part.reshape(CHIPS, ROWS, width)], axis=1
        ).astype(BF16)

    def spot(y, z, axis, absolute):
        if absolute:
            y, z = (y - at_y + SIDE) % SIDE, (z - at_z + SIDE) % SIDE
        return (y, z) if axis == 0 else (z, y)

    def put(blocks, ref, c, axis, absolute):
        width = blocks.shape[2]
        for y in range(SIDE):
            for z in range(SIDE):
                i, j = spot(y, z, axis, absolute)
                ref[c, i, j, :, 0:width] = blocks[y * SIDE + z]

    def link(source, target, ssem, rsem, c, axis, stage, k, towards):
        return pltpu.make_async_remote_copy(
            src_ref=source, dst_ref=target, send_sem=ssem.at[c, axis, stage, k - 1],
            recv_sem=rsem.at[c, axis, stage, k - 1], device_id=along(towards, k), device_id_type=MESH)

    far = slice(1, SIDE)

    class Sum:
        def __init__(self, sends, early, middle, late, sems):
            self.sends, self.early, self.middle, self.late, self.sems = sends, early, middle, late, sems

        def first(self, c, axis):
            return [
                link(self.sends[axis].at[c, k, far], self.early[axis].at[c, k, far],
                     *self.sems, c, axis, 0, k, axis)
                for k in range(1, SIDE)
            ]

        def near(self, c, axis):
            return [
                link(self.sends[axis].at[c, k, 0], self.early[axis].at[c, k, 0],
                     *self.sems, c, axis, 2, k, axis)
                for k in range(1, SIDE)
            ]

        def second(self, c, axis):
            return [
                link(self.middle[axis].at[c, k], self.late[axis].at[c, k],
                     *self.sems, c, axis, 1, k, 1 - axis)
                for k in range(1, SIDE)
            ]

        def begin(self, c, axis):
            for copy in self.first(c, axis):
                copy.start()

        def turn(self, c, axis):
            for copy in self.first(c, axis):
                copy.wait_recv()
            sums = self.sends[axis][c, 0, far].astype(F32)
            for k in range(1, SIDE):
                sums = sums + self.early[axis][c, k, far].astype(F32)
            self.middle[axis][c, far] = sums.astype(BF16)
            for copy in self.second(c, axis) + self.near(c, axis):
                copy.start()

        def end(self, c, axis):
            for copy in self.second(c, axis) + self.near(c, axis):
                copy.wait_recv()
            sums = self.sends[axis][c, 0, 0].astype(F32)
            for k in range(1, SIDE):
                sums = sums + self.early[axis][c, k, 0].astype(F32)
                sums = sums + self.late[axis][c, k].astype(F32)
            return sums

        def drain(self, c, axis):
            for copy in self.first(c, axis) + self.second(c, axis) + self.near(c, axis):
                copy.wait_send()

    class Gather:
        def __init__(self, refs, sems):
            self.refs, self.sems = refs, sems

        def first(self, c, axis):
            ref = self.refs[axis]
            return [
                link(ref.at[c, 0, 0], ref.at[c, 0, SIDE - k], *self.sems, c, axis, 0, k, 1 - axis)
                for k in range(1, SIDE)
            ]

        def near(self, c, axis):
            ref = self.refs[axis]
            return [
                link(ref.at[c, 0, 0], ref.at[c, SIDE - k, 0], *self.sems, c, axis, 2, k, axis)
                for k in range(1, SIDE)
            ]

        def second(self, c, axis):
            ref = self.refs[axis]
            return [
                link(ref.at[c, 0, far], ref.at[c, SIDE - k, far], *self.sems, c, axis, 1, k, axis)
                for k in range(1, SIDE)
            ]

        def begin(self, c, rows):
            block = jnp.concatenate([rows[:, 0:FOLD], rows[:, FOLD:]], axis=0).astype(BF16)
            for axis in range(2):
                self.refs[axis][c, 0, 0] = block[:, axis * LANES:(axis + 1) * LANES]
                for copy in self.first(c, axis):
                    copy.start()
            for axis in range(2):
                for copy in self.near(c, axis):
                    copy.start()

        def turn(self, c):
            for axis in range(2):
                for copy in self.first(c, axis):
                    copy.wait_recv()
                for copy in self.second(c, axis):
                    copy.start()

        def end(self, c, absolute):
            for axis in range(2):
                for copy in self.near(c, axis) + self.second(c, axis):
                    copy.wait_recv()
            rows = [[], []]
            for axis in range(2):
                blocks = []
                for y in range(SIDE):
                    for z in range(SIDE):
                        i, j = spot(y, z, axis, absolute)
                        blocks.append(self.refs[axis][c, i, j].astype(F32))
                rows[0].append(jnp.concatenate([block[0:ROWS] for block in blocks], axis=0))
                rows[1].append(jnp.concatenate([block[ROWS:] for block in blocks], axis=0))
            return jnp.concatenate(rows[0] + rows[1], axis=1).astype(BF16)

        def drain(self, c):
            for axis in range(2):
                for copy in self.first(c, axis) + self.near(c, axis) + self.second(c, axis):
                    copy.wait_send()

    def unfold(left, right):
        return jnp.concatenate([left[0:ROWS], right[0:ROWS], left[ROWS:], right[ROWS:]], axis=1)

    sum1 = Sum((send1a, send1b), (early1a, early1b), (middle1a, middle1b), (late1a, late1b), (ss1, rs1))
    spread1 = Gather((gather1a, gather1b), (ss2, rs2))
    sum2 = Sum((send2a, send2b), (early2a, early2b), (middle2a, middle2b), (late2a, late2b), (ss1, rs1))
    spread2 = Gather((gather2a, gather2b), (ss2, rs2))

    for c in range(CHUNKS):
        part = slice(c * PART, (c + 1) * PART)
        square = dot(squares2[:, part], pick_one, TN)
        square = folded(square, square)
        channels = both[:, part]
        for axis in range(2):
            low_at = slice(axis * LANES, (axis + 1) * LANES)
            high_at = slice(FOLD + axis * LANES, FOLD + (axis + 1) * LANES)
            terms = folded(
                dot(channels, wo[:, :, low_at].reshape(2 * HALF, LANES), TN),
                dot(channels, wo[:, :, high_at].reshape(2 * HALF, LANES), TN))
            if axis == 0:
                terms = jnp.concatenate([terms, square], axis=2)
            put(terms, sum1.sends[axis], c, axis, True)
            sum1.begin(c, axis)

    acc_column = to_column(accepted[...])
    row32 = iota((REQUESTS, TOKENS), 0)
    lane32 = iota((REQUESTS, TOKENS), 1)
    acc_lanes = jnp.sum(jnp.where(lane32 // STEPS == row32, acc_column, 0), axis=0, keepdims=True)
    last = jnp.where(lane32 == row32 * STEPS + acc_column - 1, 1.0, 0.0)
    last = jnp.where(acc_column > 0, last, 0.0).astype(BF16)
    run_all = decay[...]
    run_high = run_all.astype(BF16)
    run_low = (run_all - run_high.astype(F32)).astype(BF16)
    run_picked = dot(last, run_high, NT) + dot(last, run_low, NT)
    picked[...] = jnp.where(acc_column == 0, 1.0, run_picked)
    live = step_of < acc_lanes
    for tile in range(TOKENS // TILE):
        at = slice(tile * TILE, (tile + 1) * TILE)
        taken = jnp.where(live[:, at], values[:, at].astype(F32), 0.0)
        spread = jnp.broadcast_to(taken[None], (TILE_REQ, HALF, TILE))
        ours = iota((TILE_REQ, HALF, TILE), 0) == iota((TILE_REQ, HALF, TILE), 2) // STEPS
        spread = jnp.where(ours, spread, 0.0).astype(BF16).reshape(TILE_REQ * HALF, TILE)
        added = dot(spread, key_b[:, at], NT)
        for i in range(TILE_REQ):
            r = tile * TILE_REQ + i
            kept_v[r] = (picked[r:r + 1, :] * (state_v[r] + added[i * HALF:(i + 1) * HALF])).astype(BF16)
    for e in range(EDGES):
        place = jnp.where(lane32 == row32 * STEPS + acc_column + (e - EDGES), 1.0, 0.0)
        place = jnp.where(acc_column + e >= EDGES, place, 0.0).astype(BF16)
        kept_edge = dot(place, inputs_raw, NT)
        for i in range(EDGES):
            kept_edge = kept_edge + jnp.where(acc_column + e == i, edges[i].astype(F32), 0.0)
        edge_v[e] = kept_edge.astype(BF16)

    def cross(k):
        return [
            pltpu.make_async_remote_copy(
                src_ref=source, dst_ref=target.at[group], send_sem=ss_x.at[slot, k - 1],
                recv_sem=rs_x.at[slot, k - 1], device_id=across(k), device_id_type=MESH)
            for slot, (source, target) in enumerate(((kept_v, kept_all), (edge_v, edge_all)))
        ]

    crossing = [copy for k in range(1, GROUPS) for copy in cross(k)]
    for copy in crossing:
        copy.start()
    kept_all[group] = kept_v[...]
    edge_all[group] = edge_v[...]

    def scaled_norm(rows, gain):
        factor = lax.rsqrt(jnp.mean(rows * rows, axis=1, keepdims=True) + EPSILON)
        return rows * factor * gain

    for c in range(CHUNKS):
        for axis in range(2):
            sum1.turn(c, axis)
    for load in loads[3:]:
        load.wait()
    for c in range(CHUNKS):
        left = sum1.end(c, 0)
        right = sum1.end(c, 1)
        near = res_v[c].astype(F32)
        before = jnp.where(chip % 2 == 0, near[0:ROWS], near[ROWS:])
        square = left[0:ROWS, LANES:LANES + 1]
        attn = unfold(left[:, 0:LANES], right) * lax.rsqrt(square / WIDTH + EPSILON)
        first = (before + attn).astype(BF16).astype(F32)
        first_v[c] = first
        spread1.begin(c, scaled_norm(first, gain_mlp[...]))
    for c in range(CHUNKS):
        spread1.turn(c)
    for c in range(CHUNKS):
        for axis in range(2):
            sum1.drain(c, axis)
    for copy in shared[1:]:
        copy.wait()

    hidden_width = wd.shape[0] * wd.shape[1]
    for c in range(CHUNKS):
        both_parts = dot(wgu[...].reshape(2 * hidden_width, WIDTH), spread1.end(c, False), NT)
        gate = both_parts[0:hidden_width]
        hidden = (gate * jax.nn.sigmoid(gate) * both_parts[hidden_width:]).astype(BF16)
        for axis in range(2):
            low_at = slice(axis * LANES, (axis + 1) * LANES)
            high_at = slice(FOLD + axis * LANES, FOLD + (axis + 1) * LANES)
            put(folded(
                dot(hidden, wd[:, :, low_at].reshape(hidden_width, LANES), TN),
                dot(hidden, wd[:, :, high_at].reshape(hidden_width, LANES), TN),
            ), sum2.sends[axis], c, axis, False)
            sum2.begin(c, axis)
    for c in range(CHUNKS):
        spread1.drain(c)

    for c in range(CHUNKS):
        for axis in range(2):
            sum2.turn(c, axis)
    for c in range(CHUNKS):
        down = unfold(sum2.end(c, 0), sum2.end(c, 1))
        second = (first_v[c] + down).astype(BF16).astype(F32)
        spread2.begin(c, scaled_norm(second, gain_next[...]))
    for c in range(CHUNKS):
        spread2.turn(c)

    for copy in crossing:
        copy.wait()
    home_row = home[...]
    source_lane = iota((1, GROUPS * REQUESTS), 1)
    for i in range(REQUESTS):
        found = jnp.max(jnp.where(home_row == group * REQUESTS + i, source_lane, 0))
        kept_out[i] = kept_all[found // REQUESTS, found % REQUESTS].astype(F32)
    leaving = pltpu.make_async_copy(kept_out, kept_home, load_sem.at[8 + CHUNKS])
    leaving.start()
    target_row = iota((REQUESTS, GROUPS * REQUESTS), 0) + group * REQUESTS
    chosen = jnp.where(home_row == target_row, 1.0, 0.0).astype(BF16)
    for e in range(EDGES):
        pool = edge_all[:, e].reshape(GROUPS * REQUESTS, HALF)
        edge_out[e] = dot(chosen, pool).astype(BF16)

    for c in range(CHUNKS):
        for axis in range(2):
            sum2.drain(c, axis)

    swaps = []
    for c in range(CHUNKS):
        normed = spread2.end(c, True)
        theirs_next = dot(wn[1 - core].reshape(3 * HALF, WIDTH), normed, NT)
        next_send[c] = theirs_next.astype(BF16).reshape(3, HALF, PART)
        swaps.append(to_sibling(next_send.at[c], next_recv.at[c], 7 + c))
        swaps[c].start()
        own_next = dot(wn[core].reshape(3 * HALF, WIDTH), normed, NT)
        here = pl.ds(pl.multiple_of(core * MINE + c * PART, PART), PART)
        next_out[:, :, here] = own_next.astype(BF16).reshape(3, HALF, PART)
    for c in range(CHUNKS):
        spread2.drain(c)
        swaps[c].wait()
        there = pl.ds(pl.multiple_of((1 - core) * MINE + c * PART, PART), PART)
        next_out[:, :, there] = next_recv[c]
    leaving.wait()


PIECES = 4
PIECE = REQUESTS // PIECES


def finish(next_in, kept_in, edge_in, next_out, kept_out, edge_out, next_v, kept_v, edge_v, in_sems, out_sems):
    parts = [slice(i * PIECE, (i + 1) * PIECE) for i in range(PIECES)]
    routes = [(kept_in.at[part], kept_v.at[part], kept_out.at[part]) for part in parts]
    routes += [(next_in, next_v, next_out), (edge_in, edge_v, edge_out)]
    arrive = [pltpu.make_async_copy(a, b, in_sems.at[i]) for i, (a, b, _) in enumerate(routes)]
    leave = [pltpu.make_async_copy(b, c, out_sems.at[i]) for i, (_, b, c) in enumerate(routes)]
    for copy in arrive:
        copy.start()
    for copy, further in zip(arrive, leave):
        copy.wait()
        further.start()
    for copy in leave:
        copy.wait()


def sum_buffers(width_a):
    grids = [(SIDE, SIDE), (SIDE, SIDE), (SIDE,), (SIDE,)]
    return [
        pltpu.VMEM((CHUNKS, *grid, 2 * ROWS, width), BF16) for grid in grids for width in (width_a, LANES)
    ]


def gather_buffers():
    return [pltpu.VMEM((CHUNKS, SIDE, SIDE, 2 * ROWS, LANES), BF16)] * 2


def per_device(
    residual_in, mixer_in, forget_floor, conv_weight, conv_edges, state_in, accepted, home_slot,
    gain_mixer, w_out, gain_mlp, w_gate, w_up, w_down, gain_next, w_next,
):
    hidden_width = w_gate.shape[1]
    anywhere = pl.BlockSpec(memory_space=pl.ANY)
    vmem = pl.BlockSpec(memory_space=pltpu.VMEM)
    dma = pltpu.SemaphoreType.DMA
    outputs = (
        jax.ShapeDtypeStruct((3, HALF, TOKENS), BF16),
        jax.ShapeDtypeStruct((REQUESTS, HALF, KEYS), F32),
        jax.ShapeDtypeStruct((EDGES, REQUESTS, HALF), BF16),
    )
    results = pl.pallas_call(
        kernel,
        name="draft_check",
        out_shape=outputs,
        in_specs=[anywhere] * 16,
        out_specs=(vmem, anywhere, vmem),
        scratch_shapes=[
            pltpu.VMEM((CHIPS, KEYS), F32),
            pltpu.VMEM((TAPS, HALF), F32),
            pltpu.VMEM((EDGES, REQUESTS, HALF), BF16),
            pltpu.VMEM((1, REQUESTS), jnp.int32),
            pltpu.VMEM((1, GROUPS * REQUESTS), jnp.int32),
            pltpu.VMEM((1, HALF), F32),
            pltpu.VMEM((1, WIDTH), F32),
            pltpu.VMEM((1, WIDTH), F32),
            pltpu.VMEM((REQUESTS, HALF, KEYS), F32),
            pltpu.VMEM((3, HALF, TOKENS), BF16),
            pltpu.VMEM((2, 2, HALF, TOKENS), BF16),
            pltpu.VMEM((REQUESTS, HALF, KEYS), F32),
            pltpu.VMEM((CHUNKS, 2 * ROWS, WIDTH), BF16),
            pltpu.VMEM((2, HALF, WIDTH), BF16),
            pltpu.VMEM((2, 2, hidden_width, WIDTH), BF16),
            pltpu.VMEM((2, hidden_width, WIDTH), BF16),
            pltpu.VMEM((2, 3, HALF, WIDTH), BF16),
            pltpu.VMEM((KEYS, TOKENS), BF16),
            pltpu.VMEM((KEYS, TOKENS), BF16),
            pltpu.VMEM((KEYS, TOKENS), F32),
            pltpu.VMEM((HALF, TOKENS), BF16),
            pltpu.VMEM((REQUESTS, KEYS), F32),
            pltpu.VMEM((HALF + STEPS, TOKENS), BF16),
            pltpu.VMEM((HALF + STEPS, MINE), BF16),
            pltpu.VMEM((HALF + STEPS, MINE), BF16),
            *sum_buffers(LANES + EXTRA), *gather_buffers(),
            pltpu.VMEM((CHUNKS, ROWS, WIDTH), F32),
            *sum_buffers(LANES), *gather_buffers(),
            pltpu.VMEM((CHUNKS, 3, HALF, PART), BF16),
            pltpu.VMEM((CHUNKS, 3, HALF, PART), BF16),
            pltpu.VMEM((REQUESTS, HALF, KEYS), BF16),
            pltpu.VMEM((EDGES, REQUESTS, HALF), BF16),
            pltpu.VMEM((GROUPS, REQUESTS, HALF, KEYS), BF16),
            pltpu.VMEM((GROUPS, EDGES, REQUESTS, HALF), BF16),
            dma((9 + CHUNKS,)), dma((8,)), dma((7 + CHUNKS,)), dma((7 + CHUNKS,)),
            *[dma((CHUNKS, 2, 3, SIDE - 1))] * 4,
            dma((2, GROUPS - 1)), dma((2, GROUPS - 1)),
        ],
        compiler_params=pltpu.CompilerParams(
            collective_id=0, has_side_effects=True, vmem_limit_bytes=56 * 2**20),
    )(
        residual_in,
        mixer_in.transpose(1, 2, 0),
        forget_floor.reshape(-1, KEYS),
        conv_weight,
        conv_edges.transpose(1, 0, 2),
        state_in,
        accepted.reshape(1, -1),
        home_slot.reshape(1, -1),
        gain_mixer.reshape(1, -1),
        w_out,
        gain_mlp.reshape(1, -1),
        w_gate.T,
        w_up.T,
        w_down,
        gain_next.reshape(1, -1),
        w_next.transpose(1, 2, 0),
    )
    next_flat, kept, kept_edges = pl.pallas_call(
        finish,
        name="finish",
        out_shape=outputs,
        in_specs=[anywhere] * 3,
        out_specs=(anywhere,) * 3,
        scratch_shapes=[
            *[pltpu.VMEM(output.shape, output.dtype) for output in outputs],
            dma((PIECES + 2,)), dma((PIECES + 2,)),
        ],
        compiler_params=pltpu.CompilerParams(vmem_limit_bytes=56 * 2**20),
    )(*results)
    return next_flat.transpose(2, 0, 1), kept, kept_edges.transpose(1, 0, 2)


def solution(mesh):
    in_specs = (
        P("grp", None),
        P("grp", None, "req"),
        P(),
        P(None, "req"),
        P("grp", None, "req"),
        P("grp", "req", None),
        P("grp"),
        P(),
        P("req"),
        P("req", None),
        P(),
        P(None, "req"),
        P(None, "req"),
        P("req", None),
        P(),
        P(None, None, "req"),
    )
    out_specs = (P("grp", None, "req"), P("grp", "req", None), P("grp", None, "req"))
    return jax.shard_map(
        per_device, mesh=mesh, in_specs=in_specs, out_specs=out_specs, check_vma=False
    )
```

```python
import jax
import jax.numpy as jnp
from jax import lax
from jax.experimental import pallas as pl
from jax.experimental.pallas import tpu as pltpu
from jax.sharding import PartitionSpec as P

EPSILON = 1e-06
MESH = pl.DeviceIdType.MESH
F32 = jnp.float32
BF16 = jnp.bfloat16

SIDE = 4
CHIPS = SIDE * SIDE
GROUPS = 4
STEPS = 16
TAPS = 4
EDGES = 3
WIDTH = 2048
HALF = 64
KEYS = 128
EXTRA = 128
REQUESTS = 32
TOKENS = REQUESTS * STEPS
MINE = TOKENS // 2
TILE = 128
TILE_REQ = TILE // STEPS
CHUNKS = 2
PART = MINE // CHUNKS
ROWS = PART // CHIPS
FOLD = WIDTH // 2
LANES = FOLD // 2

NT = (((1,), (1,)), ((), ()))
TN = (((0,), (0,)), ((), ()))


def dot(left, right, dims=(((1,), (0,)), ((), ()))):
    return lax.dot_general(left, right, dims, preferred_element_type=F32)


def iota(shape, dim):
    return lax.broadcasted_iota(jnp.int32, shape, dim)


def to_column(row):
    size = row.shape[1]
    square = jnp.broadcast_to(row, (size, size))
    diagonal = iota((size, size), 0) == iota((size, size), 1)
    return jnp.sum(jnp.where(diagonal, square, jnp.zeros_like(square)), axis=1, keepdims=True)


def kernel(
    residual, mixer, floor_in, taps_in, edges_in, state, accepted_in, home_in, gain_mixer_in,
    w_out, gain_mlp_in, w_gate, w_up, w_down, gain_next_in, w_next,
    next_out, kept_home, edge_out,
    floor, taps, edges, accepted, home, gain_mixer, gain_mlp, gain_next, kept_out, mix_v, pair, state_v, res_v, wo, wgu, wd, wn,
    query_b, key_b, decay, values, picked, gained_own, gained_send, gained_recv,
    send1a, send1b, early1a, early1b, middle1a, middle1b, late1a, late1b, gather1a, gather1b, first_v,
    send2a, send2b, early2a, early2b, middle2a, middle2b, late2a, late2b, gather2a, gather2b,
    next_send, next_recv, kept_v, edge_v, kept_all, edge_all,
    load_sem, small_sem, pair_ss, pair_rs, ss1, rs1, ss2, rs2, ss_x, rs_x,
):
    member = lax.axis_index("req")
    group = lax.axis_index("grp")
    core = member % 2
    chip = member // 2
    at_y = chip // SIDE
    at_z = chip % SIDE
    sibling = {"req": chip * 2 + (1 - core), "grp": group}

    def along(axis, k):
        if axis == 0:
            chip_at = (at_y + k) % SIDE * SIDE + at_z
        else:
            chip_at = at_y * SIDE + (at_z + k) % SIDE
        return {"req": chip_at * 2 + core, "grp": group}

    def across(k):
        return {"req": member, "grp": (group + k) % GROUPS}

    barrier = pltpu.get_barrier_semaphore()

    pl.semaphore_signal(barrier, inc=1, device_id=sibling, device_id_type=MESH)
    for axis in range(2):
        for k in range(1, SIDE):
            pl.semaphore_signal(barrier, inc=1, device_id=along(axis, k), device_id_type=MESH)
    for k in range(1, GROUPS):
        pl.semaphore_signal(barrier, inc=1, device_id=across(k), device_id_type=MESH)

    loads = [
        pltpu.make_async_copy(mixer, mix_v, load_sem.at[0]),
        pltpu.make_async_copy(state, state_v, load_sem.at[1]),
        pltpu.make_async_copy(w_out, wo.at[core], load_sem.at[2]),
        pltpu.make_async_copy(w_gate, wgu.at[0, core], load_sem.at[4]),
        pltpu.make_async_copy(w_up, wgu.at[1, core], load_sem.at[5]),
        pltpu.make_async_copy(w_down, wd.at[core], load_sem.at[6]),
        pltpu.make_async_copy(w_next, wn.at[core], load_sem.at[7]),
    ]
    for c in range(CHUNKS):
        near = core * MINE + c * PART + chip // 2 * (2 * ROWS)
        loads.append(pltpu.make_async_copy(
            residual.at[pl.ds(pl.multiple_of(near, 2 * ROWS), 2 * ROWS)], res_v.at[c], load_sem.at[8 + c]))
    smalls = [
        pltpu.make_async_copy(source, target, small_sem.at[i])
        for i, (source, target) in enumerate((
            (taps_in, taps), (edges_in, edges), (floor_in, floor), (gain_mixer_in, gain_mixer),
            (accepted_in, accepted), (home_in, home), (gain_mlp_in, gain_mlp), (gain_next_in, gain_next)))
    ]
    for load in loads[:1] + smalls + loads[1:]:
        load.start()

    def to_sibling(source, target, slot):
        return pltpu.make_async_remote_copy(
            src_ref=source, dst_ref=target, send_sem=pair_ss.at[slot], recv_sem=pair_rs.at[slot],
            device_id=sibling, device_id_type=MESH)

    pl.semaphore_wait(barrier, 1 + 2 * (SIDE - 1) + GROUPS - 1)
    halves = to_sibling(mixer.at[0:2], pair.at[:, core], 0)
    halves.start()
    shared = [
        to_sibling(w_out, wo.at[core], 1),
        to_sibling(w_gate, wgu.at[0, core], 2),
        to_sibling(w_up, wgu.at[1, core], 3),
        to_sibling(w_down, wd.at[core], 4),
        to_sibling(w_next, wn.at[core], 5),
    ]
    for copy in shared:
        copy.start()

    for load in smalls + loads[:1]:
        load.wait()
    lane = iota((1, TOKENS), 1)
    step_of = lane % STEPS
    inputs_raw = mix_v[2]
    inputs_f = inputs_raw.astype(F32)
    stacked = jnp.concatenate([edges[i] for i in range(EDGES)], axis=0)
    row96 = iota((EDGES * REQUESTS, TOKENS), 0)
    lane96 = iota((EDGES * REQUESTS, TOKENS), 1)
    conv = to_column(taps[TAPS - 1:TAPS, :]) * inputs_f
    for j in range(TAPS - 1):
        shift = TAPS - 1 - j
        early = row96 // REQUESTS - j
        place = (early >= 0) & (lane96 == (row96 % REQUESTS) * STEPS + early)
        from_edges = dot(stacked, jnp.where(place, 1.0, 0.0).astype(BF16), TN)
        moved = jnp.where(step_of >= shift, pltpu.roll(inputs_f, shift, axis=1), 0.0)
        conv = conv + to_column(taps[j:j + 1, :]) * (moved + from_edges)
    values[...] = conv.astype(BF16)

    pair[:, core] = mix_v[0:2]
    floor_row = floor[pl.ds(chip, 1), :]
    low = to_column(floor_row)
    gain_column = to_column(gain_mixer[...])
    halves.wait()
    loads[1].wait()

    def gates(tile):
        at = slice(tile * TILE, (tile + 1) * TILE)
        step_t = iota((KEYS, TILE), 1) % STEPS
        q_pre = pair[0, :, :, at].reshape(KEYS, TILE).astype(F32)
        f_pre = pair[1, :, :, at].reshape(KEYS, TILE).astype(F32)
        query = q_pre * jax.nn.sigmoid(q_pre)
        forget = low + (1.0 - low) * jax.nn.sigmoid(f_pre)
        keyed = 1.0 - forget
        run = forget
        for shift in (1, 2, 4, 8):
            run = jnp.where(step_t >= shift, run * pltpu.roll(run, shift, axis=1), run)
        decay[:, at] = run
        query_b[:, at] = (query * run).astype(BF16)
        key_b[:, at] = (keyed / run).astype(BF16)

    def recurrence(tile):
        at = slice(tile * TILE, (tile + 1) * TILE)
        q_t = query_b[:, at]
        begin = state_v[tile * TILE_REQ:(tile + 1) * TILE_REQ].astype(BF16).reshape(TILE_REQ * HALF, KEYS)
        through = dot(begin, q_t).reshape(TILE_REQ, HALF, TILE)
        ours = iota((TILE_REQ, HALF, TILE), 0) == iota((TILE_REQ, HALF, TILE), 2) // STEPS
        total = jnp.sum(jnp.where(ours, through, 0.0), axis=0)
        scores = dot(key_b[:, at], q_t, TN)
        source = iota((TILE, TILE), 0)
        sink = iota((TILE, TILE), 1)
        causal = (source // STEPS == sink // STEPS) & (source <= sink)
        scores = jnp.where(causal, scores, 0.0).astype(BF16)
        total = (total + dot(values[:, at], scores)) * KEYS ** (-0.5)
        gained_own[0:HALF, at] = (total * gain_column).astype(BF16)
        square = jnp.sum(total * total, axis=0, keepdims=True)
        gained_own[HALF:HALF + STEPS, at] = jnp.broadcast_to(square, (STEPS, TILE)).astype(BF16)

    gained_swaps = []
    for c in range(CHUNKS):
        for tile in (c, CHUNKS + c):
            gates(tile)
            recurrence(tile)
        other_lanes = pl.ds(pl.multiple_of((1 - core) * MINE + c * PART, PART), PART)
        gained_send[c] = gained_own[:, other_lanes]
        gained_swaps.append(to_sibling(gained_send.at[c], gained_recv.at[c], 6 + c))
        gained_swaps[c].start()
    pick_one = jnp.where(iota((2 * STEPS, EXTRA), 0) % STEPS == 0, 1.0, 0.0).astype(BF16)

    def folded(low_part, high_part):
        width = low_part.shape[1]
        return jnp.concatenate(
            [low_part.reshape(CHIPS, ROWS, width), high_part.reshape(CHIPS, ROWS, width)], axis=1
        ).astype(BF16)

    def spot(y, z, axis, absolute):
        if absolute:
            y, z = (y - at_y + SIDE) % SIDE, (z - at_z + SIDE) % SIDE
        return (y, z) if axis == 0 else (z, y)

    def put(blocks, ref, c, axis, absolute):
        width = blocks.shape[2]
        for y in range(SIDE):
            for z in range(SIDE):
                i, j = spot(y, z, axis, absolute)
                ref[c, i, j, :, 0:width] = blocks[y * SIDE + z]

    def link(source, target, ssem, rsem, c, axis, stage, k, towards):
        return pltpu.make_async_remote_copy(
            src_ref=source, dst_ref=target, send_sem=ssem.at[c, axis, stage],
            recv_sem=rsem.at[c, axis, stage], device_id=along(towards, k), device_id_type=MESH)

    far = slice(1, SIDE)

    def wait_for(region, sem):
        pltpu.make_async_copy(region, region, sem).wait()


    class Sum:
        def __init__(self, sends, early, middle, late, sems):
            self.sends, self.early, self.middle, self.late, self.sems = sends, early, middle, late, sems

        def first(self, c, axis):
            return [
                link(self.sends[axis].at[c, k, far], self.early[axis].at[c, k, far],
                     *self.sems, c, axis, 0, k, axis)
                for k in range(1, SIDE)
            ]

        def near(self, c, axis):
            return [
                link(self.sends[axis].at[c, k, 0], self.early[axis].at[c, k, 0],
                     *self.sems, c, axis, 2, k, axis)
                for k in range(1, SIDE)
            ]

        def second(self, c, axis):
            return [
                link(self.middle[axis].at[c, k], self.late[axis].at[c, k],
                     *self.sems, c, axis, 1, k, 1 - axis)
                for k in range(1, SIDE)
            ]

        def begin(self, c, axis):
            for copy in self.first(c, axis):
                copy.start()

        def turn(self, c, axis):
            wait_for(self.early[axis].at[c, far, far], self.sems[1].at[c, axis, 0])
            sums = self.sends[axis][c, 0, far].astype(F32)
            for k in range(1, SIDE):
                sums = sums + self.early[axis][c, k, far].astype(F32)
            self.middle[axis][c, far] = sums.astype(BF16)
            for copy in self.second(c, axis) + self.near(c, axis):
                copy.start()

        def end(self, c, axis):
            wait_for(self.late[axis].at[c, far], self.sems[1].at[c, axis, 1])
            wait_for(self.early[axis].at[c, far, 0], self.sems[1].at[c, axis, 2])
            sums = self.sends[axis][c, 0, 0].astype(F32)
            for k in range(1, SIDE):
                sums = sums + self.early[axis][c, k, 0].astype(F32)
                sums = sums + self.late[axis][c, k].astype(F32)
            return sums

        def drain(self, c, axis):
            wait_for(self.sends[axis].at[c, far, far], self.sems[0].at[c, axis, 0])
            wait_for(self.middle[axis].at[c, far], self.sems[0].at[c, axis, 1])
            wait_for(self.sends[axis].at[c, far, 0], self.sems[0].at[c, axis, 2])

    class Gather:
        def __init__(self, refs, sems):
            self.refs, self.sems = refs, sems

        def first(self, c, axis):
            ref = self.refs[axis]
            return [
                link(ref.at[c, 0, 0], ref.at[c, 0, SIDE - k], *self.sems, c, axis, 0, k, 1 - axis)
                for k in range(1, SIDE)
            ]

        def near(self, c, axis):
            ref = self.refs[axis]
            return [
                link(ref.at[c, 0, 0], ref.at[c, SIDE - k, 0], *self.sems, c, axis, 2, k, axis)
                for k in range(1, SIDE)
            ]

        def second(self, c, axis):
            ref = self.refs[axis]
            return [
                link(ref.at[c, 0, far], ref.at[c, SIDE - k, far], *self.sems, c, axis, 1, k, axis)
                for k in range(1, SIDE)
            ]

        def begin(self, c, rows):
            block = jnp.concatenate([rows[:, 0:FOLD], rows[:, FOLD:]], axis=0).astype(BF16)
            for axis in range(2):
                self.refs[axis][c, 0, 0] = block[:, axis * LANES:(axis + 1) * LANES]
                for copy in self.first(c, axis):
                    copy.start()
            for axis in range(2):
                for copy in self.near(c, axis):
                    copy.start()

        def turn(self, c):
            for axis in range(2):
                wait_for(self.refs[axis].at[c, 0, far], self.sems[1].at[c, axis, 0])
                for copy in self.second(c, axis):
                    copy.start()

        def end(self, c, absolute):
            for axis in range(2):
                wait_for(self.refs[axis].at[c, far, far], self.sems[1].at[c, axis, 1])
                wait_for(self.refs[axis].at[c, far, 0], self.sems[1].at[c, axis, 2])
            rows = [[], []]
            for axis in range(2):
                blocks = []
                for y in range(SIDE):
                    for z in range(SIDE):
                        i, j = spot(y, z, axis, absolute)
                        blocks.append(self.refs[axis][c, i, j].astype(F32))
                rows[0].append(jnp.concatenate([block[0:ROWS] for block in blocks], axis=0))
                rows[1].append(jnp.concatenate([block[ROWS:] for block in blocks], axis=0))
            return jnp.concatenate(rows[0] + rows[1], axis=1).astype(BF16)

        def drain(self, c):
            for axis in range(2):
                wait_for(self.refs[axis].at[c, 0, far], self.sems[0].at[c, axis, 0])
                wait_for(self.refs[axis].at[c, far, far], self.sems[0].at[c, axis, 1])
                wait_for(self.refs[axis].at[c, far, 0], self.sems[0].at[c, axis, 2])

    def unfold(left, right):
        return jnp.concatenate([left[0:ROWS], right[0:ROWS], left[ROWS:], right[ROWS:]], axis=1)

    sum1 = Sum((send1a, send1b), (early1a, early1b), (middle1a, middle1b), (late1a, late1b), (ss1, rs1))
    spread1 = Gather((gather1a, gather1b), (ss2, rs2))
    sum2 = Sum((send2a, send2b), (early2a, early2b), (middle2a, middle2b), (late2a, late2b), (ss1, rs1))
    spread2 = Gather((gather2a, gather2b), (ss2, rs2))

    loads[2].wait()
    shared[0].wait()
    for c in range(CHUNKS):
        own_lanes = pl.ds(pl.multiple_of(core * MINE + c * PART, PART), PART)
        mine = gained_own[:, own_lanes]
        gained_swaps[c].wait()
        theirs = gained_recv[c]
        lower = jnp.where(core == 0, mine[0:HALF], theirs[0:HALF])
        upper = jnp.where(core == 0, theirs[0:HALF], mine[0:HALF])
        channels = jnp.concatenate([lower, upper], axis=0)
        squares2 = jnp.concatenate([mine[HALF:], theirs[HALF:]], axis=0)
        square = dot(squares2, pick_one, TN)
        square = folded(square, square)
        for axis in range(2):
            low_at = slice(axis * LANES, (axis + 1) * LANES)
            high_at = slice(FOLD + axis * LANES, FOLD + (axis + 1) * LANES)
            terms = folded(
                dot(channels, wo[:, :, low_at].reshape(2 * HALF, LANES), TN),
                dot(channels, wo[:, :, high_at].reshape(2 * HALF, LANES), TN))
            if axis == 0:
                terms = jnp.concatenate([terms, square], axis=2)
            put(terms, sum1.sends[axis], c, axis, True)
            sum1.begin(c, axis)

    acc_column = to_column(accepted[...])
    row32 = iota((REQUESTS, TOKENS), 0)
    lane32 = iota((REQUESTS, TOKENS), 1)
    acc_lanes = jnp.sum(jnp.where(lane32 // STEPS == row32, acc_column, 0), axis=0, keepdims=True)
    last = jnp.where(lane32 == row32 * STEPS + acc_column - 1, 1.0, 0.0)
    last = jnp.where(acc_column > 0, last, 0.0).astype(BF16)
    run_all = decay[...]
    run_high = run_all.astype(BF16)
    run_low = (run_all - run_high.astype(F32)).astype(BF16)
    run_picked = dot(last, run_high, NT) + dot(last, run_low, NT)
    picked[...] = jnp.where(acc_column == 0, 1.0, run_picked)
    live = step_of < acc_lanes
    for tile in range(TOKENS // TILE):
        at = slice(tile * TILE, (tile + 1) * TILE)
        taken = jnp.where(live[:, at], values[:, at].astype(F32), 0.0)
        spread = jnp.broadcast_to(taken[None], (TILE_REQ, HALF, TILE))
        ours = iota((TILE_REQ, HALF, TILE), 0) == iota((TILE_REQ, HALF, TILE), 2) // STEPS
        spread = jnp.where(ours, spread, 0.0).astype(BF16).reshape(TILE_REQ * HALF, TILE)
        added = dot(spread, key_b[:, at], NT)
        for i in range(TILE_REQ):
            r = tile * TILE_REQ + i
            kept_v[r] = (picked[r:r + 1, :] * (state_v[r] + added[i * HALF:(i + 1) * HALF])).astype(BF16)
    for e in range(EDGES):
        place = jnp.where(lane32 == row32 * STEPS + acc_column + (e - EDGES), 1.0, 0.0)
        place = jnp.where(acc_column + e >= EDGES, place, 0.0).astype(BF16)
        kept_edge = dot(place, inputs_raw, NT)
        for i in range(EDGES):
            kept_edge = kept_edge + jnp.where(acc_column + e == i, edges[i].astype(F32), 0.0)
        edge_v[e] = kept_edge.astype(BF16)

    def cross(k):
        return [
            pltpu.make_async_remote_copy(
                src_ref=source, dst_ref=target.at[group], send_sem=ss_x.at[slot, k - 1],
                recv_sem=rs_x.at[slot, k - 1], device_id=across(k), device_id_type=MESH)
            for slot, (source, target) in enumerate(((kept_v, kept_all), (edge_v, edge_all)))
        ]

    crossing = [copy for k in range(1, GROUPS) for copy in cross(k)]
    for copy in crossing:
        copy.start()
    kept_all[group] = kept_v[...]
    edge_all[group] = edge_v[...]

    def scaled_norm(rows, gain):
        factor = lax.rsqrt(jnp.mean(rows * rows, axis=1, keepdims=True) + EPSILON)
        return rows * factor * gain

    for c in range(CHUNKS):
        for axis in range(2):
            sum1.turn(c, axis)
    for load in loads[3:]:
        load.wait()
    for c in range(CHUNKS):
        left = sum1.end(c, 0)
        right = sum1.end(c, 1)
        near = res_v[c].astype(F32)
        before = jnp.where(chip % 2 == 0, near[0:ROWS], near[ROWS:])
        square = left[0:ROWS, LANES:LANES + 1]
        attn = unfold(left[:, 0:LANES], right) * lax.rsqrt(square / WIDTH + EPSILON)
        first = (before + attn).astype(BF16).astype(F32)
        first_v[c] = first
        spread1.begin(c, scaled_norm(first, gain_mlp[...]))
    for c in range(CHUNKS):
        spread1.turn(c)
    for c in range(CHUNKS):
        for axis in range(2):
            sum1.drain(c, axis)
    for copy in shared[1:]:
        copy.wait()

    hidden_width = wd.shape[0] * wd.shape[1]
    for c in range(CHUNKS):
        both_parts = dot(wgu[...].reshape(2 * hidden_width, WIDTH), spread1.end(c, False), NT)
        gate = both_parts[0:hidden_width]
        hidden = (gate * jax.nn.sigmoid(gate) * both_parts[hidden_width:]).astype(BF16)
        for axis in range(2):
            low_at = slice(axis * LANES, (axis + 1) * LANES)
            high_at = slice(FOLD + axis * LANES, FOLD + (axis + 1) * LANES)
            put(folded(
                dot(hidden, wd[:, :, low_at].reshape(hidden_width, LANES), TN),
                dot(hidden, wd[:, :, high_at].reshape(hidden_width, LANES), TN),
            ), sum2.sends[axis], c, axis, False)
            sum2.begin(c, axis)
    for c in range(CHUNKS):
        spread1.drain(c)

    for c in range(CHUNKS):
        for axis in range(2):
            sum2.turn(c, axis)
    for c in range(CHUNKS):
        down = unfold(sum2.end(c, 0), sum2.end(c, 1))
        second = (first_v[c] + down).astype(BF16).astype(F32)
        spread2.begin(c, scaled_norm(second, gain_next[...]))
    for c in range(CHUNKS):
        spread2.turn(c)

    for copy in crossing:
        copy.wait()
    home_row = home[...]
    source_lane = iota((1, GROUPS * REQUESTS), 1)
    for i in range(REQUESTS):
        found = jnp.max(jnp.where(home_row == group * REQUESTS + i, source_lane, 0))
        kept_out[i] = kept_all[found // REQUESTS, found % REQUESTS].astype(F32)
    leaving = pltpu.make_async_copy(kept_out, kept_home, load_sem.at[8 + CHUNKS])
    leaving.start()
    target_row = iota((REQUESTS, GROUPS * REQUESTS), 0) + group * REQUESTS
    chosen = jnp.where(home_row == target_row, 1.0, 0.0).astype(BF16)
    for e in range(EDGES):
        pool = edge_all[:, e].reshape(GROUPS * REQUESTS, HALF)
        edge_out[e] = dot(chosen, pool).astype(BF16)

    for c in range(CHUNKS):
        for axis in range(2):
            sum2.drain(c, axis)

    swaps = []
    for c in range(CHUNKS):
        normed = spread2.end(c, True)
        theirs_next = dot(wn[1 - core].reshape(3 * HALF, WIDTH), normed, NT)
        next_send[c] = theirs_next.astype(BF16).reshape(3, HALF, PART)
        swaps.append(to_sibling(next_send.at[c], next_recv.at[c], 6 + CHUNKS + c))
        swaps[c].start()
        own_next = dot(wn[core].reshape(3 * HALF, WIDTH), normed, NT)
        here = pl.ds(pl.multiple_of(core * MINE + c * PART, PART), PART)
        next_out[:, :, here] = own_next.astype(BF16).reshape(3, HALF, PART)
    for c in range(CHUNKS):
        spread2.drain(c)
        swaps[c].wait()
        there = pl.ds(pl.multiple_of((1 - core) * MINE + c * PART, PART), PART)
        next_out[:, :, there] = next_recv[c]
    leaving.wait()


PIECES = 4
PIECE = REQUESTS // PIECES


def finish(next_in, kept_in, edge_in, next_out, kept_out, edge_out, next_v, kept_v, edge_v, in_sems, out_sems):
    parts = [slice(i * PIECE, (i + 1) * PIECE) for i in range(PIECES)]
    routes = [(kept_in.at[part], kept_v.at[part], kept_out.at[part]) for part in parts]
    routes += [(next_in, next_v, next_out), (edge_in, edge_v, edge_out)]
    arrive = [pltpu.make_async_copy(a, b, in_sems.at[i]) for i, (a, b, _) in enumerate(routes)]
    leave = [pltpu.make_async_copy(b, c, out_sems.at[i]) for i, (_, b, c) in enumerate(routes)]
    for copy in arrive:
        copy.start()
    for copy, further in zip(arrive, leave):
        copy.wait()
        further.start()
    for copy in leave:
        copy.wait()


def sum_buffers(width_a):
    grids = [(SIDE, SIDE), (SIDE, SIDE), (SIDE,), (SIDE,)]
    return [
        pltpu.VMEM((CHUNKS, *grid, 2 * ROWS, width), BF16) for grid in grids for width in (width_a, LANES)
    ]


def gather_buffers():
    return [pltpu.VMEM((CHUNKS, SIDE, SIDE, 2 * ROWS, LANES), BF16)] * 2


def per_device(
    residual_in, mixer_in, forget_floor, conv_weight, conv_edges, state_in, accepted, home_slot,
    gain_mixer, w_out, gain_mlp, w_gate, w_up, w_down, gain_next, w_next,
):
    hidden_width = w_gate.shape[1]
    anywhere = pl.BlockSpec(memory_space=pl.ANY)
    vmem = pl.BlockSpec(memory_space=pltpu.VMEM)
    dma = pltpu.SemaphoreType.DMA
    outputs = (
        jax.ShapeDtypeStruct((3, HALF, TOKENS), BF16),
        jax.ShapeDtypeStruct((REQUESTS, HALF, KEYS), F32),
        jax.ShapeDtypeStruct((EDGES, REQUESTS, HALF), BF16),
    )
    results = pl.pallas_call(
        kernel,
        name="draft_check",
        out_shape=outputs,
        in_specs=[anywhere] * 16,
        out_specs=(vmem, anywhere, vmem),
        scratch_shapes=[
            pltpu.VMEM((CHIPS, KEYS), F32),
            pltpu.VMEM((TAPS, HALF), F32),
            pltpu.VMEM((EDGES, REQUESTS, HALF), BF16),
            pltpu.VMEM((1, REQUESTS), jnp.int32),
            pltpu.VMEM((1, GROUPS * REQUESTS), jnp.int32),
            pltpu.VMEM((1, HALF), F32),
            pltpu.VMEM((1, WIDTH), F32),
            pltpu.VMEM((1, WIDTH), F32),
            pltpu.VMEM((REQUESTS, HALF, KEYS), F32),
            pltpu.VMEM((3, HALF, TOKENS), BF16),
            pltpu.VMEM((2, 2, HALF, TOKENS), BF16),
            pltpu.VMEM((REQUESTS, HALF, KEYS), F32),
            pltpu.VMEM((CHUNKS, 2 * ROWS, WIDTH), BF16),
            pltpu.VMEM((2, HALF, WIDTH), BF16),
            pltpu.VMEM((2, 2, hidden_width, WIDTH), BF16),
            pltpu.VMEM((2, hidden_width, WIDTH), BF16),
            pltpu.VMEM((2, 3, HALF, WIDTH), BF16),
            pltpu.VMEM((KEYS, TOKENS), BF16),
            pltpu.VMEM((KEYS, TOKENS), BF16),
            pltpu.VMEM((KEYS, TOKENS), F32),
            pltpu.VMEM((HALF, TOKENS), BF16),
            pltpu.VMEM((REQUESTS, KEYS), F32),
            pltpu.VMEM((HALF + STEPS, TOKENS), BF16),
            pltpu.VMEM((CHUNKS, HALF + STEPS, PART), BF16),
            pltpu.VMEM((CHUNKS, HALF + STEPS, PART), BF16),
            *sum_buffers(LANES + EXTRA), *gather_buffers(),
            pltpu.VMEM((CHUNKS, ROWS, WIDTH), F32),
            *sum_buffers(LANES), *gather_buffers(),
            pltpu.VMEM((CHUNKS, 3, HALF, PART), BF16),
            pltpu.VMEM((CHUNKS, 3, HALF, PART), BF16),
            pltpu.VMEM((REQUESTS, HALF, KEYS), BF16),
            pltpu.VMEM((EDGES, REQUESTS, HALF), BF16),
            pltpu.VMEM((GROUPS, REQUESTS, HALF, KEYS), BF16),
            pltpu.VMEM((GROUPS, EDGES, REQUESTS, HALF), BF16),
            dma((9 + CHUNKS,)), dma((8,)), dma((6 + 2 * CHUNKS,)), dma((6 + 2 * CHUNKS,)),
            *[dma((CHUNKS, 2, 3))] * 4,
            dma((2, GROUPS - 1)), dma((2, GROUPS - 1)),
        ],
        compiler_params=pltpu.CompilerParams(
            collective_id=0, has_side_effects=True, vmem_limit_bytes=56 * 2**20),
    )(
        residual_in,
        mixer_in.transpose(1, 2, 0),
        forget_floor.reshape(-1, KEYS),
        conv_weight,
        conv_edges.transpose(1, 0, 2),
        state_in,
        accepted.reshape(1, -1),
        home_slot.reshape(1, -1),
        gain_mixer.reshape(1, -1),
        w_out,
        gain_mlp.reshape(1, -1),
        w_gate.T,
        w_up.T,
        w_down,
        gain_next.reshape(1, -1),
        w_next.transpose(1, 2, 0),
    )
    next_flat, kept, kept_edges = pl.pallas_call(
        finish,
        name="finish",
        out_shape=outputs,
        in_specs=[anywhere] * 3,
        out_specs=(anywhere,) * 3,
        scratch_shapes=[
            *[pltpu.VMEM(output.shape, output.dtype) for output in outputs],
            dma((PIECES + 2,)), dma((PIECES + 2,)),
        ],
        compiler_params=pltpu.CompilerParams(vmem_limit_bytes=56 * 2**20),
    )(*results)
    return next_flat.transpose(2, 0, 1), kept, kept_edges.transpose(1, 0, 2)


def solution(mesh):
    in_specs = (
        P("grp", None),
        P("grp", None, "req"),
        P(),
        P(None, "req"),
        P("grp", None, "req"),
        P("grp", "req", None),
        P("grp"),
        P(),
        P("req"),
        P("req", None),
        P(),
        P(None, "req"),
        P(None, "req"),
        P("req", None),
        P(),
        P(None, None, "req"),
    )
    out_specs = (P("grp", None, "req"), P("grp", "req", None), P("grp", None, "req"))
    return jax.shard_map(
        per_device, mesh=mesh, in_specs=in_specs, out_specs=out_specs, check_vma=False
    )
```

```python
import jax
import jax.numpy as jnp
from jax import lax
from jax.experimental import pallas as pl
from jax.experimental.pallas import tpu as pltpu
from jax.sharding import PartitionSpec as P

EPSILON = 1e-06
MESH = pl.DeviceIdType.MESH
F32 = jnp.float32
BF16 = jnp.bfloat16

SIDE = 4
CHIPS = SIDE * SIDE
GROUPS = 4
STEPS = 16
TAPS = 4
EDGES = 3
WIDTH = 2048
HALF = 64
KEYS = 128
EXTRA = 128
REQUESTS = 32
TOKENS = REQUESTS * STEPS
MINE = TOKENS // 2
TILE = 128
TILE_REQ = TILE // STEPS
CHUNKS = 2
PART = MINE // CHUNKS
ROWS = PART // CHIPS
FOLD = WIDTH // 2
LANES = FOLD // 2

NT = (((1,), (1,)), ((), ()))
TN = (((0,), (0,)), ((), ()))


def dot(left, right, dims=(((1,), (0,)), ((), ()))):
    return lax.dot_general(left, right, dims, preferred_element_type=F32)


def iota(shape, dim):
    return lax.broadcasted_iota(jnp.int32, shape, dim)


def to_column(row):
    size = row.shape[1]
    square = jnp.broadcast_to(row, (size, size))
    diagonal = iota((size, size), 0) == iota((size, size), 1)
    return jnp.sum(jnp.where(diagonal, square, jnp.zeros_like(square)), axis=1, keepdims=True)


def kernel(
    residual, mixer, floor_in, taps_in, edges_in, state, accepted_in, home_in, gain_mixer_in,
    w_out, gain_mlp_in, w_gate, w_up, w_down, gain_next_in, w_next,
    next_out, kept_home, edge_out,
    floor, taps, edges, accepted, home, gain_mixer, gain_mlp, gain_next, kept_out, mix_v, pair, state_v, res_v, wo, wgu, wd, wn,
    query_b, key_b, decay, values, picked, gained_own, gained_send, gained_recv,
    send1a, send1b, early1a, early1b, middle1a, middle1b, late1a, late1b, gather1a, gather1b, first_v,
    send2a, send2b, early2a, early2b, middle2a, middle2b, late2a, late2b, gather2a, gather2b,
    next_send, next_recv, kept_v, edge_v, kept_all, edge_all,
    load_sem, small_sem, pair_ss, pair_rs, ss1, rs1, ss2, rs2, ss_x, rs_x,
):
    member = lax.axis_index("req")
    group = lax.axis_index("grp")
    core = member % 2
    chip = member // 2
    at_y = chip // SIDE
    at_z = chip % SIDE
    sibling = {"req": chip * 2 + (1 - core), "grp": group}

    def along(axis, k):
        if axis == 0:
            chip_at = (at_y + k) % SIDE * SIDE + at_z
        else:
            chip_at = at_y * SIDE + (at_z + k) % SIDE
        return {"req": chip_at * 2 + core, "grp": group}

    def across(k):
        return {"req": member, "grp": (group + k) % GROUPS}

    barrier = pltpu.get_barrier_semaphore()

    pl.semaphore_signal(barrier, inc=1, device_id=sibling, device_id_type=MESH)
    for axis in range(2):
        for k in range(1, SIDE):
            pl.semaphore_signal(barrier, inc=1, device_id=along(axis, k), device_id_type=MESH)
    for k in range(1, GROUPS):
        pl.semaphore_signal(barrier, inc=1, device_id=across(k), device_id_type=MESH)

    loads = [
        pltpu.make_async_copy(mixer, mix_v, load_sem.at[0]),
        pltpu.make_async_copy(state, state_v, load_sem.at[1]),
        pltpu.make_async_copy(w_out, wo.at[core], load_sem.at[2]),
        pltpu.make_async_copy(w_gate, wgu.at[0, core], load_sem.at[4]),
        pltpu.make_async_copy(w_up, wgu.at[1, core], load_sem.at[5]),
        pltpu.make_async_copy(w_down, wd.at[core], load_sem.at[6]),
        pltpu.make_async_copy(w_next, wn.at[core], load_sem.at[7]),
    ]
    for c in range(CHUNKS):
        near = core * MINE + c * PART + chip // 2 * (2 * ROWS)
        loads.append(pltpu.make_async_copy(
            residual.at[pl.ds(pl.multiple_of(near, 2 * ROWS), 2 * ROWS)], res_v.at[c], load_sem.at[8 + c]))
    smalls = [
        pltpu.make_async_copy(source, target, small_sem.at[i])
        for i, (source, target) in enumerate((
            (taps_in, taps), (edges_in, edges), (floor_in, floor), (gain_mixer_in, gain_mixer),
            (accepted_in, accepted), (home_in, home), (gain_mlp_in, gain_mlp), (gain_next_in, gain_next)))
    ]
    for load in loads[:1] + smalls + loads[1:]:
        load.start()

    def to_sibling(source, target, slot):
        return pltpu.make_async_remote_copy(
            src_ref=source, dst_ref=target, send_sem=pair_ss.at[slot], recv_sem=pair_rs.at[slot],
            device_id=sibling, device_id_type=MESH)

    pl.semaphore_wait(barrier, 1 + 2 * (SIDE - 1) + GROUPS - 1)
    halves = to_sibling(mixer.at[0:2], pair.at[:, core], 0)
    halves.start()
    shared = [
        to_sibling(w_out, wo.at[core], 1),
        to_sibling(w_gate, wgu.at[0, core], 2),
        to_sibling(w_up, wgu.at[1, core], 3),
        to_sibling(w_down, wd.at[core], 4),
        to_sibling(w_next, wn.at[core], 5),
    ]
    for copy in shared:
        copy.start()

    for load in smalls + loads[:1]:
        load.wait()
    lane = iota((1, TOKENS), 1)
    step_of = lane % STEPS
    inputs_raw = mix_v[2]
    inputs_f = inputs_raw.astype(F32)
    stacked = jnp.concatenate([edges[i] for i in range(EDGES)], axis=0)
    row96 = iota((EDGES * REQUESTS, TOKENS), 0)
    lane96 = iota((EDGES * REQUESTS, TOKENS), 1)
    conv = to_column(taps[TAPS - 1:TAPS, :]) * inputs_f
    for j in range(TAPS - 1):
        shift = TAPS - 1 - j
        early = row96 // REQUESTS - j
        place = (early >= 0) & (lane96 == (row96 % REQUESTS) * STEPS + early)
        from_edges = dot(stacked, jnp.where(place, 1.0, 0.0).astype(BF16), TN)
        moved = jnp.where(step_of >= shift, pltpu.roll(inputs_f, shift, axis=1), 0.0)
        conv = conv + to_column(taps[j:j + 1, :]) * (moved + from_edges)
    values[...] = conv.astype(BF16)

    pair[:, core] = mix_v[0:2]
    floor_row = floor[pl.ds(chip, 1), :]
    low = to_column(floor_row)
    gain_column = to_column(gain_mixer[...])
    halves.wait()
    loads[1].wait()

    def gates(tile):
        at = slice(tile * TILE, (tile + 1) * TILE)
        step_t = iota((KEYS, TILE), 1) % STEPS
        q_pre = pair[0, :, :, at].reshape(KEYS, TILE).astype(F32)
        f_pre = pair[1, :, :, at].reshape(KEYS, TILE).astype(F32)
        query = q_pre * jax.nn.sigmoid(q_pre)
        forget = low + (1.0 - low) * jax.nn.sigmoid(f_pre)
        keyed = 1.0 - forget
        run = forget
        for shift in (1, 2, 4, 8):
            run = jnp.where(step_t >= shift, run * pltpu.roll(run, shift, axis=1), run)
        decay[:, at] = run
        query_b[:, at] = (query * run).astype(BF16)
        key_b[:, at] = (keyed / run).astype(BF16)

    def recurrence(tile):
        at = slice(tile * TILE, (tile + 1) * TILE)
        q_t = query_b[:, at]
        begin = state_v[tile * TILE_REQ:(tile + 1) * TILE_REQ].astype(BF16).reshape(TILE_REQ * HALF, KEYS)
        through = dot(begin, q_t).reshape(TILE_REQ, HALF, TILE)
        ours = iota((TILE_REQ, HALF, TILE), 0) == iota((TILE_REQ, HALF, TILE), 2) // STEPS
        total = jnp.sum(jnp.where(ours, through, 0.0), axis=0)
        scores = dot(key_b[:, at], q_t, TN)
        source = iota((TILE, TILE), 0)
        sink = iota((TILE, TILE), 1)
        causal = (source // STEPS == sink // STEPS) & (source <= sink)
        scores = jnp.where(causal, scores, 0.0).astype(BF16)
        total = (total + dot(values[:, at], scores)) * KEYS ** (-0.5)
        gained_own[0:HALF, at] = (total * gain_column).astype(BF16)
        square = jnp.sum(total * total, axis=0, keepdims=True)
        gained_own[HALF:HALF + STEPS, at] = jnp.broadcast_to(square, (STEPS, TILE)).astype(BF16)

    gained_swaps = []
    for c in range(CHUNKS):
        for tile in (c, CHUNKS + c):
            gates(tile)
            recurrence(tile)
        other_lanes = pl.ds(pl.multiple_of((1 - core) * MINE + c * PART, PART), PART)
        gained_send[c] = gained_own[:, other_lanes]
        gained_swaps.append(to_sibling(gained_send.at[c], gained_recv.at[c], 6 + c))
        gained_swaps[c].start()
    pick_one = jnp.where(iota((2 * STEPS, EXTRA), 0) % STEPS == 0, 1.0, 0.0).astype(BF16)

    def folded(low_part, high_part):
        width = low_part.shape[1]
        return jnp.concatenate(
            [low_part.reshape(CHIPS, ROWS, width), high_part.reshape(CHIPS, ROWS, width)], axis=1
        ).astype(BF16)

    def spot(y, z, axis, absolute):
        if absolute:
            y, z = (y - at_y + SIDE) % SIDE, (z - at_z + SIDE) % SIDE
        return (y, z) if axis == 0 else (z, y)

    def put(blocks, ref, c, axis, absolute):
        width = blocks.shape[2]
        for y in range(SIDE):
            for z in range(SIDE):
                i, j = spot(y, z, axis, absolute)
                ref[c, i, j, :, 0:width] = blocks[y * SIDE + z]

    def link(source, target, ssem, rsem, c, axis, stage, k, towards):
        return pltpu.make_async_remote_copy(
            src_ref=source, dst_ref=target, send_sem=ssem.at[c, axis, stage],
            recv_sem=rsem.at[c, axis, stage], device_id=along(towards, k), device_id_type=MESH)

    far = slice(1, SIDE)

    def wait_for(region, sem):
        pltpu.make_async_copy(region, region, sem).wait()


    class Sum:
        def __init__(self, sends, early, middle, late, sems, squares):
            self.sends, self.early, self.middle, self.late, self.sems = sends, early, middle, late, sems
            self.squares = squares

        def lanes(self, c, axis):
            return slice(0, LANES + EXTRA if self.squares and axis == c % 2 else LANES)

        def first(self, c, axis):
            return [
                link(self.sends[axis].at[c, k, far, :, self.lanes(c, axis)], self.early[axis].at[c, k, far, :, self.lanes(c, axis)],
                     *self.sems, c, axis, 0, k, axis)
                for k in range(1, SIDE)
            ]

        def near(self, c, axis):
            return [
                link(self.sends[axis].at[c, k, 0, :, self.lanes(c, axis)], self.early[axis].at[c, k, 0, :, self.lanes(c, axis)],
                     *self.sems, c, axis, 2, k, axis)
                for k in range(1, SIDE)
            ]

        def second(self, c, axis):
            return [
                link(self.middle[axis].at[c, k, :, self.lanes(c, axis)], self.late[axis].at[c, k, :, self.lanes(c, axis)],
                     *self.sems, c, axis, 1, k, 1 - axis)
                for k in range(1, SIDE)
            ]

        def begin(self, c, axis):
            for copy in self.first(c, axis):
                copy.start()

        def turn(self, c, axis):
            wait_for(self.early[axis].at[c, far, far, :, self.lanes(c, axis)], self.sems[1].at[c, axis, 0])
            sums = self.sends[axis][c, 0, far, :, self.lanes(c, axis)].astype(F32)
            for k in range(1, SIDE):
                sums = sums + self.early[axis][c, k, far, :, self.lanes(c, axis)].astype(F32)
            self.middle[axis][c, far, :, self.lanes(c, axis)] = sums.astype(BF16)
            for copy in self.second(c, axis) + self.near(c, axis):
                copy.start()

        def end(self, c, axis):
            wait_for(self.late[axis].at[c, far, :, self.lanes(c, axis)], self.sems[1].at[c, axis, 1])
            wait_for(self.early[axis].at[c, far, 0, :, self.lanes(c, axis)], self.sems[1].at[c, axis, 2])
            sums = self.sends[axis][c, 0, 0, :, self.lanes(c, axis)].astype(F32)
            for k in range(1, SIDE):
                sums = sums + self.early[axis][c, k, 0, :, self.lanes(c, axis)].astype(F32)
                sums = sums + self.late[axis][c, k, :, self.lanes(c, axis)].astype(F32)
            return sums

        def drain(self, c, axis):
            wait_for(self.sends[axis].at[c, far, far, :, self.lanes(c, axis)], self.sems[0].at[c, axis, 0])
            wait_for(self.middle[axis].at[c, far, :, self.lanes(c, axis)], self.sems[0].at[c, axis, 1])
            wait_for(self.sends[axis].at[c, far, 0, :, self.lanes(c, axis)], self.sems[0].at[c, axis, 2])

    class Gather:
        def __init__(self, refs, sems):
            self.refs, self.sems = refs, sems

        def first(self, c, axis):
            ref = self.refs[axis]
            return [
                link(ref.at[c, 0, 0], ref.at[c, 0, SIDE - k], *self.sems, c, axis, 0, k, 1 - axis)
                for k in range(1, SIDE)
            ]

        def near(self, c, axis):
            ref = self.refs[axis]
            return [
                link(ref.at[c, 0, 0], ref.at[c, SIDE - k, 0], *self.sems, c, axis, 2, k, axis)
                for k in range(1, SIDE)
            ]

        def second(self, c, axis):
            ref = self.refs[axis]
            return [
                link(ref.at[c, 0, far], ref.at[c, SIDE - k, far], *self.sems, c, axis, 1, k, axis)
                for k in range(1, SIDE)
            ]

        def begin(self, c, rows):
            block = jnp.concatenate([rows[:, 0:FOLD], rows[:, FOLD:]], axis=0).astype(BF16)
            for axis in range(2):
                self.refs[axis][c, 0, 0] = block[:, axis * LANES:(axis + 1) * LANES]
                for copy in self.first(c, axis):
                    copy.start()
            for axis in range(2):
                for copy in self.near(c, axis):
                    copy.start()

        def turn(self, c):
            for axis in range(2):
                wait_for(self.refs[axis].at[c, 0, far], self.sems[1].at[c, axis, 0])
                for copy in self.second(c, axis):
                    copy.start()

        def end(self, c, absolute):
            for axis in range(2):
                wait_for(self.refs[axis].at[c, far, far], self.sems[1].at[c, axis, 1])
                wait_for(self.refs[axis].at[c, far, 0], self.sems[1].at[c, axis, 2])
            rows = [[], []]
            for axis in range(2):
                blocks = []
                for y in range(SIDE):
                    for z in range(SIDE):
                        i, j = spot(y, z, axis, absolute)
                        blocks.append(self.refs[axis][c, i, j].astype(F32))
                rows[0].append(jnp.concatenate([block[0:ROWS] for block in blocks], axis=0))
                rows[1].append(jnp.concatenate([block[ROWS:] for block in blocks], axis=0))
            return jnp.concatenate(rows[0] + rows[1], axis=1).astype(BF16)

        def drain(self, c):
            for axis in range(2):
                wait_for(self.refs[axis].at[c, 0, far], self.sems[0].at[c, axis, 0])
                wait_for(self.refs[axis].at[c, far, far], self.sems[0].at[c, axis, 1])
                wait_for(self.refs[axis].at[c, far, 0], self.sems[0].at[c, axis, 2])

    def unfold(left, right):
        return jnp.concatenate([left[0:ROWS], right[0:ROWS], left[ROWS:], right[ROWS:]], axis=1)

    sum1 = Sum((send1a, send1b), (early1a, early1b), (middle1a, middle1b), (late1a, late1b), (ss1, rs1), True)
    spread1 = Gather((gather1a, gather1b), (ss2, rs2))
    sum2 = Sum((send2a, send2b), (early2a, early2b), (middle2a, middle2b), (late2a, late2b), (ss1, rs1), False)
    spread2 = Gather((gather2a, gather2b), (ss2, rs2))

    loads[2].wait()
    shared[0].wait()
    for c in range(CHUNKS):
        own_lanes = pl.ds(pl.multiple_of(core * MINE + c * PART, PART), PART)
        mine = gained_own[:, own_lanes]
        gained_swaps[c].wait()
        theirs = gained_recv[c]
        lower = jnp.where(core == 0, mine[0:HALF], theirs[0:HALF])
        upper = jnp.where(core == 0, theirs[0:HALF], mine[0:HALF])
        channels = jnp.concatenate([lower, upper], axis=0).T
        squares2 = jnp.concatenate([mine[HALF:], theirs[HALF:]], axis=0)
        square = dot(squares2, pick_one, TN)
        square = folded(square, square)
        for axis in range(2):
            low_at = slice(axis * LANES, (axis + 1) * LANES)
            high_at = slice(FOLD + axis * LANES, FOLD + (axis + 1) * LANES)
            terms = folded(
                dot(channels, wo[:, :, low_at].reshape(2 * HALF, LANES)),
                dot(channels, wo[:, :, high_at].reshape(2 * HALF, LANES)))
            if axis == c % 2:
                terms = jnp.concatenate([terms, square], axis=2)
            put(terms, sum1.sends[axis], c, axis, True)
            sum1.begin(c, axis)

    acc_column = to_column(accepted[...])
    row32 = iota((REQUESTS, TOKENS), 0)
    lane32 = iota((REQUESTS, TOKENS), 1)
    acc_lanes = jnp.sum(jnp.where(lane32 // STEPS == row32, acc_column, 0), axis=0, keepdims=True)
    last = jnp.where(lane32 == row32 * STEPS + acc_column - 1, 1.0, 0.0)
    last = jnp.where(acc_column > 0, last, 0.0).astype(BF16)
    run_all = decay[...]
    run_high = run_all.astype(BF16)
    run_low = (run_all - run_high.astype(F32)).astype(BF16)
    run_picked = dot(last, run_high, NT) + dot(last, run_low, NT)
    picked[...] = jnp.where(acc_column == 0, 1.0, run_picked)
    live = step_of < acc_lanes
    for tile in range(TOKENS // TILE):
        at = slice(tile * TILE, (tile + 1) * TILE)
        taken = jnp.where(live[:, at], values[:, at].astype(F32), 0.0)
        spread = jnp.broadcast_to(taken[None], (TILE_REQ, HALF, TILE))
        ours = iota((TILE_REQ, HALF, TILE), 0) == iota((TILE_REQ, HALF, TILE), 2) // STEPS
        spread = jnp.where(ours, spread, 0.0).astype(BF16).reshape(TILE_REQ * HALF, TILE)
        added = dot(spread, key_b[:, at], NT)
        for i in range(TILE_REQ):
            r = tile * TILE_REQ + i
            kept_v[r] = (picked[r:r + 1, :] * (state_v[r] + added[i * HALF:(i + 1) * HALF])).astype(BF16)
    for e in range(EDGES):
        place = jnp.where(lane32 == row32 * STEPS + acc_column + (e - EDGES), 1.0, 0.0)
        place = jnp.where(acc_column + e >= EDGES, place, 0.0).astype(BF16)
        kept_edge = dot(place, inputs_raw, NT)
        for i in range(EDGES):
            kept_edge = kept_edge + jnp.where(acc_column + e == i, edges[i].astype(F32), 0.0)
        edge_v[e] = kept_edge.astype(BF16)

    def cross(k):
        return [
            pltpu.make_async_remote_copy(
                src_ref=source, dst_ref=target.at[group], send_sem=ss_x.at[slot, k - 1],
                recv_sem=rs_x.at[slot, k - 1], device_id=across(k), device_id_type=MESH)
            for slot, (source, target) in enumerate(((kept_v, kept_all), (edge_v, edge_all)))
        ]

    crossing = [copy for k in range(1, GROUPS) for copy in cross(k)]
    for copy in crossing:
        copy.start()
    kept_all[group] = kept_v[...]
    edge_all[group] = edge_v[...]

    def scaled_norm(rows, gain):
        factor = lax.rsqrt(jnp.mean(rows * rows, axis=1, keepdims=True) + EPSILON)
        return rows * factor * gain

    for c in range(CHUNKS):
        for axis in range(2):
            sum1.turn(c, axis)
    for load in loads[3:]:
        load.wait()
    for c in range(CHUNKS):
        left = sum1.end(c, 0)
        right = sum1.end(c, 1)
        near = res_v[c].astype(F32)
        before = jnp.where(chip % 2 == 0, near[0:ROWS], near[ROWS:])
        square = (left if c % 2 == 0 else right)[0:ROWS, LANES:LANES + 1]
        attn = unfold(left[:, 0:LANES], right[:, 0:LANES]) * lax.rsqrt(square / WIDTH + EPSILON)
        first = (before + attn).astype(BF16).astype(F32)
        first_v[c] = first
        spread1.begin(c, scaled_norm(first, gain_mlp[...]))
    for c in range(CHUNKS):
        spread1.turn(c)
    for c in range(CHUNKS):
        for axis in range(2):
            sum1.drain(c, axis)
    for copy in shared[1:]:
        copy.wait()

    hidden_width = wd.shape[0] * wd.shape[1]
    for c in range(CHUNKS):
        rows = spread1.end(c, False)
        both_parts = dot(rows, wgu[...].reshape(2 * hidden_width, WIDTH), NT)
        gate = both_parts[:, 0:hidden_width]
        hidden = (gate * jax.nn.sigmoid(gate) * both_parts[:, hidden_width:]).astype(BF16)
        for axis in range(2):
            low_at = slice(axis * LANES, (axis + 1) * LANES)
            high_at = slice(FOLD + axis * LANES, FOLD + (axis + 1) * LANES)
            put(folded(
                dot(hidden, wd[:, :, low_at].reshape(hidden_width, LANES)),
                dot(hidden, wd[:, :, high_at].reshape(hidden_width, LANES)),
            ), sum2.sends[axis], c, axis, False)
            sum2.begin(c, axis)
    for c in range(CHUNKS):
        spread1.drain(c)

    for c in range(CHUNKS):
        for axis in range(2):
            sum2.turn(c, axis)
    for c in range(CHUNKS):
        down = unfold(sum2.end(c, 0), sum2.end(c, 1))
        second = (first_v[c] + down).astype(BF16).astype(F32)
        spread2.begin(c, scaled_norm(second, gain_next[...]))
    for c in range(CHUNKS):
        spread2.turn(c)

    for copy in crossing:
        copy.wait()
    home_row = home[...]
    source_lane = iota((1, GROUPS * REQUESTS), 1)
    for i in range(REQUESTS):
        found = jnp.max(jnp.where(home_row == group * REQUESTS + i, source_lane, 0))
        kept_out[i] = kept_all[found // REQUESTS, found % REQUESTS].astype(F32)
    leaving = pltpu.make_async_copy(kept_out, kept_home, load_sem.at[8 + CHUNKS])
    leaving.start()
    target_row = iota((REQUESTS, GROUPS * REQUESTS), 0) + group * REQUESTS
    chosen = jnp.where(home_row == target_row, 1.0, 0.0).astype(BF16)
    for e in range(EDGES):
        pool = edge_all[:, e].reshape(GROUPS * REQUESTS, HALF)
        edge_out[e] = dot(chosen, pool).astype(BF16)

    for c in range(CHUNKS):
        for axis in range(2):
            sum2.drain(c, axis)

    swaps = []
    for c in range(CHUNKS):
        normed = spread2.end(c, True)
        theirs_next = dot(wn[1 - core].reshape(3 * HALF, WIDTH), normed, NT)
        next_send[c] = theirs_next.astype(BF16).reshape(3, HALF, PART)
        swaps.append(to_sibling(next_send.at[c], next_recv.at[c], 6 + CHUNKS + c))
        swaps[c].start()
        own_next = dot(wn[core].reshape(3 * HALF, WIDTH), normed, NT)
        here = pl.ds(pl.multiple_of(core * MINE + c * PART, PART), PART)
        next_out[:, :, here] = own_next.astype(BF16).reshape(3, HALF, PART)
    for c in range(CHUNKS):
        spread2.drain(c)
        swaps[c].wait()
        there = pl.ds(pl.multiple_of((1 - core) * MINE + c * PART, PART), PART)
        next_out[:, :, there] = next_recv[c]
    leaving.wait()


PIECES = 4
PIECE = REQUESTS // PIECES


def finish(next_in, kept_in, edge_in, next_out, kept_out, edge_out, next_v, kept_v, edge_v, in_sems, out_sems):
    parts = [slice(i * PIECE, (i + 1) * PIECE) for i in range(PIECES)]
    routes = [(kept_in.at[part], kept_v.at[part], kept_out.at[part]) for part in parts]
    routes += [(next_in, next_v, next_out), (edge_in, edge_v, edge_out)]
    arrive = [pltpu.make_async_copy(a, b, in_sems.at[i]) for i, (a, b, _) in enumerate(routes)]
    leave = [pltpu.make_async_copy(b, c, out_sems.at[i]) for i, (_, b, c) in enumerate(routes)]
    for copy in arrive:
        copy.start()
    for copy, further in zip(arrive, leave):
        copy.wait()
        further.start()
    for copy in leave:
        copy.wait()


def sum_buffers(width):
    grids = [(SIDE, SIDE), (SIDE, SIDE), (SIDE,), (SIDE,)]
    return [pltpu.VMEM((CHUNKS, *grid, 2 * ROWS, width), BF16) for grid in grids for _ in range(2)]


def gather_buffers():
    return [pltpu.VMEM((CHUNKS, SIDE, SIDE, 2 * ROWS, LANES), BF16)] * 2


def per_device(
    residual_in, mixer_in, forget_floor, conv_weight, conv_edges, state_in, accepted, home_slot,
    gain_mixer, w_out, gain_mlp, w_gate, w_up, w_down, gain_next, w_next,
):
    hidden_width = w_gate.shape[1]
    anywhere = pl.BlockSpec(memory_space=pl.ANY)
    vmem = pl.BlockSpec(memory_space=pltpu.VMEM)
    dma = pltpu.SemaphoreType.DMA
    outputs = (
        jax.ShapeDtypeStruct((3, HALF, TOKENS), BF16),
        jax.ShapeDtypeStruct((REQUESTS, HALF, KEYS), F32),
        jax.ShapeDtypeStruct((EDGES, REQUESTS, HALF), BF16),
    )
    results = pl.pallas_call(
        kernel,
        name="draft_check",
        out_shape=outputs,
        in_specs=[anywhere] * 16,
        out_specs=(vmem, anywhere, vmem),
        scratch_shapes=[
            pltpu.VMEM((CHIPS, KEYS), F32),
            pltpu.VMEM((TAPS, HALF), F32),
            pltpu.VMEM((EDGES, REQUESTS, HALF), BF16),
            pltpu.VMEM((1, REQUESTS), jnp.int32),
            pltpu.VMEM((1, GROUPS * REQUESTS), jnp.int32),
            pltpu.VMEM((1, HALF), F32),
            pltpu.VMEM((1, WIDTH), F32),
            pltpu.VMEM((1, WIDTH), F32),
            pltpu.VMEM((REQUESTS, HALF, KEYS), F32),
            pltpu.VMEM((3, HALF, TOKENS), BF16),
            pltpu.VMEM((2, 2, HALF, TOKENS), BF16),
            pltpu.VMEM((REQUESTS, HALF, KEYS), F32),
            pltpu.VMEM((CHUNKS, 2 * ROWS, WIDTH), BF16),
            pltpu.VMEM((2, HALF, WIDTH), BF16),
            pltpu.VMEM((2, 2, hidden_width, WIDTH), BF16),
            pltpu.VMEM((2, hidden_width, WIDTH), BF16),
            pltpu.VMEM((2, 3, HALF, WIDTH), BF16),
            pltpu.VMEM((KEYS, TOKENS), BF16),
            pltpu.VMEM((KEYS, TOKENS), BF16),
            pltpu.VMEM((KEYS, TOKENS), F32),
            pltpu.VMEM((HALF, TOKENS), BF16),
            pltpu.VMEM((REQUESTS, KEYS), F32),
            pltpu.VMEM((HALF + STEPS, TOKENS), BF16),
            pltpu.VMEM((CHUNKS, HALF + STEPS, PART), BF16),
            pltpu.VMEM((CHUNKS, HALF + STEPS, PART), BF16),
            *sum_buffers(LANES + EXTRA), *gather_buffers(),
            pltpu.VMEM((CHUNKS, ROWS, WIDTH), F32),
            *sum_buffers(LANES), *gather_buffers(),
            pltpu.VMEM((CHUNKS, 3, HALF, PART), BF16),
            pltpu.VMEM((CHUNKS, 3, HALF, PART), BF16),
            pltpu.VMEM((REQUESTS, HALF, KEYS), BF16),
            pltpu.VMEM((EDGES, REQUESTS, HALF), BF16),
            pltpu.VMEM((GROUPS, REQUESTS, HALF, KEYS), BF16),
            pltpu.VMEM((GROUPS, EDGES, REQUESTS, HALF), BF16),
            dma((9 + CHUNKS,)), dma((8,)), dma((6 + 2 * CHUNKS,)), dma((6 + 2 * CHUNKS,)),
            *[dma((CHUNKS, 2, 3))] * 4,
            dma((2, GROUPS - 1)), dma((2, GROUPS - 1)),
        ],
        compiler_params=pltpu.CompilerParams(
            collective_id=0, has_side_effects=True, vmem_limit_bytes=56 * 2**20),
    )(
        residual_in,
        mixer_in.transpose(1, 2, 0),
        forget_floor.reshape(-1, KEYS),
        conv_weight,
        conv_edges.transpose(1, 0, 2),
        state_in,
        accepted.reshape(1, -1),
        home_slot.reshape(1, -1),
        gain_mixer.reshape(1, -1),
        w_out,
        gain_mlp.reshape(1, -1),
        w_gate.T,
        w_up.T,
        w_down,
        gain_next.reshape(1, -1),
        w_next.transpose(1, 2, 0),
    )
    next_flat, kept, kept_edges = pl.pallas_call(
        finish,
        name="finish",
        out_shape=outputs,
        in_specs=[anywhere] * 3,
        out_specs=(anywhere,) * 3,
        scratch_shapes=[
            *[pltpu.VMEM(output.shape, output.dtype) for output in outputs],
            dma((PIECES + 2,)), dma((PIECES + 2,)),
        ],
        compiler_params=pltpu.CompilerParams(vmem_limit_bytes=56 * 2**20),
    )(*results)
    return next_flat.transpose(2, 0, 1), kept, kept_edges.transpose(1, 0, 2)


def solution(mesh):
    in_specs = (
        P("grp", None),
        P("grp", None, "req"),
        P(),
        P(None, "req"),
        P("grp", None, "req"),
        P("grp", "req", None),
        P("grp"),
        P(),
        P("req"),
        P("req", None),
        P(),
        P(None, "req"),
        P(None, "req"),
        P("req", None),
        P(),
        P(None, None, "req"),
    )
    out_specs = (P("grp", None, "req"), P("grp", "req", None), P("grp", None, "req"))
    return jax.shard_map(
        per_device, mesh=mesh, in_specs=in_specs, out_specs=out_specs, check_vma=False
    )
```

```python
import jax
import jax.numpy as jnp
from jax import lax
from jax.experimental import pallas as pl
from jax.experimental.pallas import tpu as pltpu
from jax.sharding import PartitionSpec as P

EPSILON = 1e-06
MESH = pl.DeviceIdType.MESH
F32 = jnp.float32
BF16 = jnp.bfloat16

SIDE = 4
CHIPS = SIDE * SIDE
GROUPS = 4
STEPS = 16
TAPS = 4
EDGES = 3
WIDTH = 2048
HALF = 64
KEYS = 128
EXTRA = 128
REQUESTS = 32
TOKENS = REQUESTS * STEPS
MINE = TOKENS // 2
TILE = 128
TILE_REQ = TILE // STEPS
CHUNKS = 2
PART = MINE // CHUNKS
ROWS = PART // CHIPS
FOLD = WIDTH // 2
LANES = FOLD // 2

NT = (((1,), (1,)), ((), ()))
TN = (((0,), (0,)), ((), ()))


def dot(left, right, dims=(((1,), (0,)), ((), ()))):
    return lax.dot_general(left, right, dims, preferred_element_type=F32)


def iota(shape, dim):
    return lax.broadcasted_iota(jnp.int32, shape, dim)


def to_column(row):
    size = row.shape[1]
    square = jnp.broadcast_to(row, (size, size))
    diagonal = iota((size, size), 0) == iota((size, size), 1)
    return jnp.sum(jnp.where(diagonal, square, jnp.zeros_like(square)), axis=1, keepdims=True)


def kernel(
    residual, mixer, floor_in, taps_in, edges_in, state, accepted_in, home_in, gain_mixer_in,
    w_out, gain_mlp_in, w_gate, w_up, w_down, gain_next_in, w_next,
    next_out, kept_home, edge_out,
    floor, taps, edges, accepted, home, gain_mixer, gain_mlp, gain_next, kept_out, mix_v, pair, state_v, res_v, wo, wgu, wd, wn,
    query_b, key_b, decay, values, picked, gained_own, gained_send, gained_recv,
    send1a, send1b, early1a, early1b, middle1a, middle1b, late1a, late1b, gather1a, gather1b, first_v,
    send2a, send2b, early2a, early2b, middle2a, middle2b, late2a, late2b, gather2a, gather2b,
    next_send, next_recv, kept_v, edge_v, kept_all, edge_all,
    load_sem, small_sem, pair_ss, pair_rs, ss1, rs1, ss2, rs2, ss_x, rs_x,
):
    member = lax.axis_index("req")
    group = lax.axis_index("grp")
    core = member % 2
    chip = member // 2
    at_y = chip // SIDE
    at_z = chip % SIDE
    sibling = {"req": chip * 2 + (1 - core), "grp": group}

    def along(axis, k):
        if axis == 0:
            chip_at = (at_y + k) % SIDE * SIDE + at_z
        else:
            chip_at = at_y * SIDE + (at_z + k) % SIDE
        return {"req": chip_at * 2 + core, "grp": group}

    def across(k):
        return {"req": member, "grp": (group + k) % GROUPS}

    barrier = pltpu.get_barrier_semaphore()

    pl.semaphore_signal(barrier, inc=1, device_id=sibling, device_id_type=MESH)
    for axis in range(2):
        for k in range(1, SIDE):
            pl.semaphore_signal(barrier, inc=1, device_id=along(axis, k), device_id_type=MESH)
    for k in range(1, GROUPS):
        pl.semaphore_signal(barrier, inc=1, device_id=across(k), device_id_type=MESH)

    loads = [
        pltpu.make_async_copy(mixer, mix_v, load_sem.at[0]),
        pltpu.make_async_copy(state, state_v, load_sem.at[1]),
        pltpu.make_async_copy(w_out, wo.at[core], load_sem.at[2]),
        pltpu.make_async_copy(w_gate, wgu.at[0, core], load_sem.at[4]),
        pltpu.make_async_copy(w_up, wgu.at[1, core], load_sem.at[5]),
        pltpu.make_async_copy(w_down, wd.at[core], load_sem.at[6]),
        pltpu.make_async_copy(w_next, wn.at[core], load_sem.at[7]),
    ]
    for c in range(CHUNKS):
        near = core * MINE + c * PART + chip // 2 * (2 * ROWS)
        loads.append(pltpu.make_async_copy(
            residual.at[pl.ds(pl.multiple_of(near, 2 * ROWS), 2 * ROWS)], res_v.at[c], load_sem.at[8 + c]))
    smalls = [
        pltpu.make_async_copy(source, target, small_sem.at[i])
        for i, (source, target) in enumerate((
            (taps_in, taps), (edges_in, edges), (floor_in, floor), (gain_mixer_in, gain_mixer),
            (accepted_in, accepted), (home_in, home), (gain_mlp_in, gain_mlp), (gain_next_in, gain_next)))
    ]
    for load in loads[:1] + smalls + loads[1:]:
        load.start()

    def to_sibling(source, target, slot):
        return pltpu.make_async_remote_copy(
            src_ref=source, dst_ref=target, send_sem=pair_ss.at[slot], recv_sem=pair_rs.at[slot],
            device_id=sibling, device_id_type=MESH)

    pl.semaphore_wait(barrier, 1 + 2 * (SIDE - 1) + GROUPS - 1)
    halves = to_sibling(mixer.at[0:2], pair.at[:, core], 0)
    halves.start()
    shared = [
        to_sibling(w_out, wo.at[core], 1),
        to_sibling(w_gate, wgu.at[0, core], 2),
        to_sibling(w_up, wgu.at[1, core], 3),
        to_sibling(w_down, wd.at[core], 4),
        to_sibling(w_next, wn.at[core], 5),
    ]
    for copy in shared:
        copy.start()

    for load in smalls + loads[:1]:
        load.wait()
    lane = iota((1, TOKENS), 1)
    step_of = lane % STEPS
    inputs_raw = mix_v[2]
    inputs_f = inputs_raw.astype(F32)
    stacked = jnp.concatenate([edges[i] for i in range(EDGES)], axis=0)
    row96 = iota((EDGES * REQUESTS, TOKENS), 0)
    lane96 = iota((EDGES * REQUESTS, TOKENS), 1)
    conv = to_column(taps[TAPS - 1:TAPS, :]) * inputs_f
    for j in range(TAPS - 1):
        shift = TAPS - 1 - j
        early = row96 // REQUESTS - j
        place = (early >= 0) & (lane96 == (row96 % REQUESTS) * STEPS + early)
        from_edges = dot(stacked, jnp.where(place, 1.0, 0.0).astype(BF16), TN)
        moved = jnp.where(step_of >= shift, pltpu.roll(inputs_f, shift, axis=1), 0.0)
        conv = conv + to_column(taps[j:j + 1, :]) * (moved + from_edges)
    values[...] = conv.astype(BF16)

    pair[:, core] = mix_v[0:2]
    floor_row = floor[pl.ds(chip, 1), :]
    low = to_column(floor_row)
    gain_column = to_column(gain_mixer[...])
    halves.wait()
    loads[1].wait()

    def gates(tile):
        at = slice(tile * TILE, (tile + 1) * TILE)
        step_t = iota((KEYS, TILE), 1) % STEPS
        q_pre = pair[0, :, :, at].reshape(KEYS, TILE).astype(F32)
        f_pre = pair[1, :, :, at].reshape(KEYS, TILE).astype(F32)
        query = q_pre * jax.nn.sigmoid(q_pre)
        forget = low + (1.0 - low) * jax.nn.sigmoid(f_pre)
        keyed = 1.0 - forget
        run = forget
        for shift in (1, 2, 4, 8):
            run = jnp.where(step_t >= shift, run * pltpu.roll(run, shift, axis=1), run)
        decay[:, at] = run
        query_b[:, at] = (query * run).astype(BF16)
        key_b[:, at] = (keyed / run).astype(BF16)

    def recurrence(tile):
        at = slice(tile * TILE, (tile + 1) * TILE)
        q_t = query_b[:, at]
        begin = state_v[tile * TILE_REQ:(tile + 1) * TILE_REQ].astype(BF16).reshape(TILE_REQ * HALF, KEYS)
        through = dot(begin, q_t).reshape(TILE_REQ, HALF, TILE)
        ours = iota((TILE_REQ, HALF, TILE), 0) == iota((TILE_REQ, HALF, TILE), 2) // STEPS
        total = jnp.sum(jnp.where(ours, through, 0.0), axis=0)
        scores = dot(key_b[:, at], q_t, TN)
        source = iota((TILE, TILE), 0)
        sink = iota((TILE, TILE), 1)
        causal = (source // STEPS == sink // STEPS) & (source <= sink)
        scores = jnp.where(causal, scores, 0.0).astype(BF16)
        total = (total + dot(values[:, at], scores)) * KEYS ** (-0.5)
        gained_own[0:HALF, at] = (total * gain_column).astype(BF16)
        square = jnp.sum(total * total, axis=0, keepdims=True)
        gained_own[HALF:HALF + STEPS, at] = jnp.broadcast_to(square, (STEPS, TILE)).astype(BF16)

    gained_swaps = []
    for c in range(CHUNKS):
        for tile in (c, CHUNKS + c):
            gates(tile)
            recurrence(tile)
        other_lanes = pl.ds(pl.multiple_of((1 - core) * MINE + c * PART, PART), PART)
        gained_send[c] = gained_own[:, other_lanes]
        gained_swaps.append(to_sibling(gained_send.at[c], gained_recv.at[c], 6 + c))
        gained_swaps[c].start()
    pick_one = jnp.where(iota((2 * STEPS, EXTRA), 0) % STEPS == 0, 1.0, 0.0).astype(BF16)

    def folded(low_part, high_part):
        width = low_part.shape[1]
        return jnp.concatenate(
            [low_part.reshape(CHIPS, ROWS, width), high_part.reshape(CHIPS, ROWS, width)], axis=1
        ).astype(BF16)

    def spot(y, z, axis, absolute):
        if absolute:
            y, z = (y - at_y + SIDE) % SIDE, (z - at_z + SIDE) % SIDE
        return (y, z) if axis == 0 else (z, y)

    def put(blocks, ref, c, axis, absolute):
        width = blocks.shape[2]
        for y in range(SIDE):
            for z in range(SIDE):
                i, j = spot(y, z, axis, absolute)
                ref[c, i, j, :, 0:width] = blocks[y * SIDE + z]

    def link(source, target, ssem, rsem, c, axis, stage, k, towards):
        return pltpu.make_async_remote_copy(
            src_ref=source, dst_ref=target, send_sem=ssem.at[c, axis, stage],
            recv_sem=rsem.at[c, axis, stage], device_id=along(towards, k), device_id_type=MESH)

    far = slice(1, SIDE)
    opposite_first = (2, 1, 3)

    def wait_for(region, sem):
        pltpu.make_async_copy(region, region, sem).wait()


    class Sum:
        def __init__(self, sends, early, middle, late, sems, squares):
            self.sends, self.early, self.middle, self.late, self.sems = sends, early, middle, late, sems
            self.squares = squares

        def lanes(self, c, axis):
            return slice(0, LANES + EXTRA if self.squares and axis == c % 2 else LANES)

        def first(self, c, axis):
            return [
                link(self.sends[axis].at[c, k, far, :, self.lanes(c, axis)], self.early[axis].at[c, k, far, :, self.lanes(c, axis)],
                     *self.sems, c, axis, 0, k, axis)
                for k in opposite_first
            ]

        def near(self, c, axis):
            return [
                link(self.sends[axis].at[c, k, 0, :, self.lanes(c, axis)], self.early[axis].at[c, k, 0, :, self.lanes(c, axis)],
                     *self.sems, c, axis, 2, k, axis)
                for k in opposite_first
            ]

        def second(self, c, axis):
            return [
                link(self.middle[axis].at[c, k, :, self.lanes(c, axis)], self.late[axis].at[c, k, :, self.lanes(c, axis)],
                     *self.sems, c, axis, 1, k, 1 - axis)
                for k in opposite_first
            ]

        def begin(self, c, axis):
            for copy in self.first(c, axis):
                copy.start()

        def turn(self, c, axis):
            wait_for(self.early[axis].at[c, far, far, :, self.lanes(c, axis)], self.sems[1].at[c, axis, 0])
            sums = self.sends[axis][c, 0, far, :, self.lanes(c, axis)].astype(F32)
            for k in range(1, SIDE):
                sums = sums + self.early[axis][c, k, far, :, self.lanes(c, axis)].astype(F32)
            self.middle[axis][c, far, :, self.lanes(c, axis)] = sums.astype(BF16)
            for copy in self.second(c, axis) + self.near(c, axis):
                copy.start()

        def end(self, c, axis):
            wait_for(self.late[axis].at[c, far, :, self.lanes(c, axis)], self.sems[1].at[c, axis, 1])
            wait_for(self.early[axis].at[c, far, 0, :, self.lanes(c, axis)], self.sems[1].at[c, axis, 2])
            sums = self.sends[axis][c, 0, 0, :, self.lanes(c, axis)].astype(F32)
            for k in range(1, SIDE):
                sums = sums + self.early[axis][c, k, 0, :, self.lanes(c, axis)].astype(F32)
                sums = sums + self.late[axis][c, k, :, self.lanes(c, axis)].astype(F32)
            return sums

        def drain(self, c, axis):
            wait_for(self.sends[axis].at[c, far, far, :, self.lanes(c, axis)], self.sems[0].at[c, axis, 0])
            wait_for(self.middle[axis].at[c, far, :, self.lanes(c, axis)], self.sems[0].at[c, axis, 1])
            wait_for(self.sends[axis].at[c, far, 0, :, self.lanes(c, axis)], self.sems[0].at[c, axis, 2])

    class Gather:
        def __init__(self, refs, sems):
            self.refs, self.sems = refs, sems

        def first(self, c, axis):
            ref = self.refs[axis]
            return [
                link(ref.at[c, 0, 0], ref.at[c, 0, SIDE - k], *self.sems, c, axis, 0, k, 1 - axis)
                for k in opposite_first
            ]

        def near(self, c, axis):
            ref = self.refs[axis]
            return [
                link(ref.at[c, 0, 0], ref.at[c, SIDE - k, 0], *self.sems, c, axis, 2, k, axis)
                for k in opposite_first
            ]

        def second(self, c, axis):
            ref = self.refs[axis]
            return [
                link(ref.at[c, 0, far], ref.at[c, SIDE - k, far], *self.sems, c, axis, 1, k, axis)
                for k in opposite_first
            ]

        def begin(self, c, rows):
            block = jnp.concatenate([rows[:, 0:FOLD], rows[:, FOLD:]], axis=0).astype(BF16)
            for axis in range(2):
                self.refs[axis][c, 0, 0] = block[:, axis * LANES:(axis + 1) * LANES]
                for copy in self.first(c, axis):
                    copy.start()
            for axis in range(2):
                for copy in self.near(c, axis):
                    copy.start()

        def turn(self, c):
            for axis in range(2):
                wait_for(self.refs[axis].at[c, 0, far], self.sems[1].at[c, axis, 0])
                for copy in self.second(c, axis):
                    copy.start()

        def end(self, c, absolute):
            for axis in range(2):
                wait_for(self.refs[axis].at[c, far, far], self.sems[1].at[c, axis, 1])
                wait_for(self.refs[axis].at[c, far, 0], self.sems[1].at[c, axis, 2])
            rows = [[], []]
            for axis in range(2):
                blocks = []
                for y in range(SIDE):
                    for z in range(SIDE):
                        i, j = spot(y, z, axis, absolute)
                        blocks.append(self.refs[axis][c, i, j].astype(F32))
                rows[0].append(jnp.concatenate([block[0:ROWS] for block in blocks], axis=0))
                rows[1].append(jnp.concatenate([block[ROWS:] for block in blocks], axis=0))
            return jnp.concatenate(rows[0] + rows[1], axis=1).astype(BF16)

        def drain(self, c):
            for axis in range(2):
                wait_for(self.refs[axis].at[c, 0, far], self.sems[0].at[c, axis, 0])
                wait_for(self.refs[axis].at[c, far, far], self.sems[0].at[c, axis, 1])
                wait_for(self.refs[axis].at[c, far, 0], self.sems[0].at[c, axis, 2])

    def unfold(left, right):
        return jnp.concatenate([left[0:ROWS], right[0:ROWS], left[ROWS:], right[ROWS:]], axis=1)

    sum1 = Sum((send1a, send1b), (early1a, early1b), (middle1a, middle1b), (late1a, late1b), (ss1, rs1), True)
    spread1 = Gather((gather1a, gather1b), (ss2, rs2))
    sum2 = Sum((send2a, send2b), (early2a, early2b), (middle2a, middle2b), (late2a, late2b), (ss1, rs1), False)
    spread2 = Gather((gather2a, gather2b), (ss2, rs2))

    loads[2].wait()
    shared[0].wait()
    for c in range(CHUNKS):
        own_lanes = pl.ds(pl.multiple_of(core * MINE + c * PART, PART), PART)
        mine = gained_own[:, own_lanes]
        gained_swaps[c].wait()
        theirs = gained_recv[c]
        lower = jnp.where(core == 0, mine[0:HALF], theirs[0:HALF])
        upper = jnp.where(core == 0, theirs[0:HALF], mine[0:HALF])
        channels = jnp.concatenate([lower, upper], axis=0).T
        squares2 = jnp.concatenate([mine[HALF:], theirs[HALF:]], axis=0)
        square = dot(squares2, pick_one, TN)
        square = folded(square, square)
        for axis in range(2):
            low_at = slice(axis * LANES, (axis + 1) * LANES)
            high_at = slice(FOLD + axis * LANES, FOLD + (axis + 1) * LANES)
            terms = folded(
                dot(channels, wo[:, :, low_at].reshape(2 * HALF, LANES)),
                dot(channels, wo[:, :, high_at].reshape(2 * HALF, LANES)))
            if axis == c % 2:
                terms = jnp.concatenate([terms, square], axis=2)
            put(terms, sum1.sends[axis], c, axis, True)
            sum1.begin(c, axis)

    acc_column = to_column(accepted[...])
    row32 = iota((REQUESTS, TOKENS), 0)
    lane32 = iota((REQUESTS, TOKENS), 1)
    acc_lanes = jnp.sum(jnp.where(lane32 // STEPS == row32, acc_column, 0), axis=0, keepdims=True)
    last = jnp.where(lane32 == row32 * STEPS + acc_column - 1, 1.0, 0.0)
    last = jnp.where(acc_column > 0, last, 0.0).astype(BF16)
    run_all = decay[...]
    run_high = run_all.astype(BF16)
    run_low = (run_all - run_high.astype(F32)).astype(BF16)
    run_picked = dot(last, run_high, NT) + dot(last, run_low, NT)
    picked[...] = jnp.where(acc_column == 0, 1.0, run_picked)
    live = step_of < acc_lanes
    for tile in range(TOKENS // TILE):
        at = slice(tile * TILE, (tile + 1) * TILE)
        taken = jnp.where(live[:, at], values[:, at].astype(F32), 0.0)
        spread = jnp.broadcast_to(taken[None], (TILE_REQ, HALF, TILE))
        ours = iota((TILE_REQ, HALF, TILE), 0) == iota((TILE_REQ, HALF, TILE), 2) // STEPS
        spread = jnp.where(ours, spread, 0.0).astype(BF16).reshape(TILE_REQ * HALF, TILE)
        added = dot(spread, key_b[:, at], NT)
        for i in range(TILE_REQ):
            r = tile * TILE_REQ + i
            kept_v[r] = (picked[r:r + 1, :] * (state_v[r] + added[i * HALF:(i + 1) * HALF])).astype(BF16)
    for e in range(EDGES):
        place = jnp.where(lane32 == row32 * STEPS + acc_column + (e - EDGES), 1.0, 0.0)
        place = jnp.where(acc_column + e >= EDGES, place, 0.0).astype(BF16)
        kept_edge = dot(place, inputs_raw, NT)
        for i in range(EDGES):
            kept_edge = kept_edge + jnp.where(acc_column + e == i, edges[i].astype(F32), 0.0)
        edge_v[e] = kept_edge.astype(BF16)

    def cross(k):
        return [
            pltpu.make_async_remote_copy(
                src_ref=source, dst_ref=target.at[group], send_sem=ss_x.at[slot, k - 1],
                recv_sem=rs_x.at[slot, k - 1], device_id=across(k), device_id_type=MESH)
            for slot, (source, target) in enumerate(((kept_v, kept_all), (edge_v, edge_all)))
        ]

    crossing = [copy for k in range(1, GROUPS) for copy in cross(k)]
    for copy in crossing:
        copy.start()
    kept_all[group] = kept_v[...]
    edge_all[group] = edge_v[...]

    def scaled_norm(rows, gain):
        factor = lax.rsqrt(jnp.mean(rows * rows, axis=1, keepdims=True) + EPSILON)
        return rows * factor * gain

    for c in range(CHUNKS):
        for axis in range(2):
            sum1.turn(c, axis)
    for load in loads[3:]:
        load.wait()
    for c in range(CHUNKS):
        left = sum1.end(c, 0)
        right = sum1.end(c, 1)
        near = res_v[c].astype(F32)
        before = jnp.where(chip % 2 == 0, near[0:ROWS], near[ROWS:])
        square = (left if c % 2 == 0 else right)[0:ROWS, LANES:LANES + 1]
        attn = unfold(left[:, 0:LANES], right[:, 0:LANES]) * lax.rsqrt(square / WIDTH + EPSILON)
        first = (before + attn).astype(BF16).astype(F32)
        first_v[c] = first
        spread1.begin(c, scaled_norm(first, gain_mlp[...]))
    for c in range(CHUNKS):
        spread1.turn(c)
    for c in range(CHUNKS):
        for axis in range(2):
            sum1.drain(c, axis)
    for copy in shared[1:]:
        copy.wait()

    hidden_width = wd.shape[0] * wd.shape[1]
    for c in range(CHUNKS):
        rows = spread1.end(c, False)
        both_parts = dot(rows, wgu[...].reshape(2 * hidden_width, WIDTH), NT)
        gate = both_parts[:, 0:hidden_width]
        hidden = (gate * jax.nn.sigmoid(gate) * both_parts[:, hidden_width:]).astype(BF16)
        for axis in range(2):
            low_at = slice(axis * LANES, (axis + 1) * LANES)
            high_at = slice(FOLD + axis * LANES, FOLD + (axis + 1) * LANES)
            put(folded(
                dot(hidden, wd[:, :, low_at].reshape(hidden_width, LANES)),
                dot(hidden, wd[:, :, high_at].reshape(hidden_width, LANES)),
            ), sum2.sends[axis], c, axis, False)
            sum2.begin(c, axis)
    for c in range(CHUNKS):
        spread1.drain(c)

    for c in range(CHUNKS):
        for axis in range(2):
            sum2.turn(c, axis)
    for c in range(CHUNKS):
        down = unfold(sum2.end(c, 0), sum2.end(c, 1))
        second = (first_v[c] + down).astype(BF16).astype(F32)
        spread2.begin(c, scaled_norm(second, gain_next[...]))
    for c in range(CHUNKS):
        spread2.turn(c)

    for copy in crossing:
        copy.wait()
    home_row = home[...]
    source_lane = iota((1, GROUPS * REQUESTS), 1)
    for i in range(REQUESTS):
        found = jnp.max(jnp.where(home_row == group * REQUESTS + i, source_lane, 0))
        kept_out[i] = kept_all[found // REQUESTS, found % REQUESTS].astype(F32)
    leaving = pltpu.make_async_copy(kept_out, kept_home, load_sem.at[8 + CHUNKS])
    leaving.start()
    target_row = iota((REQUESTS, GROUPS * REQUESTS), 0) + group * REQUESTS
    chosen = jnp.where(home_row == target_row, 1.0, 0.0).astype(BF16)
    for e in range(EDGES):
        pool = edge_all[:, e].reshape(GROUPS * REQUESTS, HALF)
        edge_out[e] = dot(chosen, pool).astype(BF16)

    for c in range(CHUNKS):
        for axis in range(2):
            sum2.drain(c, axis)

    swaps = []
    for c in range(CHUNKS):
        normed = spread2.end(c, True)
        theirs_next = dot(wn[1 - core].reshape(3 * HALF, WIDTH), normed, NT)
        next_send[c] = theirs_next.astype(BF16).reshape(3, HALF, PART)
        swaps.append(to_sibling(next_send.at[c], next_recv.at[c], 6 + CHUNKS + c))
        swaps[c].start()
        own_next = dot(wn[core].reshape(3 * HALF, WIDTH), normed, NT)
        here = pl.ds(pl.multiple_of(core * MINE + c * PART, PART), PART)
        next_out[:, :, here] = own_next.astype(BF16).reshape(3, HALF, PART)
    for c in range(CHUNKS):
        spread2.drain(c)
        swaps[c].wait()
        there = pl.ds(pl.multiple_of((1 - core) * MINE + c * PART, PART), PART)
        next_out[:, :, there] = next_recv[c]
    leaving.wait()


PIECES = 4
PIECE = REQUESTS // PIECES


def finish(next_in, kept_in, edge_in, next_out, kept_out, edge_out, next_v, kept_v, edge_v, in_sems, out_sems):
    parts = [slice(i * PIECE, (i + 1) * PIECE) for i in range(PIECES)]
    routes = [(kept_in.at[part], kept_v.at[part], kept_out.at[part]) for part in parts]
    routes += [(next_in, next_v, next_out), (edge_in, edge_v, edge_out)]
    arrive = [pltpu.make_async_copy(a, b, in_sems.at[i]) for i, (a, b, _) in enumerate(routes)]
    leave = [pltpu.make_async_copy(b, c, out_sems.at[i]) for i, (_, b, c) in enumerate(routes)]
    for copy in arrive:
        copy.start()
    for copy, further in zip(arrive, leave):
        copy.wait()
        further.start()
    for copy in leave:
        copy.wait()


def sum_buffers(width):
    grids = [(SIDE, SIDE), (SIDE, SIDE), (SIDE,), (SIDE,)]
    return [pltpu.VMEM((CHUNKS, *grid, 2 * ROWS, width), BF16) for grid in grids for _ in range(2)]


def gather_buffers():
    return [pltpu.VMEM((CHUNKS, SIDE, SIDE, 2 * ROWS, LANES), BF16)] * 2


def per_device(
    residual_in, mixer_in, forget_floor, conv_weight, conv_edges, state_in, accepted, home_slot,
    gain_mixer, w_out, gain_mlp, w_gate, w_up, w_down, gain_next, w_next,
):
    hidden_width = w_gate.shape[1]
    anywhere = pl.BlockSpec(memory_space=pl.ANY)
    vmem = pl.BlockSpec(memory_space=pltpu.VMEM)
    dma = pltpu.SemaphoreType.DMA
    outputs = (
        jax.ShapeDtypeStruct((3, HALF, TOKENS), BF16),
        jax.ShapeDtypeStruct((REQUESTS, HALF, KEYS), F32),
        jax.ShapeDtypeStruct((EDGES, REQUESTS, HALF), BF16),
    )
    results = pl.pallas_call(
        kernel,
        name="draft_check",
        out_shape=outputs,
        in_specs=[anywhere] * 16,
        out_specs=(vmem, anywhere, vmem),
        scratch_shapes=[
            pltpu.VMEM((CHIPS, KEYS), F32),
            pltpu.VMEM((TAPS, HALF), F32),
            pltpu.VMEM((EDGES, REQUESTS, HALF), BF16),
            pltpu.VMEM((1, REQUESTS), jnp.int32),
            pltpu.VMEM((1, GROUPS * REQUESTS), jnp.int32),
            pltpu.VMEM((1, HALF), F32),
            pltpu.VMEM((1, WIDTH), F32),
            pltpu.VMEM((1, WIDTH), F32),
            pltpu.VMEM((REQUESTS, HALF, KEYS), F32),
            pltpu.VMEM((3, HALF, TOKENS), BF16),
            pltpu.VMEM((2, 2, HALF, TOKENS), BF16),
            pltpu.VMEM((REQUESTS, HALF, KEYS), F32),
            pltpu.VMEM((CHUNKS, 2 * ROWS, WIDTH), BF16),
            pltpu.VMEM((2, HALF, WIDTH), BF16),
            pltpu.VMEM((2, 2, hidden_width, WIDTH), BF16),
            pltpu.VMEM((2, hidden_width, WIDTH), BF16),
            pltpu.VMEM((2, 3, HALF, WIDTH), BF16),
            pltpu.VMEM((KEYS, TOKENS), BF16),
            pltpu.VMEM((KEYS, TOKENS), BF16),
            pltpu.VMEM((KEYS, TOKENS), F32),
            pltpu.VMEM((HALF, TOKENS), BF16),
            pltpu.VMEM((REQUESTS, KEYS), F32),
            pltpu.VMEM((HALF + STEPS, TOKENS), BF16),
            pltpu.VMEM((CHUNKS, HALF + STEPS, PART), BF16),
            pltpu.VMEM((CHUNKS, HALF + STEPS, PART), BF16),
            *sum_buffers(LANES + EXTRA), *gather_buffers(),
            pltpu.VMEM((CHUNKS, ROWS, WIDTH), F32),
            *sum_buffers(LANES), *gather_buffers(),
            pltpu.VMEM((CHUNKS, 3, HALF, PART), BF16),
            pltpu.VMEM((CHUNKS, 3, HALF, PART), BF16),
            pltpu.VMEM((REQUESTS, HALF, KEYS), BF16),
            pltpu.VMEM((EDGES, REQUESTS, HALF), BF16),
            pltpu.VMEM((GROUPS, REQUESTS, HALF, KEYS), BF16),
            pltpu.VMEM((GROUPS, EDGES, REQUESTS, HALF), BF16),
            dma((9 + CHUNKS,)), dma((8,)), dma((6 + 2 * CHUNKS,)), dma((6 + 2 * CHUNKS,)),
            *[dma((CHUNKS, 2, 3))] * 4,
            dma((2, GROUPS - 1)), dma((2, GROUPS - 1)),
        ],
        compiler_params=pltpu.CompilerParams(
            collective_id=0, has_side_effects=True, vmem_limit_bytes=56 * 2**20),
    )(
        residual_in,
        mixer_in.transpose(1, 2, 0),
        forget_floor.reshape(-1, KEYS),
        conv_weight,
        conv_edges.transpose(1, 0, 2),
        state_in,
        accepted.reshape(1, -1),
        home_slot.reshape(1, -1),
        gain_mixer.reshape(1, -1),
        w_out,
        gain_mlp.reshape(1, -1),
        w_gate.T,
        w_up.T,
        w_down,
        gain_next.reshape(1, -1),
        w_next.transpose(1, 2, 0),
    )
    next_flat, kept, kept_edges = pl.pallas_call(
        finish,
        name="finish",
        out_shape=outputs,
        in_specs=[anywhere] * 3,
        out_specs=(anywhere,) * 3,
        scratch_shapes=[
            *[pltpu.VMEM(output.shape, output.dtype) for output in outputs],
            dma((PIECES + 2,)), dma((PIECES + 2,)),
        ],
        compiler_params=pltpu.CompilerParams(vmem_limit_bytes=56 * 2**20),
    )(*results)
    return next_flat.transpose(2, 0, 1), kept, kept_edges.transpose(1, 0, 2)


def solution(mesh):
    in_specs = (
        P("grp", None),
        P("grp", None, "req"),
        P(),
        P(None, "req"),
        P("grp", None, "req"),
        P("grp", "req", None),
        P("grp"),
        P(),
        P("req"),
        P("req", None),
        P(),
        P(None, "req"),
        P(None, "req"),
        P("req", None),
        P(),
        P(None, None, "req"),
    )
    out_specs = (P("grp", None, "req"), P("grp", "req", None), P("grp", None, "req"))
    return jax.shard_map(
        per_device, mesh=mesh, in_specs=in_specs, out_specs=out_specs, check_vma=False
    )
```

```python
import jax
import jax.numpy as jnp
from jax import lax
from jax.experimental import pallas as pl
from jax.experimental.pallas import tpu as pltpu
from jax.sharding import PartitionSpec as P

EPSILON = 1e-06
MESH = pl.DeviceIdType.MESH
F32 = jnp.float32
BF16 = jnp.bfloat16

SIDE = 4
CHIPS = SIDE * SIDE
GROUPS = 4
STEPS = 16
TAPS = 4
EDGES = 3
WIDTH = 2048
HALF = 64
KEYS = 128
EXTRA = 128
REQUESTS = 32
TOKENS = REQUESTS * STEPS
MINE = TOKENS // 2
TILE = 128
TILE_REQ = TILE // STEPS
CHUNKS = 2
PART = MINE // CHUNKS
ROWS = PART // CHIPS
FOLD = WIDTH // 2
LANES = FOLD // 2

NT = (((1,), (1,)), ((), ()))
TN = (((0,), (0,)), ((), ()))


def dot(left, right, dims=(((1,), (0,)), ((), ()))):
    return lax.dot_general(left, right, dims, preferred_element_type=F32)


def iota(shape, dim):
    return lax.broadcasted_iota(jnp.int32, shape, dim)


def to_column(row):
    size = row.shape[1]
    square = jnp.broadcast_to(row, (size, size))
    diagonal = iota((size, size), 0) == iota((size, size), 1)
    return jnp.sum(jnp.where(diagonal, square, jnp.zeros_like(square)), axis=1, keepdims=True)


def kernel(
    residual, mixer, floor_in, taps_in, edges_in, state, accepted_in, home_in, gain_mixer_in,
    w_out, gain_mlp_in, w_gate, w_up, w_down, gain_next_in, w_next,
    next_out, kept_home, edge_out,
    floor, taps, edges, accepted, home, gain_mixer, gain_mlp, gain_next, kept_out, mix_v, pair, state_v, res_v, wo, wgu, wd, wn,
    query_b, key_b, decay, values, picked, gained_own, gained_send, gained_recv,
    send1a, send1b, early1a, early1b, middle1a, middle1b, late1a, late1b, gather1a, gather1b, first_v,
    send2a, send2b, early2a, early2b, middle2a, middle2b, late2a, late2b, gather2a, gather2b,
    next_send, next_recv, kept_v, edge_v, kept_all, edge_all,
    load_sem, small_sem, pair_ss, pair_rs, ss1, rs1, ss2, rs2, ss_x, rs_x,
):
    member = lax.axis_index("req")
    group = lax.axis_index("grp")
    core = member % 2
    chip = member // 2
    at_y = chip // SIDE
    at_z = chip % SIDE
    sibling = {"req": chip * 2 + (1 - core), "grp": group}

    def along(axis, k):
        if axis == 0:
            chip_at = (at_y + k) % SIDE * SIDE + at_z
        else:
            chip_at = at_y * SIDE + (at_z + k) % SIDE
        return {"req": chip_at * 2 + core, "grp": group}

    def across(k):
        return {"req": member, "grp": (group + k) % GROUPS}

    barrier = pltpu.get_barrier_semaphore()

    pl.semaphore_signal(barrier, inc=1, device_id=sibling, device_id_type=MESH)
    for axis in range(2):
        for k in range(1, SIDE):
            pl.semaphore_signal(barrier, inc=1, device_id=along(axis, k), device_id_type=MESH)
    for k in range(1, GROUPS):
        pl.semaphore_signal(barrier, inc=1, device_id=across(k), device_id_type=MESH)

    loads = [
        pltpu.make_async_copy(mixer, mix_v, load_sem.at[0]),
        pltpu.make_async_copy(state, state_v, load_sem.at[1]),
        pltpu.make_async_copy(w_out, wo.at[core], load_sem.at[2]),
        pltpu.make_async_copy(w_gate, wgu.at[0, core], load_sem.at[4]),
        pltpu.make_async_copy(w_up, wgu.at[1, core], load_sem.at[5]),
        pltpu.make_async_copy(w_down, wd.at[core], load_sem.at[6]),
        pltpu.make_async_copy(w_next, wn.at[core], load_sem.at[7]),
    ]
    for c in range(CHUNKS):
        near = core * MINE + c * PART + chip // 2 * (2 * ROWS)
        loads.append(pltpu.make_async_copy(
            residual.at[pl.ds(pl.multiple_of(near, 2 * ROWS), 2 * ROWS)], res_v.at[c], load_sem.at[8 + c]))
    smalls = [
        pltpu.make_async_copy(source, target, small_sem.at[i])
        for i, (source, target) in enumerate((
            (taps_in, taps), (edges_in, edges), (floor_in, floor), (gain_mixer_in, gain_mixer),
            (accepted_in, accepted), (home_in, home), (gain_mlp_in, gain_mlp), (gain_next_in, gain_next)))
    ]
    for load in loads[:1] + smalls + loads[1:]:
        load.start()

    def to_sibling(source, target, slot):
        return pltpu.make_async_remote_copy(
            src_ref=source, dst_ref=target, send_sem=pair_ss.at[slot], recv_sem=pair_rs.at[slot],
            device_id=sibling, device_id_type=MESH)

    pl.semaphore_wait(barrier, 1 + 2 * (SIDE - 1) + GROUPS - 1)
    halves = to_sibling(mixer.at[0:2], pair.at[:, core], 0)
    halves.start()
    shared = [
        to_sibling(w_out, wo.at[core], 1),
        to_sibling(w_gate, wgu.at[0, core], 2),
        to_sibling(w_up, wgu.at[1, core], 3),
        to_sibling(w_down, wd.at[core], 4),
        to_sibling(w_next, wn.at[core], 5),
    ]
    for copy in shared:
        copy.start()

    for load in smalls + loads[:1]:
        load.wait()
    lane = iota((1, TOKENS), 1)
    step_of = lane % STEPS
    inputs_raw = mix_v[2]
    inputs_f = inputs_raw.astype(F32)
    stacked = jnp.concatenate([edges[i] for i in range(EDGES)], axis=0)
    row96 = iota((EDGES * REQUESTS, TOKENS), 0)
    lane96 = iota((EDGES * REQUESTS, TOKENS), 1)
    conv = to_column(taps[TAPS - 1:TAPS, :]) * inputs_f
    for j in range(TAPS - 1):
        shift = TAPS - 1 - j
        early = row96 // REQUESTS - j
        place = (early >= 0) & (lane96 == (row96 % REQUESTS) * STEPS + early)
        from_edges = dot(stacked, jnp.where(place, 1.0, 0.0).astype(BF16), TN)
        moved = jnp.where(step_of >= shift, pltpu.roll(inputs_f, shift, axis=1), 0.0)
        conv = conv + to_column(taps[j:j + 1, :]) * (moved + from_edges)
    values[...] = conv.astype(BF16)

    pair[:, core] = mix_v[0:2]
    floor_row = floor[pl.ds(chip, 1), :]
    low = to_column(floor_row)
    gain_column = to_column(gain_mixer[...])
    halves.wait()
    loads[1].wait()

    def gates(tile):
        at = slice(tile * TILE, (tile + 1) * TILE)
        step_t = iota((KEYS, TILE), 1) % STEPS
        q_pre = pair[0, :, :, at].reshape(KEYS, TILE).astype(F32)
        f_pre = pair[1, :, :, at].reshape(KEYS, TILE).astype(F32)
        query = q_pre * jax.nn.sigmoid(q_pre)
        forget = low + (1.0 - low) * jax.nn.sigmoid(f_pre)
        keyed = 1.0 - forget
        run = forget
        for shift in (1, 2, 4, 8):
            run = jnp.where(step_t >= shift, run * pltpu.roll(run, shift, axis=1), run)
        decay[:, at] = run
        query_b[:, at] = (query * run).astype(BF16)
        key_b[:, at] = (keyed / run).astype(BF16)

    def recurrence(tile):
        at = slice(tile * TILE, (tile + 1) * TILE)
        q_t = query_b[:, at]
        begin = state_v[tile * TILE_REQ:(tile + 1) * TILE_REQ].astype(BF16).reshape(TILE_REQ * HALF, KEYS)
        through = dot(begin, q_t).reshape(TILE_REQ, HALF, TILE)
        ours = iota((TILE_REQ, HALF, TILE), 0) == iota((TILE_REQ, HALF, TILE), 2) // STEPS
        total = jnp.sum(jnp.where(ours, through, 0.0), axis=0)
        scores = dot(key_b[:, at], q_t, TN)
        source = iota((TILE, TILE), 0)
        sink = iota((TILE, TILE), 1)
        causal = (source // STEPS == sink // STEPS) & (source <= sink)
        scores = jnp.where(causal, scores, 0.0).astype(BF16)
        total = (total + dot(values[:, at], scores)) * KEYS ** (-0.5)
        gained_own[0:HALF, at] = (total * gain_column).astype(BF16)
        square = jnp.sum(total * total, axis=0, keepdims=True)
        gained_own[HALF:HALF + STEPS, at] = jnp.broadcast_to(square, (STEPS, TILE)).astype(BF16)

    gained_swaps = []
    for c in range(CHUNKS):
        for tile in (c, CHUNKS + c):
            gates(tile)
            recurrence(tile)
        other_lanes = pl.ds(pl.multiple_of((1 - core) * MINE + c * PART, PART), PART)
        gained_send[c] = gained_own[:, other_lanes]
        gained_swaps.append(to_sibling(gained_send.at[c], gained_recv.at[c], 6 + c))
        gained_swaps[c].start()
    pick_one = jnp.where(iota((2 * STEPS, EXTRA), 0) % STEPS == 0, 1.0, 0.0).astype(BF16)

    def folded(low_part, high_part):
        width = low_part.shape[1]
        return jnp.concatenate(
            [low_part.reshape(CHIPS, ROWS, width), high_part.reshape(CHIPS, ROWS, width)], axis=1
        ).astype(BF16)

    def spot(y, z, axis, absolute):
        if absolute:
            y, z = (y - at_y + SIDE) % SIDE, (z - at_z + SIDE) % SIDE
        return (y, z) if axis == 0 else (z, y)

    def put(blocks, ref, c, axis, absolute):
        width = blocks.shape[2]
        for y in range(SIDE):
            for z in range(SIDE):
                i, j = spot(y, z, axis, absolute)
                ref[c, i, j, :, 0:width] = blocks[y * SIDE + z]

    def link(source, target, ssem, rsem, c, axis, stage, k, towards):
        return pltpu.make_async_remote_copy(
            src_ref=source, dst_ref=target, send_sem=ssem.at[c, axis, stage],
            recv_sem=rsem.at[c, axis, stage], device_id=along(towards, k), device_id_type=MESH)

    far = slice(1, SIDE)
    opposite_first = (2, 1, 3)

    def wait_for(region, sem):
        pltpu.make_async_copy(region, region, sem).wait()


    class Sum:
        def __init__(self, sends, early, middle, late, sems, squares):
            self.sends, self.early, self.middle, self.late, self.sems = sends, early, middle, late, sems
            self.squares = squares

        def lanes(self, c, axis):
            return slice(0, LANES + EXTRA if self.squares and axis == c % 2 else LANES)

        def first(self, c, axis):
            return [
                link(self.sends[axis].at[c, k, far, :, self.lanes(c, axis)], self.early[axis].at[c, k, far, :, self.lanes(c, axis)],
                     *self.sems, c, axis, 0, k, axis)
                for k in opposite_first
            ]

        def near(self, c, axis):
            return [
                link(self.sends[axis].at[c, k, 0, :, self.lanes(c, axis)], self.early[axis].at[c, k, 0, :, self.lanes(c, axis)],
                     *self.sems, c, axis, 2, k, axis)
                for k in opposite_first
            ]

        def second(self, c, axis):
            return [
                link(self.middle[axis].at[c, k, :, self.lanes(c, axis)], self.late[axis].at[c, k, :, self.lanes(c, axis)],
                     *self.sems, c, axis, 1, k, 1 - axis)
                for k in opposite_first
            ]

        def begin(self, c, axis):
            for copy in self.first(c, axis):
                copy.start()

        def turn(self, c, axis):
            wait_for(self.early[axis].at[c, far, far, :, self.lanes(c, axis)], self.sems[1].at[c, axis, 0])
            sums = self.sends[axis][c, 0, far, :, self.lanes(c, axis)].astype(F32)
            for k in range(1, SIDE):
                sums = sums + self.early[axis][c, k, far, :, self.lanes(c, axis)].astype(F32)
            self.middle[axis][c, far, :, self.lanes(c, axis)] = sums.astype(BF16)
            for copy in self.second(c, axis) + self.near(c, axis):
                copy.start()

        def end(self, c, axis):
            wait_for(self.late[axis].at[c, far, :, self.lanes(c, axis)], self.sems[1].at[c, axis, 1])
            wait_for(self.early[axis].at[c, far, 0, :, self.lanes(c, axis)], self.sems[1].at[c, axis, 2])
            sums = self.sends[axis][c, 0, 0, :, self.lanes(c, axis)].astype(F32)
            for k in range(1, SIDE):
                sums = sums + self.early[axis][c, k, 0, :, self.lanes(c, axis)].astype(F32)
                sums = sums + self.late[axis][c, k, :, self.lanes(c, axis)].astype(F32)
            return sums

        def drain(self, c, axis):
            wait_for(self.sends[axis].at[c, far, far, :, self.lanes(c, axis)], self.sems[0].at[c, axis, 0])
            wait_for(self.middle[axis].at[c, far, :, self.lanes(c, axis)], self.sems[0].at[c, axis, 1])
            wait_for(self.sends[axis].at[c, far, 0, :, self.lanes(c, axis)], self.sems[0].at[c, axis, 2])

    class Gather:
        def __init__(self, refs, sems):
            self.refs, self.sems = refs, sems

        def first(self, c, axis):
            ref = self.refs[axis]
            return [
                link(ref.at[c, 0, 0], ref.at[c, 0, SIDE - k], *self.sems, c, axis, 0, k, 1 - axis)
                for k in opposite_first
            ]

        def near(self, c, axis):
            ref = self.refs[axis]
            return [
                link(ref.at[c, 0, 0], ref.at[c, SIDE - k, 0], *self.sems, c, axis, 2, k, axis)
                for k in opposite_first
            ]

        def second(self, c, axis):
            ref = self.refs[axis]
            return [
                link(ref.at[c, 0, far], ref.at[c, SIDE - k, far], *self.sems, c, axis, 1, k, axis)
                for k in opposite_first
            ]

        def begin(self, c, rows):
            block = jnp.concatenate([rows[:, 0:FOLD], rows[:, FOLD:]], axis=0).astype(BF16)
            for axis in range(2):
                self.refs[axis][c, 0, 0] = block[:, axis * LANES:(axis + 1) * LANES]
                for copy in self.first(c, axis):
                    copy.start()
            for axis in range(2):
                for copy in self.near(c, axis):
                    copy.start()

        def turn(self, c):
            for axis in range(2):
                wait_for(self.refs[axis].at[c, 0, far], self.sems[1].at[c, axis, 0])
                for copy in self.second(c, axis):
                    copy.start()

        def end(self, c, absolute):
            for axis in range(2):
                wait_for(self.refs[axis].at[c, far, far], self.sems[1].at[c, axis, 1])
                wait_for(self.refs[axis].at[c, far, 0], self.sems[1].at[c, axis, 2])
            rows = [[], []]
            for axis in range(2):
                blocks = []
                for y in range(SIDE):
                    for z in range(SIDE):
                        i, j = spot(y, z, axis, absolute)
                        blocks.append(self.refs[axis][c, i, j].astype(F32))
                rows[0].append(jnp.concatenate([block[0:ROWS] for block in blocks], axis=0))
                rows[1].append(jnp.concatenate([block[ROWS:] for block in blocks], axis=0))
            return jnp.concatenate(rows[0] + rows[1], axis=1).astype(BF16)

        def drain(self, c):
            for axis in range(2):
                wait_for(self.refs[axis].at[c, 0, far], self.sems[0].at[c, axis, 0])
                wait_for(self.refs[axis].at[c, far, far], self.sems[0].at[c, axis, 1])
                wait_for(self.refs[axis].at[c, far, 0], self.sems[0].at[c, axis, 2])

    def unfold(left, right):
        return jnp.concatenate([left[0:ROWS], right[0:ROWS], left[ROWS:], right[ROWS:]], axis=1)

    sum1 = Sum((send1a, send1b), (early1a, early1b), (middle1a, middle1b), (late1a, late1b), (ss1, rs1), True)
    spread1 = Gather((gather1a, gather1b), (ss2, rs2))
    sum2 = Sum((send2a, send2b), (early2a, early2b), (middle2a, middle2b), (late2a, late2b), (ss1, rs1), False)
    spread2 = Gather((gather2a, gather2b), (ss2, rs2))

    loads[2].wait()
    shared[0].wait()
    for c in range(CHUNKS):
        own_lanes = pl.ds(pl.multiple_of(core * MINE + c * PART, PART), PART)
        mine = gained_own[:, own_lanes]
        gained_swaps[c].wait()
        theirs = gained_recv[c]
        lower = jnp.where(core == 0, mine[0:HALF], theirs[0:HALF])
        upper = jnp.where(core == 0, theirs[0:HALF], mine[0:HALF])
        channels = jnp.concatenate([lower, upper], axis=0).T
        squares2 = jnp.concatenate([mine[HALF:], theirs[HALF:]], axis=0)
        square = dot(squares2, pick_one, TN)
        square = folded(square, square)
        for axis in range(2):
            low_at = slice(axis * LANES, (axis + 1) * LANES)
            high_at = slice(FOLD + axis * LANES, FOLD + (axis + 1) * LANES)
            terms = folded(
                dot(channels, wo[:, :, low_at].reshape(2 * HALF, LANES)),
                dot(channels, wo[:, :, high_at].reshape(2 * HALF, LANES)))
            if axis == c % 2:
                terms = jnp.concatenate([terms, square], axis=2)
            put(terms, sum1.sends[axis], c, axis, True)
            sum1.begin(c, axis)

    acc_column = to_column(accepted[...])
    row32 = iota((REQUESTS, TOKENS), 0)
    lane32 = iota((REQUESTS, TOKENS), 1)
    acc_lanes = jnp.sum(jnp.where(lane32 // STEPS == row32, acc_column, 0), axis=0, keepdims=True)
    last = jnp.where(lane32 == row32 * STEPS + acc_column - 1, 1.0, 0.0)
    last = jnp.where(acc_column > 0, last, 0.0).astype(BF16)
    run_all = decay[...]
    run_high = run_all.astype(BF16)
    run_low = (run_all - run_high.astype(F32)).astype(BF16)
    run_picked = dot(last, run_high, NT) + dot(last, run_low, NT)
    picked[...] = jnp.where(acc_column == 0, 1.0, run_picked)
    live = step_of < acc_lanes
    for tile in range(TOKENS // TILE):
        at = slice(tile * TILE, (tile + 1) * TILE)
        taken = jnp.where(live[:, at], values[:, at].astype(F32), 0.0)
        spread = jnp.broadcast_to(taken[None], (TILE_REQ, HALF, TILE))
        ours = iota((TILE_REQ, HALF, TILE), 0) == iota((TILE_REQ, HALF, TILE), 2) // STEPS
        spread = jnp.where(ours, spread, 0.0).astype(BF16).reshape(TILE_REQ * HALF, TILE)
        added = dot(spread, key_b[:, at], NT)
        for i in range(TILE_REQ):
            r = tile * TILE_REQ + i
            kept_v[r] = (picked[r:r + 1, :] * (state_v[r] + added[i * HALF:(i + 1) * HALF])).astype(BF16)
    for e in range(EDGES):
        place = jnp.where(lane32 == row32 * STEPS + acc_column + (e - EDGES), 1.0, 0.0)
        place = jnp.where(acc_column + e >= EDGES, place, 0.0).astype(BF16)
        kept_edge = dot(place, inputs_raw, NT)
        for i in range(EDGES):
            kept_edge = kept_edge + jnp.where(acc_column + e == i, edges[i].astype(F32), 0.0)
        edge_v[e] = kept_edge.astype(BF16)

    def cross(k):
        return [
            pltpu.make_async_remote_copy(
                src_ref=source, dst_ref=target.at[group], send_sem=ss_x.at[slot, k - 1],
                recv_sem=rs_x.at[slot, k - 1], device_id=across(k), device_id_type=MESH)
            for slot, (source, target) in enumerate(((kept_v, kept_all), (edge_v, edge_all)))
        ]

    crossing = [copy for k in range(1, GROUPS) for copy in cross(k)]
    for copy in crossing:
        copy.start()
    kept_all[group] = kept_v[...]
    edge_all[group] = edge_v[...]

    def scaled_norm(rows, gain):
        factor = lax.rsqrt(jnp.mean(rows * rows, axis=1, keepdims=True) + EPSILON)
        return rows * factor * gain

    for c in range(CHUNKS):
        for axis in range(2):
            sum1.turn(c, axis)
    for load in loads[3:]:
        load.wait()
    for c in range(CHUNKS):
        left = sum1.end(c, 0)
        right = sum1.end(c, 1)
        near = res_v[c].astype(F32)
        before = jnp.where(chip % 2 == 0, near[0:ROWS], near[ROWS:])
        square = (left if c % 2 == 0 else right)[0:ROWS, LANES:LANES + 1]
        attn = unfold(left[:, 0:LANES], right[:, 0:LANES]) * lax.rsqrt(square / WIDTH + EPSILON)
        first = (before + attn).astype(BF16).astype(F32)
        first_v[c] = first
        spread1.begin(c, scaled_norm(first, gain_mlp[...]))
    for c in range(CHUNKS):
        spread1.turn(c)
    for c in range(CHUNKS):
        for axis in range(2):
            sum1.drain(c, axis)
    for copy in shared[1:]:
        copy.wait()

    hidden_width = wd.shape[0] * wd.shape[1]
    for c in range(CHUNKS):
        rows = spread1.end(c, False)
        both_parts = dot(rows, wgu[...].reshape(2 * hidden_width, WIDTH), NT)
        gate = both_parts[:, 0:hidden_width]
        hidden = (gate * jax.nn.sigmoid(gate) * both_parts[:, hidden_width:]).astype(BF16)
        for axis in range(2):
            low_at = slice(axis * LANES, (axis + 1) * LANES)
            high_at = slice(FOLD + axis * LANES, FOLD + (axis + 1) * LANES)
            put(folded(
                dot(hidden, wd[:, :, low_at].reshape(hidden_width, LANES)),
                dot(hidden, wd[:, :, high_at].reshape(hidden_width, LANES)),
            ), sum2.sends[axis], c, axis, False)
            sum2.begin(c, axis)
    for c in range(CHUNKS):
        spread1.drain(c)

    for c in range(CHUNKS):
        for axis in range(2):
            sum2.turn(c, axis)
    for c in range(CHUNKS):
        down = unfold(sum2.end(c, 0), sum2.end(c, 1))
        second = (first_v[c] + down).astype(BF16).astype(F32)
        spread2.begin(c, scaled_norm(second, gain_next[...]))
    for c in range(CHUNKS):
        spread2.turn(c)

    for copy in crossing:
        copy.wait()
    home_row = home[...]
    source_lane = iota((1, GROUPS * REQUESTS), 1)
    for i in range(REQUESTS):
        found = jnp.max(jnp.where(home_row == group * REQUESTS + i, source_lane, 0))
        kept_out[i] = kept_all[found // REQUESTS, found % REQUESTS]
    leaving = pltpu.make_async_copy(kept_out, kept_home, load_sem.at[8 + CHUNKS])
    leaving.start()
    target_row = iota((REQUESTS, GROUPS * REQUESTS), 0) + group * REQUESTS
    chosen = jnp.where(home_row == target_row, 1.0, 0.0).astype(BF16)
    for e in range(EDGES):
        pool = edge_all[:, e].reshape(GROUPS * REQUESTS, HALF)
        edge_out[e] = dot(chosen, pool).astype(BF16)

    for c in range(CHUNKS):
        for axis in range(2):
            sum2.drain(c, axis)

    swaps = []
    for c in range(CHUNKS):
        normed = spread2.end(c, True)
        theirs_next = dot(wn[1 - core].reshape(3 * HALF, WIDTH), normed, NT)
        next_send[c] = theirs_next.astype(BF16).reshape(3, HALF, PART)
        swaps.append(to_sibling(next_send.at[c], next_recv.at[c], 6 + CHUNKS + c))
        swaps[c].start()
        own_next = dot(wn[core].reshape(3 * HALF, WIDTH), normed, NT)
        here = pl.ds(pl.multiple_of(core * MINE + c * PART, PART), PART)
        next_out[:, :, here] = own_next.astype(BF16).reshape(3, HALF, PART)
    for c in range(CHUNKS):
        spread2.drain(c)
        swaps[c].wait()
        there = pl.ds(pl.multiple_of((1 - core) * MINE + c * PART, PART), PART)
        next_out[:, :, there] = next_recv[c]
    leaving.wait()


PIECES = 4
PIECE = REQUESTS // PIECES


def finish(next_in, kept_in, edge_in, next_out, kept_out, edge_out, next_v, kept_v, edge_v, narrow_v, in_sems, out_sems):
    parts = [slice(i * PIECE, (i + 1) * PIECE) for i in range(PIECES)]
    routes = [(kept_in.at[part], narrow_v.at[part], kept_v.at[part], kept_out.at[part]) for part in parts]
    routes += [(next_in, next_v, next_v, next_out), (edge_in, edge_v, edge_v, edge_out)]
    arrive = [pltpu.make_async_copy(a, b, in_sems.at[i]) for i, (a, b, _, _) in enumerate(routes)]
    leave = [pltpu.make_async_copy(b, c, out_sems.at[i]) for i, (_, _, b, c) in enumerate(routes)]
    for copy in arrive:
        copy.start()
    for i, (copy, further) in enumerate(zip(arrive, leave)):
        copy.wait()
        if i < PIECES:
            kept_v[parts[i]] = narrow_v[parts[i]].astype(F32)
        further.start()
    for copy in leave:
        copy.wait()


def sum_buffers(width):
    grids = [(SIDE, SIDE), (SIDE, SIDE), (SIDE,), (SIDE,)]
    return [pltpu.VMEM((CHUNKS, *grid, 2 * ROWS, width), BF16) for grid in grids for _ in range(2)]


def gather_buffers():
    return [pltpu.VMEM((CHUNKS, SIDE, SIDE, 2 * ROWS, LANES), BF16)] * 2


def per_device(
    residual_in, mixer_in, forget_floor, conv_weight, conv_edges, state_in, accepted, home_slot,
    gain_mixer, w_out, gain_mlp, w_gate, w_up, w_down, gain_next, w_next,
):
    hidden_width = w_gate.shape[1]
    anywhere = pl.BlockSpec(memory_space=pl.ANY)
    vmem = pl.BlockSpec(memory_space=pltpu.VMEM)
    dma = pltpu.SemaphoreType.DMA
    outputs = (
        jax.ShapeDtypeStruct((3, HALF, TOKENS), BF16),
        jax.ShapeDtypeStruct((REQUESTS, HALF, KEYS), F32),
        jax.ShapeDtypeStruct((EDGES, REQUESTS, HALF), BF16),
    )
    results = pl.pallas_call(
        kernel,
        name="draft_check",
        out_shape=(outputs[0], jax.ShapeDtypeStruct(outputs[1].shape, BF16), outputs[2]),
        in_specs=[anywhere] * 16,
        out_specs=(vmem, anywhere, vmem),
        scratch_shapes=[
            pltpu.VMEM((CHIPS, KEYS), F32),
            pltpu.VMEM((TAPS, HALF), F32),
            pltpu.VMEM((EDGES, REQUESTS, HALF), BF16),
            pltpu.VMEM((1, REQUESTS), jnp.int32),
            pltpu.VMEM((1, GROUPS * REQUESTS), jnp.int32),
            pltpu.VMEM((1, HALF), F32),
            pltpu.VMEM((1, WIDTH), F32),
            pltpu.VMEM((1, WIDTH), F32),
            pltpu.VMEM((REQUESTS, HALF, KEYS), BF16),
            pltpu.VMEM((3, HALF, TOKENS), BF16),
            pltpu.VMEM((2, 2, HALF, TOKENS), BF16),
            pltpu.VMEM((REQUESTS, HALF, KEYS), F32),
            pltpu.VMEM((CHUNKS, 2 * ROWS, WIDTH), BF16),
            pltpu.VMEM((2, HALF, WIDTH), BF16),
            pltpu.VMEM((2, 2, hidden_width, WIDTH), BF16),
            pltpu.VMEM((2, hidden_width, WIDTH), BF16),
            pltpu.VMEM((2, 3, HALF, WIDTH), BF16),
            pltpu.VMEM((KEYS, TOKENS), BF16),
            pltpu.VMEM((KEYS, TOKENS), BF16),
            pltpu.VMEM((KEYS, TOKENS), F32),
            pltpu.VMEM((HALF, TOKENS), BF16),
            pltpu.VMEM((REQUESTS, KEYS), F32),
            pltpu.VMEM((HALF + STEPS, TOKENS), BF16),
            pltpu.VMEM((CHUNKS, HALF + STEPS, PART), BF16),
            pltpu.VMEM((CHUNKS, HALF + STEPS, PART), BF16),
            *sum_buffers(LANES + EXTRA), *gather_buffers(),
            pltpu.VMEM((CHUNKS, ROWS, WIDTH), F32),
            *sum_buffers(LANES), *gather_buffers(),
            pltpu.VMEM((CHUNKS, 3, HALF, PART), BF16),
            pltpu.VMEM((CHUNKS, 3, HALF, PART), BF16),
            pltpu.VMEM((REQUESTS, HALF, KEYS), BF16),
            pltpu.VMEM((EDGES, REQUESTS, HALF), BF16),
            pltpu.VMEM((GROUPS, REQUESTS, HALF, KEYS), BF16),
            pltpu.VMEM((GROUPS, EDGES, REQUESTS, HALF), BF16),
            dma((9 + CHUNKS,)), dma((8,)), dma((6 + 2 * CHUNKS,)), dma((6 + 2 * CHUNKS,)),
            *[dma((CHUNKS, 2, 3))] * 4,
            dma((2, GROUPS - 1)), dma((2, GROUPS - 1)),
        ],
        compiler_params=pltpu.CompilerParams(
            collective_id=0, has_side_effects=True, vmem_limit_bytes=56 * 2**20),
    )(
        residual_in,
        mixer_in.transpose(1, 2, 0),
        forget_floor.reshape(-1, KEYS),
        conv_weight,
        conv_edges.transpose(1, 0, 2),
        state_in,
        accepted.reshape(1, -1),
        home_slot.reshape(1, -1),
        gain_mixer.reshape(1, -1),
        w_out,
        gain_mlp.reshape(1, -1),
        w_gate.T,
        w_up.T,
        w_down,
        gain_next.reshape(1, -1),
        w_next.transpose(1, 2, 0),
    )
    next_flat, kept, kept_edges = pl.pallas_call(
        finish,
        name="finish",
        out_shape=outputs,
        in_specs=[anywhere] * 3,
        out_specs=(anywhere,) * 3,
        scratch_shapes=[
            *[pltpu.VMEM(output.shape, output.dtype) for output in outputs],
            pltpu.VMEM(outputs[1].shape, BF16),
            dma((PIECES + 2,)), dma((PIECES + 2,)),
        ],
        compiler_params=pltpu.CompilerParams(vmem_limit_bytes=56 * 2**20),
    )(*results)
    return next_flat.transpose(2, 0, 1), kept, kept_edges.transpose(1, 0, 2)


def solution(mesh):
    in_specs = (
        P("grp", None),
        P("grp", None, "req"),
        P(),
        P(None, "req"),
        P("grp", None, "req"),
        P("grp", "req", None),
        P("grp"),
        P(),
        P("req"),
        P("req", None),
        P(),
        P(None, "req"),
        P(None, "req"),
        P("req", None),
        P(),
        P(None, None, "req"),
    )
    out_specs = (P("grp", None, "req"), P("grp", "req", None), P("grp", None, "req"))
    return jax.shard_map(
        per_device, mesh=mesh, in_specs=in_specs, out_specs=out_specs, check_vma=False
    )
```
